512 devices in a mesh: rows: 16 (over z, core), cols: 32 (over y, x).
Axes of the slice: x: 4, y: 8, z: 8, core: 2. Of those that a mesh axis runs over, the one named last changes fastest.
Arguments:
- fine_in: bfloat16 [16, 32, 312, 196], P('rows', 'cols'), may hold values from -6 to 6
- coarse_in: bfloat16 [16, 32, 624, 49], P('rows', 'cols'), may hold values from -6 to 6
- inproj_fine: bfloat16 [3, 312, 312], replicated, as said below
- outproj_fine: bfloat16 [312, 312], replicated, may hold values from -0.3125 to 0.3125
- expand_fine: bfloat16 [1248, 312], replicated, may hold values from -0.3125 to 0.3125
- depth_fine: float32 [9, 1248], replicated, may hold values from -2 to 2
- shrink_fine: bfloat16 [312, 1248], replicated, may hold values from -0.15625 to 0.15625
- inproj_coarse: bfloat16 [3, 624, 624], P(None, 'rows'), as said below
- outproj_coarse: bfloat16 [624, 624], P(None, 'rows'), may hold values from -0.25 to 0.25
- expand_coarse: bfloat16 [2496, 624], P('rows'), may hold values from -0.25 to 0.25
- depth_coarse: float32 [9, 2496], replicated, may hold values from -2 to 2
- shrink_coarse: bfloat16 [624, 2496], P(None, 'rows'), may hold values from -0.125 to 0.125
- to_fine: bfloat16 [312, 624], replicated, may hold values from -0.25 to 0.25
- to_coarse: bfloat16 [9, 624, 312], P(None, 'rows'), may hold values from -0.109375 to 0.109375
Outputs:
- fine_out: bfloat16 [16, 32, 312, 196], P('rows', 'cols')
- coarse_out: bfloat16 [16, 32, 624, 49], P('rows', 'cols')
The draws below stay inside these ranges and needn't reach their ends.
Inputs may be any that keep to these rules, and one draw needn't show every extreme that they name: `inproj_fine`: queries, keys and values projections stacked in this order along the first dimension, output channel second. `inproj_coarse`: queries, keys and values projections stacked in this order along the first dimension, output channel second.
All inputs are finite; a program needn't handle non-finite values.
Results may differ from the reference program's by a relative error of at most 0.014.
Values may be sent and summed in bfloat16 or wider, within the bound.
No kernel may reach another device: no remote copies, remote signals or barrier semaphores. Data moves between devices by JAX's collectives and lax.ppermute only.
A program may use at most 64 MiB of HBM per device.

```python
import math
import jax
import jax.numpy as jnp
from jax import lax

HEAD_DIM = 39
HEADS_FINE = 8
HEADS_COARSE = 16
WIN = 7
WIN_DEV = 1
CH_FINE = 312
CH_COARSE = 624
FF_FINE = 1248
FF_COARSE = 2496
CELLS_FINE = 196
CELLS_COARSE = 49
GRID_R = 16
GRID_C = 32


def draw_inproj_fine(key, part):
    key = jax.random.fold_in(key, 11)
    channels = HEADS_FINE * HEAD_DIM
    base_key = jax.random.fold_in(key, 0)
    return (jax.random.normal(base_key, (3, channels, channels), jnp.float32) / math.sqrt(channels)).astype(jnp.bfloat16)


def draw_inproj_coarse(key, part):
    key = jax.random.fold_in(key, 23)
    channels = HEADS_COARSE * HEAD_DIM
    base_key = jax.random.fold_in(key, 0)
    return (jax.random.normal(base_key, (3, channels, channels), jnp.float32) / math.sqrt(channels)).astype(jnp.bfloat16)


def level_of(stream_key, extent, pieces, low, largest):
    level = 1.0
    for dim, shards_of in pieces:
        heights = jax.random.uniform(jax.random.fold_in(jax.random.fold_in(stream_key, 6), dim), (shards_of,), jnp.float32, low / len(pieces), largest / len(pieces))
        level = level * jnp.repeat(jnp.exp(heights), extent[dim] // shards_of).reshape((-1,) + (1,) * (len(extent) - 1 - dim))
    return level


def normal_values(stream_key, shape, scale, bound, shards=(), kind=jnp.bfloat16):
    values = scale * jax.random.normal(stream_key, shape, jnp.float32)
    if shards:
        values = values * level_of(stream_key, shape, shards, -0.22, 0.18)
    return jnp.clip(values, -bound, bound).astype(kind)


def setup_inputs(seed: int = 0) -> dict:
    keys = jax.random.split(jax.random.key(seed), 15)
    fine_in = normal_values(keys[0], (GRID_R, GRID_C, CH_FINE, CELLS_FINE), 1.0, 6.0, ((0, 16), (1, 32)))
    coarse_in = normal_values(keys[1], (GRID_R, GRID_C, CH_COARSE, CELLS_COARSE), 1.0, 6.0, ((0, 16), (1, 32)))
    inproj_fine = draw_inproj_fine(jax.random.fold_in(keys[14], 71), 0)
    outproj_fine = normal_values(keys[3], (CH_FINE, CH_FINE), CH_FINE ** -0.5, 0.3125)
    expand_fine = normal_values(keys[4], (FF_FINE, CH_FINE), CH_FINE ** -0.5, 0.3125)
    depth_fine = normal_values(keys[5], (9, FF_FINE), 9 ** -0.5, 2.0, (), jnp.float32)
    shrink_fine = normal_values(keys[6], (CH_FINE, FF_FINE), FF_FINE ** -0.5, 0.15625)
    inproj_coarse = draw_inproj_coarse(jax.random.fold_in(keys[14], 71), 0)
    outproj_coarse = normal_values(keys[8], (CH_COARSE, CH_COARSE), CH_COARSE ** -0.5, 0.25, ((1, 16),))
    expand_coarse = normal_values(keys[9], (FF_COARSE, CH_COARSE), CH_COARSE ** -0.5, 0.25, ((0, 16),))
    depth_coarse = normal_values(keys[10], (9, FF_COARSE), 9 ** -0.5, 2.0, (), jnp.float32)
    shrink_coarse = normal_values(keys[11], (CH_COARSE, FF_COARSE), FF_COARSE ** -0.5, 0.125, ((1, 16),))
    to_fine = normal_values(keys[12], (CH_FINE, CH_COARSE), CH_COARSE ** -0.5, 0.25)
    to_coarse = normal_values(keys[13], (9, CH_COARSE, CH_FINE), (9 * CH_FINE) ** -0.5, 0.109375, ((1, 16),))
    return dict(fine_in=fine_in, coarse_in=coarse_in, inproj_fine=inproj_fine, outproj_fine=outproj_fine, expand_fine=expand_fine, depth_fine=depth_fine, shrink_fine=shrink_fine, inproj_coarse=inproj_coarse, outproj_coarse=outproj_coarse, expand_coarse=expand_coarse, depth_coarse=depth_coarse, shrink_coarse=shrink_coarse, to_fine=to_fine, to_coarse=to_coarse)


EPSILON = 1e-05

def to_picture(tiles, tile_rows, tile_cols):
    grid_rows, grid_cols, channels, cellcount = tiles.shape
    shaped = tiles.reshape(grid_rows, grid_cols, channels, tile_rows, tile_cols)
    return shaped.transpose(2, 0, 3, 1, 4).reshape(channels, grid_rows * tile_rows, grid_cols * tile_cols)

def to_tiles(picture, grid_rows, grid_cols):
    channels, height, breadth = picture.shape
    tile_rows = height // grid_rows
    tile_cols = breadth // grid_cols
    shaped = picture.reshape(channels, grid_rows, tile_rows, grid_cols, tile_cols)
    return shaped.transpose(1, 3, 0, 2, 4).reshape(grid_rows, grid_cols, channels, tile_rows * tile_cols)

def normalize(values_in):
    values = values_in.astype(jnp.float32)
    center = lax.optimization_barrier(jnp.mean(values, axis=0, keepdims=True))
    spread = lax.optimization_barrier(jnp.mean((values - center) ** 2, axis=0, keepdims=True))
    return ((values - center) * lax.rsqrt(spread + EPSILON)).astype(jnp.bfloat16)

def to_windows(picture, head_count):
    channels, height, breadth = picture.shape
    head_width = channels // head_count
    shaped = picture.reshape(head_count, head_width, height // WIN, WIN, breadth // WIN, WIN)
    return shaped.transpose(0, 2, 4, 3, 5, 1).reshape(head_count, height // WIN, breadth // WIN, WIN * WIN, head_width)

def from_windows(blocks, height, breadth):
    head_count, grid_rows, grid_cols, cellcount, head_width = blocks.shape
    shaped = blocks.reshape(head_count, grid_rows, grid_cols, WIN, WIN, head_width)
    return shaped.transpose(0, 5, 1, 3, 2, 4).reshape(head_count * head_width, height, breadth)

def attend(queries, key_rows, value_rows, head_count):
    channels, height, breadth = queries.shape
    scaling = 1.0 / math.sqrt(channels // head_count)
    query_win = to_windows(queries, head_count).astype(jnp.float32)
    key_win = to_windows(key_rows, head_count).astype(jnp.float32)
    value_win = to_windows(value_rows, head_count).astype(jnp.float32)
    scores = jnp.einsum('hrcqd,hrckd->hrcqk', query_win, key_win) * scaling
    row_max = lax.optimization_barrier(jnp.max(scores, axis=-1, keepdims=True))
    exponent = jnp.exp(scores - row_max)
    probabilities = (exponent / lax.optimization_barrier(jnp.sum(exponent, axis=-1, keepdims=True))).astype(jnp.bfloat16)
    mixture = jnp.einsum('hrcqk,hrckd->hrcqd', probabilities.astype(jnp.float32), value_win).astype(jnp.bfloat16)
    return from_windows(mixture, height, breadth)

def depthwise(padded, kernel):
    height = padded.shape[1] - 2
    breadth = padded.shape[2] - 2
    running = jnp.zeros((padded.shape[0], height, breadth), jnp.float32)
    for offset in range(9):
        row_step, col_step = divmod(offset, 3)
        sample = padded[:, row_step:row_step + height, col_step:col_step + breadth].astype(jnp.float32)
        running = running + kernel[offset][:, None, None] * sample
    return running

def stream_block(picture, inproj, outproj, expand, kernel, shrink, head_count):
    channels, height, breadth = picture.shape
    normed = normalize(picture).reshape(channels, height * breadth)
    projected = jnp.einsum('tnc,cs->tns', inproj.astype(jnp.float32), normed.astype(jnp.float32)).astype(jnp.bfloat16)
    queries = projected[0].reshape(channels, height, breadth)
    key_rows = projected[1].reshape(channels, height, breadth)
    value_rows = projected[2].reshape(channels, height, breadth)
    attended = attend(queries, key_rows, value_rows, head_count).reshape(channels, height * breadth)
    middle = (picture.reshape(channels, height * breadth).astype(jnp.float32) + jnp.dot(outproj, attended, preferred_element_type=jnp.float32)).astype(jnp.bfloat16)
    normed_mid = normalize(middle)
    hidden = jax.nn.gelu(jnp.dot(expand, normed_mid, preferred_element_type=jnp.float32), approximate=False).astype(jnp.bfloat16)
    padded = jnp.pad(hidden.reshape(-1, height, breadth), ((0, 0), (1, 1), (1, 1)))
    convolved = jax.nn.gelu(depthwise(padded, kernel), approximate=False).astype(jnp.bfloat16)
    convolved = convolved.reshape(-1, height * breadth)
    result = (middle.astype(jnp.float32) + jnp.dot(shrink, convolved, preferred_element_type=jnp.float32)).astype(jnp.bfloat16)
    return result.reshape(channels, height, breadth)

def reference(fine_in, coarse_in, inproj_fine, outproj_fine, expand_fine, depth_fine, shrink_fine, inproj_coarse, outproj_coarse, expand_coarse, depth_coarse, shrink_coarse, to_fine, to_coarse):
    grid_rows, grid_cols = (fine_in.shape[0], fine_in.shape[1])
    fine_pic = to_picture(fine_in, 2 * WIN * WIN_DEV, 2 * WIN)
    coarse_pic = to_picture(coarse_in, WIN * WIN_DEV, WIN)
    fine_res = stream_block(fine_pic, inproj_fine, outproj_fine, expand_fine, depth_fine, shrink_fine, HEADS_FINE)
    coarse_res = stream_block(coarse_pic, inproj_coarse, outproj_coarse, expand_coarse, depth_coarse, shrink_coarse, HEADS_COARSE)
    coarse_ch, coarse_h, coarse_w = coarse_res.shape
    fine_ch = fine_res.shape[0]
    upsampled = jnp.dot(to_fine, coarse_res.reshape(coarse_ch, -1), preferred_element_type=jnp.float32)
    upsampled = upsampled.reshape(fine_ch, coarse_h, coarse_w)
    upsampled = jnp.repeat(jnp.repeat(upsampled, 2, axis=1), 2, axis=2)
    fine_pic_out = jax.nn.relu(fine_res.astype(jnp.float32) + upsampled).astype(jnp.bfloat16)
    padded = jnp.pad(fine_res, ((0, 0), (1, 1), (1, 1)))
    running = jnp.zeros((coarse_ch, coarse_h * coarse_w), jnp.float32)
    for offset in range(9):
        row_step, col_step = divmod(offset, 3)
        sample = padded[:, row_step:row_step + 2 * coarse_h:2, col_step:col_step + 2 * coarse_w:2].reshape(fine_ch, -1)
        running = running + jnp.dot(to_coarse[offset], sample, preferred_element_type=jnp.float32)
    downsampled = running.astype(jnp.bfloat16).reshape(coarse_ch, coarse_h, coarse_w)
    coarse_pic_out = jax.nn.relu(coarse_res.astype(jnp.float32) + downsampled.astype(jnp.float32)).astype(jnp.bfloat16)
    return (to_tiles(fine_pic_out, grid_rows, grid_cols), to_tiles(coarse_pic_out, grid_rows, grid_cols))
```

```python
import math

import jax
import jax.numpy as jnp
from jax import lax
from jax.sharding import PartitionSpec as P

HEADS_FINE = 8
HEADS_COARSE = 16
WIN = 7


EPSILON = 1e-05


def padded_2(shard, sides, width):
    for axis, dim in sides:
        size, length = (lax.axis_size(axis), shard.shape[dim])
        up = [(i, (i + 1) % size) for i in range(size - 1)]
        down = [(j, i) for i, j in up]
        last = lax.slice_in_dim(shard, length - width, length, axis=dim)
        first = lax.slice_in_dim(shard, 0, width, axis=dim)
        before = lax.ppermute(last, axis, up)
        after = lax.ppermute(first, axis, down)
        shard = jnp.concatenate([before, shard, after], axis=dim)
    return shard


def passed_along(block, axis, distance):
    devices = range(lax.axis_size(axis))
    route = [(i - distance, i) for i in devices if i - distance in devices]
    return lax.ppermute(block, axis, route)


def normalize(values_in):
    values = values_in.astype(jnp.float32)
    center = jnp.mean(values, axis=0, keepdims=True)
    spread = jnp.mean((values - center) ** 2, axis=0, keepdims=True)
    return ((values - center) * lax.rsqrt(spread + EPSILON)).astype(jnp.bfloat16)


def to_windows(picture, head_count):
    channels, height, breadth = picture.shape
    head_width = channels // head_count
    shaped = picture.reshape(head_count, head_width, height // WIN, WIN, breadth // WIN, WIN)
    return shaped.transpose(0, 2, 4, 3, 5, 1).reshape(
        head_count, height // WIN, breadth // WIN, WIN * WIN, head_width
    )


def from_windows(blocks, height, breadth):
    head_count, grid_rows, grid_cols, cellcount, head_width = blocks.shape
    shaped = blocks.reshape(head_count, grid_rows, grid_cols, WIN, WIN, head_width)
    return shaped.transpose(0, 5, 1, 3, 2, 4).reshape(head_count * head_width, height, breadth)


def attend(queries, key_rows, value_rows, head_count):
    channels, height, breadth = queries.shape
    scaling = 1.0 / math.sqrt(channels // head_count)
    query_win = to_windows(queries, head_count)
    key_win = to_windows(key_rows, head_count)
    value_win = to_windows(value_rows, head_count)
    scores = (
        jnp.einsum("hrcqd,hrckd->hrcqk", query_win, key_win, preferred_element_type=jnp.float32)
        * scaling
    )
    row_max = jnp.max(scores, axis=-1, keepdims=True)
    exponent = jnp.exp(scores - row_max)
    probabilities = (exponent / jnp.sum(exponent, axis=-1, keepdims=True)).astype(jnp.bfloat16)
    mixture = jnp.einsum(
        "hrcqk,hrckd->hrcqd", probabilities, value_win, preferred_element_type=jnp.float32
    ).astype(jnp.bfloat16)
    return from_windows(mixture, height, breadth)


def attend_whole(queries, key_rows, value_rows):
    scores = jnp.einsum(
        "hdq,hdk->hqk", queries, key_rows, preferred_element_type=jnp.float32
    ) * (1.0 / math.sqrt(39))
    row_max = jnp.max(scores, axis=-1, keepdims=True)
    exponent = jnp.exp(scores - row_max)
    probabilities = (exponent / jnp.sum(exponent, axis=-1, keepdims=True)).astype(jnp.bfloat16)
    return jnp.einsum(
        "hqk,hdk->hdq", probabilities, value_rows, preferred_element_type=jnp.float32
    ).astype(jnp.bfloat16)


def pack(inproj, outproj, expand, shrink, to_coarse):
    width = inproj.shape[-1]
    one = ((0, 0), (0, 1), (0, 0))
    taps = jnp.pad(to_coarse, ((0, 1), (0, 1), (0, 0))).reshape(5, 2, 40, -1)
    return jnp.concatenate(
        [
            jnp.pad(inproj, one).reshape(-1, width),
            jnp.pad(outproj.T, ((0, 1), (0, 0))),
            jnp.pad(expand, ((0, 4), (0, 0))),
            jnp.pad(shrink.T, ((0, 4), (0, 0))),
            taps.transpose(0, 2, 1, 3).reshape(-1, width),
            jnp.zeros((8, width), inproj.dtype),
        ]
    )


def depthwise(padded, kernel):
    height = padded.shape[1] - 2
    breadth = padded.shape[2] - 2
    running = jnp.zeros((padded.shape[0], height, breadth), jnp.float32)
    for offset in range(9):
        row_step, col_step = divmod(offset, 3)
        sample = padded[:, row_step : row_step + height, col_step : col_step + breadth].astype(
            jnp.float32
        )
        running = running + kernel[offset][:, None, None] * sample
    return running


def local(
    fine_in,
    coarse_in,
    inproj_fine,
    outproj_fine,
    expand_fine,
    depth_fine,
    shrink_fine,
    inproj_coarse,
    outproj_coarse,
    expand_coarse,
    depth_coarse,
    shrink_coarse,
    to_fine,
    to_coarse,
):
    fine_ch = fine_in.shape[2]
    coarse_ch = coarse_in.shape[2]
    fine_cells = fine_in.shape[3]
    coarse_cells = coarse_in.shape[3]
    gathered = lax.all_gather(
        pack(inproj_coarse, outproj_coarse, expand_coarse, shrink_coarse, to_coarse), "rows"
    )
    fine_rows = fine_cells // (2 * WIN)
    coarse_rows = coarse_cells // WIN
    fine_pic = fine_in.reshape(fine_ch, fine_rows, 2 * WIN)
    coarse_pic = coarse_in.reshape(coarse_ch, coarse_rows, WIN)
    normed = normalize(fine_pic).reshape(fine_ch, fine_cells)
    projected = jnp.einsum(
        "tnc,cs->tns", inproj_fine, normed, preferred_element_type=jnp.float32
    ).astype(jnp.bfloat16)
    attended = attend(
        projected[0].reshape(fine_pic.shape),
        projected[1].reshape(fine_pic.shape),
        projected[2].reshape(fine_pic.shape),
        HEADS_FINE,
    ).reshape(fine_ch, fine_cells)
    middle = (
        fine_pic.reshape(fine_ch, fine_cells).astype(jnp.float32)
        + jnp.dot(outproj_fine, attended, preferred_element_type=jnp.float32)
    ).astype(jnp.bfloat16)
    normed_mid = normalize(middle)
    hidden = jax.nn.gelu(
        jnp.dot(expand_fine, normed_mid, preferred_element_type=jnp.float32), approximate=False
    ).astype(jnp.bfloat16)
    padded = padded_2(hidden.reshape(-1, fine_rows, 2 * WIN), (("rows", 1), ("cols", 2)), 1)
    convolved = (
        jax.nn.gelu(depthwise(padded, depth_fine), approximate=False)
        .astype(jnp.bfloat16)
        .reshape(-1, fine_cells)
    )
    fine_res = (
        middle.astype(jnp.float32)
        + jnp.dot(shrink_fine, convolved, preferred_element_type=jnp.float32)
    ).astype(jnp.bfloat16)
    coarse_norm = normalize(coarse_pic).reshape(coarse_ch, coarse_cells)
    coarse_proj = jnp.einsum(
        "drc,cs->drs", gathered[:, :120], coarse_norm, preferred_element_type=jnp.float32
    ).astype(jnp.bfloat16)
    coarse_att = attend_whole(coarse_proj[:, :40], coarse_proj[:, 40:80], coarse_proj[:, 80:120])
    mixture = jnp.einsum(
        "drn,drs->ns", gathered[:, 120:160], coarse_att, preferred_element_type=jnp.float32
    )
    coarse_mid = (coarse_pic.reshape(coarse_ch, coarse_cells).astype(jnp.float32) + mixture).astype(
        jnp.bfloat16
    )
    coarse_normed_mid = normalize(coarse_mid)
    coarse_hidden = jax.nn.gelu(
        jnp.einsum(
            "drc,cs->drs",
            gathered[:, 160:320],
            coarse_normed_mid,
            preferred_element_type=jnp.float32,
        ),
        approximate=False,
    ).astype(jnp.bfloat16)
    coarse_pad = padded_2(
        coarse_hidden.reshape(-1, coarse_rows, WIN), (("rows", 1), ("cols", 2)), 1
    )
    members = gathered.shape[0]
    kernel = jnp.pad(depth_coarse.reshape(9, members, -1), ((0, 0), (0, 0), (0, 4)))
    coarse_conv = (
        jax.nn.gelu(depthwise(coarse_pad, kernel.reshape(9, -1)), approximate=False)
        .astype(jnp.bfloat16)
        .reshape(members, -1, coarse_cells)
    )
    update = jnp.einsum(
        "drn,drs->ns", gathered[:, 320:480], coarse_conv, preferred_element_type=jnp.float32
    )
    coarse_res = (coarse_mid.astype(jnp.float32) + update).astype(jnp.bfloat16)
    upsampled = jnp.dot(to_fine, coarse_res, preferred_element_type=jnp.float32).reshape(
        fine_ch, coarse_rows, WIN
    )
    upsampled = jnp.repeat(jnp.repeat(upsampled, 2, axis=1), 2, axis=2)
    fine_grid = fine_res.reshape(fine_ch, fine_rows, 2 * WIN)
    fine_out = (
        jax.nn.relu(fine_grid.astype(jnp.float32) + upsampled)
        .astype(jnp.bfloat16)
        .reshape(fine_in.shape)
    )
    above_row = passed_along(fine_grid[:, -1:, :], "rows", 1)
    extended = jnp.concatenate([above_row, fine_grid], axis=1)
    beside = passed_along(extended[:, :, -1:], "cols", 1)
    extended = jnp.concatenate([beside, extended], axis=2)
    extended = jnp.pad(extended, ((0, 0), (0, 1), (0, 1)))
    grouped = extended.reshape(fine_ch, coarse_rows + 1, 2, WIN + 1, 2)
    samples = []
    for offset in range(9):
        row_step, col_step = divmod(offset, 3)
        sample = grouped[
            :,
            row_step // 2 : row_step // 2 + coarse_rows,
            row_step % 2,
            col_step // 2 : col_step // 2 + WIN,
            col_step % 2,
        ]
        samples.append(sample.reshape(fine_ch, coarse_cells))
    stacked = jnp.stack(samples + [jnp.zeros_like(samples[0])]).reshape(5, -1, coarse_cells)
    taps = gathered[:, 480:680].reshape(members, 5, 40, -1)
    downsampled = (
        jnp.einsum("dbrc,bcs->drs", taps, stacked, preferred_element_type=jnp.float32)[:, :39]
        .astype(jnp.bfloat16)
        .reshape(coarse_ch, coarse_cells)
    )
    coarse_out = jax.nn.relu(
        coarse_res.astype(jnp.float32) + downsampled.astype(jnp.float32)
    ).astype(jnp.bfloat16)
    return (fine_out, coarse_out.reshape(coarse_in.shape))


def solution(mesh):
    return jax.shard_map(
        local,
        mesh=mesh,
        in_specs=(
            P("rows", "cols", None, None),
            P("rows", "cols", None, None),
            P(),
            P(),
            P(),
            P(),
            P(),
            P(None, "rows", None),
            P(None, "rows"),
            P("rows", None),
            P(),
            P(None, "rows"),
            P(),
            P(None, "rows", None),
        ),
        out_specs=(P("rows", "cols", None, None), P("rows", "cols", None, None)),
        check_vma=False,
    )
```

```python
import math

import jax
import jax.numpy as jnp
from jax import lax
import numpy as np
from jax.experimental import pallas as pl
from jax.experimental.pallas import tpu as pltpu
from jax.sharding import PartitionSpec as P

HEADS_FINE = 8
HEADS_COARSE = 16
WIN = 7


EPSILON = 1e-05


def padded_2(shard, sides, width):
    for axis, dim in sides:
        size, length = (lax.axis_size(axis), shard.shape[dim])
        up = [(i, (i + 1) % size) for i in range(size - 1)]
        down = [(j, i) for i, j in up]
        last = lax.slice_in_dim(shard, length - width, length, axis=dim)
        first = lax.slice_in_dim(shard, 0, width, axis=dim)
        before = lax.ppermute(last, axis, up)
        after = lax.ppermute(first, axis, down)
        shard = jnp.concatenate([before, shard, after], axis=dim)
    return shard


def passed_along(block, axis, distance):
    devices = range(lax.axis_size(axis))
    route = [(i - distance, i) for i in devices if i - distance in devices]
    return lax.ppermute(block, axis, route)


def normalize(values_in):
    values = values_in.astype(jnp.float32)
    center = jnp.mean(values, axis=0, keepdims=True)
    spread = jnp.mean((values - center) ** 2, axis=0, keepdims=True)
    return ((values - center) * lax.rsqrt(spread + EPSILON)).astype(jnp.bfloat16)


def to_windows(picture, head_count):
    channels, height, breadth = picture.shape
    head_width = channels // head_count
    shaped = picture.reshape(head_count, head_width, height // WIN, WIN, breadth // WIN, WIN)
    return shaped.transpose(0, 2, 4, 3, 5, 1).reshape(
        head_count, height // WIN, breadth // WIN, WIN * WIN, head_width
    )


def from_windows(blocks, height, breadth):
    head_count, grid_rows, grid_cols, cellcount, head_width = blocks.shape
    shaped = blocks.reshape(head_count, grid_rows, grid_cols, WIN, WIN, head_width)
    return shaped.transpose(0, 5, 1, 3, 2, 4).reshape(head_count * head_width, height, breadth)


def attend(queries, key_rows, value_rows, head_count):
    channels, height, breadth = queries.shape
    scaling = 1.0 / math.sqrt(channels // head_count)
    query_win = to_windows(queries, head_count)
    key_win = to_windows(key_rows, head_count)
    value_win = to_windows(value_rows, head_count)
    scores = (
        jnp.einsum("hrcqd,hrckd->hrcqk", query_win, key_win, preferred_element_type=jnp.float32)
        * scaling
    )
    row_max = jnp.max(scores, axis=-1, keepdims=True)
    exponent = jnp.exp(scores - row_max)
    probabilities = (exponent / jnp.sum(exponent, axis=-1, keepdims=True)).astype(jnp.bfloat16)
    mixture = jnp.einsum(
        "hrcqk,hrckd->hrcqd", probabilities, value_win, preferred_element_type=jnp.float32
    ).astype(jnp.bfloat16)
    return from_windows(mixture, height, breadth)


CELLS = WIN * WIN
RING = WIN + 2
HEAD_ROWS = 40
BLOCK_ROWS = 4 * HEAD_ROWS
TAP_ROWS = 5 * HEAD_ROWS + 8
SHARD_ROWS = 3 * BLOCK_ROWS + TAP_ROWS
SHARDS = 16
KEYS = 448
QUERIES = 96


def pack(inproj, outproj, expand, shrink, to_coarse):
    width = inproj.shape[-1]
    heads = jnp.concatenate([outproj.T[None], inproj[2:], inproj[:2]])
    taps = jnp.pad(to_coarse, ((0, 1), (0, 1), (0, 0))).reshape(5, 2, HEAD_ROWS, -1)
    return jnp.concatenate(
        [
            jnp.pad(heads, ((0, 0), (0, 1), (0, 0))).reshape(-1, width),
            jnp.pad(expand, ((0, 4), (0, 0))),
            jnp.pad(shrink.T, ((0, 4), (0, 0))),
            taps.transpose(0, 2, 1, 3).reshape(-1, width),
            jnp.zeros((8, width), inproj.dtype),
        ]
    )


def all_shards(mine):
    size = lax.axis_size("rows")
    swap = [(i, i ^ 1) for i in range(size)]
    ring = [(i, (i + (2 if i % 2 == 0 else -2)) % size) for i in range(size)]
    held = jnp.stack([mine, lax.ppermute(mine, "rows", swap)])
    pairs = [held]
    for _ in range(3):
        held = lax.ppermute(held, "rows", ring)
        pairs += [held, lax.ppermute(held, "rows", swap)]
    last = lax.ppermute(held[0], "rows", ring)
    singles = [last, lax.ppermute(last, "rows", swap)]
    place = lax.axis_index("rows")
    chip, core = place // 2, place % 2
    step = 1 - 2 * core
    owners = [2 * chip + core, 2 * chip + 1 - core]
    for k in (1, 2, 3):
        for sign in (-1, 1):
            away = 2 * ((chip + sign * step * k) % (size // 2))
            first = core if sign < 0 else 1 - core
            owners += [away + first, away + 1 - first]
    across = 2 * ((chip + 4) % (size // 2))
    owners += [across + core, across + 1 - core]
    return pairs, singles, jnp.stack(owners).astype(jnp.int32)


def tables():
    pick = np.zeros((QUERIES, KEYS), np.float32)
    bias = np.full((QUERIES, KEYS), -1e30, np.float32)
    centre = np.zeros((64, QUERIES), np.float32)
    for row in range(RING):
        for col in range(RING):
            down = 1 if row == 0 else 2 if row == RING - 1 else 0
            side = 1 if col == 0 else 2 if col == RING - 1 else 0
            window = 3 * side + down
            cell = (row - 1) % WIN * WIN + (col - 1) % WIN
            query = row * RING + col
            pick[query, window * CELLS + cell] = 1
            bias[query, window * CELLS : (window + 1) * CELLS] = 0
            if window == 0:
                centre[(row - 1) * 8 + col - 1, query] = 1
    bias[RING * RING :, :CELLS] = 0
    repeat = np.zeros((4 * CELLS, 64), np.float32)
    compact = np.zeros((CELLS, 64), np.float32)
    for row in range(2 * WIN):
        for col in range(2 * WIN):
            repeat[row * 2 * WIN + col, row // 2 * 8 + col // 2] = 1
    for row in range(WIN):
        for col in range(WIN):
            compact[row * WIN + col, row * 8 + col] = 1
    order = np.zeros((SHARDS * HEAD_ROWS, SHARDS * 39), np.float32)
    for shard in range(SHARDS):
        for row in range(39):
            order[shard * HEAD_ROWS + row, shard * 39 + row] = 1
    half = jnp.bfloat16
    return (
        jnp.asarray(bias),
        *(jnp.asarray(t).astype(half) for t in (pick, centre, repeat, compact, order)),
    )


def gelu(values):
    return values * (lax.erf(values * math.sqrt(0.5)) + 1.0) * 0.5


def norm_rows(values):
    center = jnp.mean(values, axis=1, keepdims=True)
    away = values - center
    spread = jnp.mean(away * away, axis=1, keepdims=True)
    return (away * lax.rsqrt(spread + EPSILON)).astype(jnp.bfloat16)


def nn(left, right):
    return lax.dot_general(
        left, right, (((1,), (0,)), ((), ())), preferred_element_type=jnp.float32
    )


def nt(left, right):
    return lax.dot_general(
        left, right, (((1,), (1,)), ((), ())), preferred_element_type=jnp.float32
    )


def coarse_kernel(
    owner_ref,
    edge_ref,
    *refs,
):
    sources, rest = refs[:9], refs[9:]
    (
        tiles_ref,
        depth_ref,
        taps_in_ref,
        fine_ref,
        to_fine_ref,
        bias_ref,
        pick_ref,
        centre_ref,
        repeat_ref,
        compact_ref,
        order_ref,
        fine_out_ref,
        coarse_out_ref,
        heads_ref,
        expand_ref,
        shrink_ref,
        taps_ref,
        proj_ref,
        hidden_ref,
        conv_ref,
        down_ref,
        sems,
    ) = rest
    slots = []
    for index, source in enumerate(sources):
        if index < 7:
            slots += [source.at[0], source.at[1]]
        else:
            slots += [source]
    spans = (
        (heads_ref, 0, BLOCK_ROWS),
        (expand_ref, BLOCK_ROWS, BLOCK_ROWS),
        (shrink_ref, 2 * BLOCK_ROWS, BLOCK_ROWS),
        (taps_ref, 3 * BLOCK_ROWS, TAP_ROWS),
    )
    copies = []
    for part, (target, first, count) in enumerate(spans):
        copies.append(
            [
                pltpu.make_async_copy(
                    slot.at[pl.ds(first, count)], target.at[owner_ref[place]], sems.at[part, place]
                )
                for place, slot in enumerate(slots)
            ]
        )
        for copy in copies[-1]:
            copy.start()

    def arrive(part):
        for copy in copies[part]:
            copy.wait()

    width = tiles_ref.shape[1]
    tiles = tiles_ref[...]
    normed = norm_rows(tiles.astype(jnp.float32))
    pick = pick_ref[...]
    arrive(0)
    heads = heads_ref[...].reshape(SHARDS * BLOCK_ROWS, width)
    proj_ref[...] = nt(heads, normed).reshape(SHARDS, BLOCK_ROWS, KEYS)
    mixed = nn(pick, tiles)
    for head in range(SHARDS):
        values = proj_ref[head, HEAD_ROWS : 2 * HEAD_ROWS].astype(jnp.bfloat16)
        queries = proj_ref[head, 2 * HEAD_ROWS : 3 * HEAD_ROWS].astype(jnp.bfloat16)
        keys = proj_ref[head, 3 * HEAD_ROWS :].astype(jnp.bfloat16)
        chosen = nt(pick, queries).astype(jnp.bfloat16)
        scores = nn(chosen, keys) * (1.0 / math.sqrt(39)) + bias_ref[...]
        exponent = jnp.exp(scores - jnp.max(scores, axis=1, keepdims=True))
        total = jnp.sum(exponent, axis=1, keepdims=True)
        probabilities = (exponent * (1.0 / total)).astype(jnp.bfloat16)
        attended = nt(probabilities, values).astype(jnp.bfloat16)
        mixed += nn(attended, heads_ref[head][:HEAD_ROWS])
    middle = mixed.astype(jnp.bfloat16)
    normed_mid = norm_rows(middle.astype(jnp.float32))
    query = lax.broadcasted_iota(jnp.int32, (QUERIES, 128), 0)
    column = query % RING
    outside = (
        ((query < RING) & (edge_ref[0] == 0))
        | ((query >= RING * (RING - 1)) & (edge_ref[1] == 0))
        | ((column == 0) & (edge_ref[2] == 0))
        | ((column == RING - 1) & (edge_ref[3] == 0))
    )
    inside = jnp.where(outside, 0.0, 1.0)[:, :1]
    arrive(1)
    conv_ref[CELLS // WIN * 8 :, :] = jnp.zeros((8, conv_ref.shape[1]), jnp.float32)
    chunk = 512
    for first in range(0, SHARDS * BLOCK_ROWS, chunk):
        span = pl.ds(first, chunk)
        rows = expand_ref[...].reshape(SHARDS * BLOCK_ROWS, width)[first : first + chunk]
        hidden = gelu(nt(normed_mid, rows)) * inside
        hidden_ref[:, span] = hidden.astype(jnp.bfloat16).astype(jnp.float32)
        for row in range(WIN):
            total = jnp.zeros((8, chunk), jnp.float32)
            for tap in range(9):
                down, side = divmod(tap, 3)
                window = hidden_ref[pl.ds((row + down) * RING + side, 8), span]
                total += depth_ref[tap : tap + 1, span] * window
            conv_ref[row * 8 : row * 8 + 8, span] = gelu(total)
    arrive(2)
    shrink = shrink_ref[...].reshape(SHARDS * BLOCK_ROWS, width)
    update = nn(conv_ref[...].astype(jnp.bfloat16), shrink)
    result = (nn(centre_ref[...], middle) + update).astype(jnp.bfloat16)
    spread = nn(repeat_ref[...], result).astype(jnp.bfloat16)
    upsampled = nt(spread, to_fine_ref[...])
    fine_out_ref[...] = jnp.maximum(
        fine_ref[...].astype(jnp.float32) + upsampled, 0.0
    ).astype(jnp.bfloat16)
    arrive(3)
    samples = taps_in_ref[...]
    for shard in range(SHARDS):
        four = nt(taps_ref[shard], samples[: 4 * 64])
        fifth = nt(taps_ref[shard][4 * HEAD_ROWS :], samples[4 * 64 :])
        total = fifth[:HEAD_ROWS]
        for block in range(4):
            rows = slice(block * HEAD_ROWS, (block + 1) * HEAD_ROWS)
            total += four[rows, block * 64 : (block + 1) * 64]
        down_ref[shard * HEAD_ROWS : (shard + 1) * HEAD_ROWS, :64] = total
    turned = down_ref[...].T.astype(jnp.bfloat16)
    downsampled = nn(turned, order_ref[...])[:CELLS]
    coarse_out_ref[...] = jnp.maximum(
        nn(compact_ref[...], result) + downsampled, 0.0
    ).astype(jnp.bfloat16)


def coarse_tail(sources, owners, edges, tiles, depth, samples, fine_res, to_fine):
    width = tiles.shape[1]
    fine_cells, fine_ch = fine_res.shape
    operands = (tiles, depth, samples, fine_res, to_fine, *tables())
    smem, vmem, anywhere = (
        pl.BlockSpec(memory_space=space) for space in (pltpu.SMEM, pltpu.VMEM, pl.ANY)
    )
    return pl.pallas_call(
        coarse_kernel,
        out_shape=(
            jax.ShapeDtypeStruct((fine_cells, fine_ch), jnp.bfloat16),
            jax.ShapeDtypeStruct((CELLS, width), jnp.bfloat16),
        ),
        in_specs=[smem, smem] + [anywhere] * len(sources) + [vmem] * len(operands),
        out_specs=(vmem, vmem),
        scratch_shapes=[
            pltpu.VMEM((SHARDS, BLOCK_ROWS, width), jnp.bfloat16),
            pltpu.VMEM((SHARDS, BLOCK_ROWS, width), jnp.bfloat16),
            pltpu.VMEM((SHARDS, BLOCK_ROWS, width), jnp.bfloat16),
            pltpu.VMEM((SHARDS, TAP_ROWS, width), jnp.bfloat16),
            pltpu.VMEM((SHARDS, BLOCK_ROWS, KEYS), jnp.float32),
            pltpu.VMEM((QUERIES, SHARDS * BLOCK_ROWS), jnp.float32),
            pltpu.VMEM((64, SHARDS * BLOCK_ROWS), jnp.float32),
            pltpu.VMEM((SHARDS * HEAD_ROWS, 128), jnp.float32),
            pltpu.SemaphoreType.DMA((4, SHARDS)),
        ],
        compiler_params=pltpu.CompilerParams(vmem_limit_bytes=48 * 1024 * 1024),
    )(owners, edges, *sources, *operands)


def around(tile):
    for axis in ("rows", "cols"):
        size = lax.axis_size(axis)
        up = [(i, i + 1) for i in range(size - 1)]
        down = [(j, i) for i, j in up]
        tile = jnp.concatenate(
            [tile, lax.ppermute(tile, axis, up), lax.ppermute(tile, axis, down)]
        )
    return jnp.pad(tile, ((0, KEYS - tile.shape[0]), (0, 0)))


def depthwise(padded, kernel):
    height = padded.shape[1] - 2
    breadth = padded.shape[2] - 2
    running = jnp.zeros((padded.shape[0], height, breadth), jnp.float32)
    for offset in range(9):
        row_step, col_step = divmod(offset, 3)
        sample = padded[:, row_step : row_step + height, col_step : col_step + breadth].astype(
            jnp.float32
        )
        running = running + kernel[offset][:, None, None] * sample
    return running


def local(
    fine_in,
    coarse_in,
    inproj_fine,
    outproj_fine,
    expand_fine,
    depth_fine,
    shrink_fine,
    inproj_coarse,
    outproj_coarse,
    expand_coarse,
    depth_coarse,
    shrink_coarse,
    to_fine,
    to_coarse,
):
    fine_ch = fine_in.shape[2]
    coarse_ch = coarse_in.shape[2]
    fine_cells = fine_in.shape[3]
    coarse_cells = coarse_in.shape[3]
    pairs, singles, owners = all_shards(
        pack(inproj_coarse, outproj_coarse, expand_coarse, shrink_coarse, to_coarse)
    )
    tiles = around(coarse_in.reshape(coarse_ch, coarse_cells).T)
    fine_rows = fine_cells // (2 * WIN)
    coarse_rows = coarse_cells // WIN
    fine_pic = fine_in.reshape(fine_ch, fine_rows, 2 * WIN)
    normed = normalize(fine_pic).reshape(fine_ch, fine_cells)
    projected = jnp.einsum(
        "tnc,cs->tns", inproj_fine, normed, preferred_element_type=jnp.float32
    ).astype(jnp.bfloat16)
    attended = attend(
        projected[0].reshape(fine_pic.shape),
        projected[1].reshape(fine_pic.shape),
        projected[2].reshape(fine_pic.shape),
        HEADS_FINE,
    ).reshape(fine_ch, fine_cells)
    middle = (
        fine_pic.reshape(fine_ch, fine_cells).astype(jnp.float32)
        + jnp.dot(outproj_fine, attended, preferred_element_type=jnp.float32)
    ).astype(jnp.bfloat16)
    normed_mid = normalize(middle)
    hidden = jax.nn.gelu(
        jnp.dot(expand_fine, normed_mid, preferred_element_type=jnp.float32), approximate=False
    ).astype(jnp.bfloat16)
    padded = padded_2(hidden.reshape(-1, fine_rows, 2 * WIN), (("rows", 1), ("cols", 2)), 1)
    convolved = (
        jax.nn.gelu(depthwise(padded, depth_fine), approximate=False)
        .astype(jnp.bfloat16)
        .reshape(-1, fine_cells)
    )
    fine_res = (
        middle.astype(jnp.float32)
        + jnp.dot(shrink_fine, convolved, preferred_element_type=jnp.float32)
    ).astype(jnp.bfloat16)
    fine_grid = fine_res.reshape(fine_ch, fine_rows, 2 * WIN)
    above_row = passed_along(fine_grid[:, -1:, :], "rows", 1)
    extended = jnp.concatenate([above_row, fine_grid], axis=1)
    beside = passed_along(extended[:, :, -1:], "cols", 1)
    extended = jnp.concatenate([beside, extended], axis=2)
    extended = jnp.pad(extended, ((0, 0), (0, 1), (0, 1)))
    grouped = extended.reshape(fine_ch, coarse_rows + 1, 2, WIN + 1, 2)
    samples = []
    for offset in range(9):
        row_step, col_step = divmod(offset, 3)
        sample = grouped[
            :,
            row_step // 2 : row_step // 2 + coarse_rows,
            row_step % 2,
            col_step // 2 : col_step // 2 + WIN,
            col_step % 2,
        ]
        samples.append(sample.reshape(fine_ch, coarse_cells))
    stacked = jnp.stack(samples + [jnp.zeros_like(samples[0])]).reshape(5, -1, coarse_cells)
    stacked = jnp.pad(stacked.transpose(0, 2, 1), ((0, 0), (0, 64 - coarse_cells), (0, 0)))
    depth = jnp.pad(depth_coarse.reshape(9, SHARDS, -1), ((0, 0), (0, 0), (0, 4)))
    row, col = lax.axis_index("rows"), lax.axis_index("cols")
    edges = jnp.stack(
        [row > 0, row < lax.axis_size("rows") - 1, col > 0, col < lax.axis_size("cols") - 1]
    ).astype(jnp.int32)
    fine_out, coarse_out = coarse_tail(
        pairs + singles,
        owners,
        edges,
        tiles,
        depth.reshape(9, -1),
        stacked.reshape(5 * 64, -1),
        fine_res.reshape(fine_ch, fine_cells).T,
        to_fine,
    )
    return (fine_out.T.reshape(fine_in.shape), coarse_out.T.reshape(coarse_in.shape))


def solution(mesh):
    return jax.shard_map(
        local,
        mesh=mesh,
        in_specs=(
            P("rows", "cols", None, None),
            P("rows", "cols", None, None),
            P(),
            P(),
            P(),
            P(),
            P(),
            P(None, "rows", None),
            P(None, "rows"),
            P("rows", None),
            P(),
            P(None, "rows"),
            P(),
            P(None, "rows", None),
        ),
        out_specs=(P("rows", "cols", None, None), P("rows", "cols", None, None)),
        check_vma=False,
    )
```

```python
import math

import jax
import jax.numpy as jnp
from jax import lax
import numpy as np
from jax.experimental import pallas as pl
from jax.experimental.pallas import tpu as pltpu
from jax.sharding import PartitionSpec as P

HEADS_FINE = 8
HEADS_COARSE = 16
WIN = 7


EPSILON = 1e-05


def padded_2(shard, sides, width):
    for axis, dim in sides:
        size, length = (lax.axis_size(axis), shard.shape[dim])
        up = [(i, (i + 1) % size) for i in range(size - 1)]
        down = [(j, i) for i, j in up]
        last = lax.slice_in_dim(shard, length - width, length, axis=dim)
        first = lax.slice_in_dim(shard, 0, width, axis=dim)
        before = lax.ppermute(last, axis, up)
        after = lax.ppermute(first, axis, down)
        shard = jnp.concatenate([before, shard, after], axis=dim)
    return shard


def passed_along(block, axis, distance):
    devices = range(lax.axis_size(axis))
    route = [(i - distance, i) for i in devices if i - distance in devices]
    return lax.ppermute(block, axis, route)


def normalize(values_in):
    values = values_in.astype(jnp.float32)
    center = jnp.mean(values, axis=0, keepdims=True)
    spread = jnp.mean((values - center) ** 2, axis=0, keepdims=True)
    return ((values - center) * lax.rsqrt(spread + EPSILON)).astype(jnp.bfloat16)


def to_windows(picture, head_count):
    channels, height, breadth = picture.shape
    head_width = channels // head_count
    shaped = picture.reshape(head_count, head_width, height // WIN, WIN, breadth // WIN, WIN)
    return shaped.transpose(0, 2, 4, 3, 5, 1).reshape(
        head_count, height // WIN, breadth // WIN, WIN * WIN, head_width
    )


def from_windows(blocks, height, breadth):
    head_count, grid_rows, grid_cols, cellcount, head_width = blocks.shape
    shaped = blocks.reshape(head_count, grid_rows, grid_cols, WIN, WIN, head_width)
    return shaped.transpose(0, 5, 1, 3, 2, 4).reshape(head_count * head_width, height, breadth)


def attend(queries, key_rows, value_rows, head_count):
    channels, height, breadth = queries.shape
    scaling = 1.0 / math.sqrt(channels // head_count)
    query_win = to_windows(queries, head_count)
    key_win = to_windows(key_rows, head_count)
    value_win = to_windows(value_rows, head_count)
    scores = (
        jnp.einsum("hrcqd,hrckd->hrcqk", query_win, key_win, preferred_element_type=jnp.float32)
        * scaling
    )
    row_max = jnp.max(scores, axis=-1, keepdims=True)
    exponent = jnp.exp(scores - row_max)
    probabilities = (exponent / jnp.sum(exponent, axis=-1, keepdims=True)).astype(jnp.bfloat16)
    mixture = jnp.einsum(
        "hrcqk,hrckd->hrcqd", probabilities, value_win, preferred_element_type=jnp.float32
    ).astype(jnp.bfloat16)
    return from_windows(mixture, height, breadth)


CELLS = WIN * WIN
RING = WIN + 2
HEAD_ROWS = 40
BLOCK_ROWS = 4 * HEAD_ROWS
TAP_ROWS = 5 * HEAD_ROWS + 8
SHARDS = 16
TILE = 56
KEYS = 9 * TILE + 8
QUERIES = 96
ABOVE = 200
BESIDE = 216


def pack_heads(inproj, outproj):
    heads = jnp.concatenate([outproj.T[None], inproj[2:], inproj[:2]])
    return jnp.pad(heads, ((0, 0), (0, 1), (0, 0))).reshape(BLOCK_ROWS, -1)


def pack_rest(expand, shrink, to_coarse):
    width = expand.shape[-1]
    taps = jnp.pad(to_coarse, ((0, 1), (0, 1), (0, 0))).reshape(5, 2, HEAD_ROWS, -1)
    return jnp.concatenate(
        [
            jnp.pad(expand, ((0, 4), (0, 0))),
            jnp.pad(shrink.T, ((0, 4), (0, 0))),
            taps.transpose(0, 2, 1, 3).reshape(-1, width),
            jnp.zeros((8, width), expand.dtype),
        ]
    )


def all_shards(mine):
    size = lax.axis_size("rows")
    swap = [(i, i ^ 1) for i in range(size)]
    ring = [(i, (i + (2 if i % 2 == 0 else -2)) % size) for i in range(size)]
    held = jnp.stack([mine, lax.ppermute(mine, "rows", swap)])
    pairs = [held]
    for _ in range(3):
        held = lax.ppermute(held, "rows", ring)
        pairs += [held, lax.ppermute(held, "rows", swap)]
    last = lax.ppermute(held[0], "rows", ring)
    singles = [last, lax.ppermute(last, "rows", swap)]
    return pairs + singles


def attention_tables():
    pick = np.zeros((QUERIES, KEYS), np.float32)
    bias = np.full((QUERIES, KEYS), -1e30, np.float32)
    for row in range(RING):
        for col in range(RING):
            down = 1 if row == 0 else 2 if row == RING - 1 else 0
            side = 1 if col == 0 else 2 if col == RING - 1 else 0
            first = (3 * side + down) * TILE
            query = row * RING + col
            pick[query, first + (row - 1) % WIN * WIN + (col - 1) % WIN] = 1
            bias[query, first : first + CELLS] = 0
    bias[RING * RING :, :CELLS] = 0
    return jnp.asarray(bias), jnp.asarray(pick).astype(jnp.bfloat16)


def tail_tables():
    side = 2 * WIN
    centre = np.zeros((64, QUERIES), np.float32)
    repeat = np.zeros((side * side, 64), np.float32)
    compact = np.zeros((CELLS, 64), np.float32)
    sample = np.zeros((5 * 64, 512), np.float32)
    order = np.zeros((SHARDS * HEAD_ROWS, SHARDS * 39), np.float32)
    for cell in range(CELLS):
        row, col = divmod(cell, WIN)
        centre[row * 8 + col, (row + 1) * RING + col + 1] = 1
        compact[cell, row * 8 + col] = 1
        for tap in range(9):
            down, right = 2 * row + tap // 3 - 1, 2 * col + tap % 3 - 1
            if right < 0:
                source = BESIDE + down + 1
            elif down < 0:
                source = ABOVE + right
            else:
                source = down * side + right
            sample[tap // 2 * 64 + cell, tap % 2 * 256 + source] = 1
    for cell in range(side * side):
        row, col = divmod(cell, side)
        repeat[cell, row // 2 * 8 + col // 2] = 1
    for shard in range(SHARDS):
        for row in range(39):
            order[shard * HEAD_ROWS + row, shard * 39 + row] = 1
    return tuple(
        jnp.asarray(t).astype(jnp.bfloat16) for t in (centre, repeat, compact, sample, order)
    )


def gelu(values):
    return values * (lax.erf(values * math.sqrt(0.5)) + 1.0) * 0.5


def norm_rows(values):
    center = jnp.mean(values, axis=1, keepdims=True)
    away = values - center
    spread = jnp.mean(away * away, axis=1, keepdims=True)
    return (away * lax.rsqrt(spread + EPSILON)).astype(jnp.bfloat16)


def nn(left, right):
    return lax.dot_general(
        left, right, (((1,), (0,)), ((), ())), preferred_element_type=jnp.float32
    )


def nt(left, right):
    return lax.dot_general(
        left, right, (((1,), (1,)), ((), ())), preferred_element_type=jnp.float32
    )


def attention_kernel(
    centre_ref,
    above_ref,
    below_ref,
    left_ref,
    right_ref,
    bias_ref,
    pick_ref,
    *refs,
):
    sources, (middle_ref, heads_ref, tiles_ref, proj_ref, sems) = refs[:9], refs[9:]
    copies = []
    for index, source in enumerate(sources):
        target = heads_ref.at[pl.ds(2 * index, 2)] if index < 7 else heads_ref.at[7 + index]
        copies.append(pltpu.make_async_copy(source, target, sems.at[index]))
        copies[-1].start()
    tiles_ref[9 * TILE :, :] = jnp.zeros((KEYS - 9 * TILE, tiles_ref.shape[1]), jnp.float32)
    first = 0
    for piece in (centre_ref, above_ref, below_ref, left_ref, right_ref):
        count = piece.shape[0]
        tiles_ref[first : first + count, :] = piece[...].astype(jnp.float32)
        first += count
    tiles = tiles_ref[...]
    normed = norm_rows(tiles)
    pick = pick_ref[...]
    mixed = nn(pick, tiles.astype(jnp.bfloat16))
    for copy in copies:
        copy.wait()
    heads = heads_ref[...].reshape(SHARDS * BLOCK_ROWS, tiles.shape[1])
    proj_ref[...] = nt(heads, normed).reshape(SHARDS, BLOCK_ROWS, KEYS)
    for head in range(SHARDS):
        values = proj_ref[head, HEAD_ROWS : 2 * HEAD_ROWS].astype(jnp.bfloat16)
        queries = proj_ref[head, 2 * HEAD_ROWS : 3 * HEAD_ROWS].astype(jnp.bfloat16)
        keys = proj_ref[head, 3 * HEAD_ROWS :].astype(jnp.bfloat16)
        chosen = nt(pick, queries).astype(jnp.bfloat16)
        scores = nn(chosen, keys) * (1.0 / math.sqrt(39)) + bias_ref[...]
        exponent = jnp.exp(scores - jnp.max(scores, axis=1, keepdims=True))
        total = jnp.sum(exponent, axis=1, keepdims=True)
        probabilities = (exponent * (1.0 / total)).astype(jnp.bfloat16)
        attended = nt(probabilities, values).astype(jnp.bfloat16)
        mixed += nn(attended, heads_ref[head][:HEAD_ROWS])
    middle_ref[...] = mixed.astype(jnp.bfloat16)


def coarse_attention(sources, tiles):
    width = tiles[0].shape[1]
    operands = (*tiles, *attention_tables())
    vmem, anywhere = (pl.BlockSpec(memory_space=space) for space in (pltpu.VMEM, pl.ANY))
    return pl.pallas_call(
        attention_kernel,
        out_shape=jax.ShapeDtypeStruct((QUERIES, width), jnp.bfloat16),
        in_specs=[vmem] * len(operands) + [anywhere] * len(sources),
        out_specs=vmem,
        scratch_shapes=[
            pltpu.VMEM((SHARDS, BLOCK_ROWS, width), jnp.bfloat16),
            pltpu.VMEM((KEYS, width), jnp.float32),
            pltpu.VMEM((SHARDS, BLOCK_ROWS, KEYS), jnp.float32),
            pltpu.SemaphoreType.DMA((9,)),
        ],
        compiler_params=pltpu.CompilerParams(vmem_limit_bytes=32 * 1024 * 1024),
    )(*operands, *sources)


def tail_kernel(
    edge_ref,
    gathered_ref,
    middle_ref,
    depth_ref,
    fine_ref,
    above_ref,
    beside_ref,
    to_fine_ref,
    centre_ref,
    repeat_ref,
    compact_ref,
    sample_ref,
    order_ref,
    fine_out_ref,
    coarse_out_ref,
    expand_ref,
    shrink_ref,
    taps_ref,
    hidden_ref,
    conv_ref,
    field_ref,
    twice_ref,
    down_ref,
    sems,
):
    spans = (
        (expand_ref, 0, BLOCK_ROWS),
        (shrink_ref, BLOCK_ROWS, BLOCK_ROWS),
        (taps_ref, 2 * BLOCK_ROWS, TAP_ROWS),
    )
    copies = [
        pltpu.make_async_copy(gathered_ref.at[:, pl.ds(first, count)], target, sems.at[part])
        for part, (target, first, count) in enumerate(spans)
    ]
    for copy in copies:
        copy.start()
    width = middle_ref.shape[1]
    channels = fine_ref.shape[1]
    middle = middle_ref[...]
    normed_mid = norm_rows(middle.astype(jnp.float32))
    query = lax.broadcasted_iota(jnp.int32, (QUERIES, 128), 0)
    column = query % RING
    outside = (
        ((query < RING) & (edge_ref[0] == 0))
        | ((query >= RING * (RING - 1)) & (edge_ref[1] == 0))
        | ((column == 0) & (edge_ref[2] == 0))
        | ((column == RING - 1) & (edge_ref[3] == 0))
    )
    inside = jnp.where(outside, 0.0, 1.0)[:, :1]
    conv_ref[8 * WIN :, :] = jnp.zeros((8, conv_ref.shape[1]), jnp.float32)
    field_ref[...] = jnp.zeros(field_ref.shape, jnp.float32)
    field_ref[: fine_ref.shape[0], :] = fine_ref[...].astype(jnp.float32)
    field_ref[ABOVE : ABOVE + 16, :] = above_ref[...].astype(jnp.float32)
    field_ref[BESIDE : BESIDE + 16, :] = beside_ref[...].astype(jnp.float32)
    twice_ref[...] = jnp.zeros(twice_ref.shape, jnp.float32)
    twice_ref[:256, :channels] = field_ref[...]
    twice_ref[256:, channels:] = field_ref[...]
    samples = nn(sample_ref[...], twice_ref[...].astype(jnp.bfloat16)).astype(jnp.bfloat16)
    copies[0].wait()
    chunk = 512
    expand = expand_ref[...].reshape(SHARDS * BLOCK_ROWS, width)
    for first in range(0, SHARDS * BLOCK_ROWS, chunk):
        span = pl.ds(first, chunk)
        hidden = gelu(nt(normed_mid, expand[first : first + chunk])) * inside
        hidden_ref[:, span] = hidden.astype(jnp.bfloat16).astype(jnp.float32)
        for row in range(WIN):
            total = jnp.zeros((8, chunk), jnp.float32)
            for tap in range(9):
                down, side = divmod(tap, 3)
                window = hidden_ref[pl.ds((row + down) * RING + side, 8), span]
                total += depth_ref[tap : tap + 1, span] * window
            conv_ref[row * 8 : row * 8 + 8, span] = gelu(total)
    copies[1].wait()
    shrink = shrink_ref[...].reshape(SHARDS * BLOCK_ROWS, width)
    update = nn(conv_ref[...].astype(jnp.bfloat16), shrink)
    result = (nn(centre_ref[...], middle) + update).astype(jnp.bfloat16)
    spread = nn(repeat_ref[...], result).astype(jnp.bfloat16)
    upsampled = nt(spread, to_fine_ref[...])
    fine_out_ref[...] = jnp.maximum(
        fine_ref[...].astype(jnp.float32) + upsampled, 0.0
    ).astype(jnp.bfloat16)
    copies[2].wait()
    for shard in range(SHARDS):
        four = nt(taps_ref[shard], samples[: 4 * 64])
        fifth = nt(taps_ref[shard][4 * HEAD_ROWS :], samples[4 * 64 :])
        total = fifth[:HEAD_ROWS]
        for block in range(4):
            rows = slice(block * HEAD_ROWS, (block + 1) * HEAD_ROWS)
            total += four[rows, block * 64 : (block + 1) * 64]
        down_ref[shard * HEAD_ROWS : (shard + 1) * HEAD_ROWS, :64] = total
    turned = down_ref[...].T.astype(jnp.bfloat16)
    downsampled = nn(turned, order_ref[...])[:CELLS]
    coarse_out_ref[...] = jnp.maximum(
        nn(compact_ref[...], result) + downsampled, 0.0
    ).astype(jnp.bfloat16)


def coarse_tail(gathered, edges, middle, depth, fine_res, above, beside, to_fine):
    width = middle.shape[1]
    fine_cells, fine_ch = fine_res.shape
    operands = (middle, depth, fine_res, above, beside, to_fine, *tail_tables())
    smem, vmem, anywhere = (
        pl.BlockSpec(memory_space=space) for space in (pltpu.SMEM, pltpu.VMEM, pl.ANY)
    )
    return pl.pallas_call(
        tail_kernel,
        out_shape=(
            jax.ShapeDtypeStruct((fine_cells, fine_ch), jnp.bfloat16),
            jax.ShapeDtypeStruct((CELLS, width), jnp.bfloat16),
        ),
        in_specs=[smem, anywhere] + [vmem] * len(operands),
        out_specs=(vmem, vmem),
        scratch_shapes=[
            pltpu.VMEM((SHARDS, BLOCK_ROWS, width), jnp.bfloat16),
            pltpu.VMEM((SHARDS, BLOCK_ROWS, width), jnp.bfloat16),
            pltpu.VMEM((SHARDS, TAP_ROWS, width), jnp.bfloat16),
            pltpu.VMEM((QUERIES, SHARDS * BLOCK_ROWS), jnp.float32),
            pltpu.VMEM((64, SHARDS * BLOCK_ROWS), jnp.float32),
            pltpu.VMEM((256, fine_ch), jnp.float32),
            pltpu.VMEM((512, 2 * fine_ch), jnp.float32),
            pltpu.VMEM((SHARDS * HEAD_ROWS, 128), jnp.float32),
            pltpu.SemaphoreType.DMA((3,)),
        ],
        compiler_params=pltpu.CompilerParams(vmem_limit_bytes=40 * 1024 * 1024),
    )(edges, gathered, *operands)


def neighbours(tile, axis):
    size = lax.axis_size(axis)
    up = [(i, i + 1) for i in range(size - 1)]
    down = [(j, i) for i, j in up]
    return lax.ppermute(tile, axis, up), lax.ppermute(tile, axis, down)


def depthwise(padded, kernel):
    height = padded.shape[1] - 2
    breadth = padded.shape[2] - 2
    running = jnp.zeros((padded.shape[0], height, breadth), jnp.float32)
    for offset in range(9):
        row_step, col_step = divmod(offset, 3)
        sample = padded[:, row_step : row_step + height, col_step : col_step + breadth].astype(
            jnp.float32
        )
        running = running + kernel[offset][:, None, None] * sample
    return running


def local(
    fine_in,
    coarse_in,
    inproj_fine,
    outproj_fine,
    expand_fine,
    depth_fine,
    shrink_fine,
    inproj_coarse,
    outproj_coarse,
    expand_coarse,
    depth_coarse,
    shrink_coarse,
    to_fine,
    to_coarse,
):
    fine_ch = fine_in.shape[2]
    coarse_ch = coarse_in.shape[2]
    fine_cells = fine_in.shape[3]
    coarse_cells = coarse_in.shape[3]
    gathered = lax.all_gather(pack_rest(expand_coarse, shrink_coarse, to_coarse), "rows")
    heads = all_shards(pack_heads(inproj_coarse, outproj_coarse))
    tile = jnp.pad(coarse_in.reshape(coarse_ch, coarse_cells).T, ((0, TILE - coarse_cells), (0, 0)))
    above, below = neighbours(tile, "rows")
    left, right = neighbours(jnp.concatenate([tile, above, below]), "cols")
    coarse_mid = coarse_attention(heads, (tile, above, below, left, right))
    fine_rows = fine_cells // (2 * WIN)
    coarse_rows = coarse_cells // WIN
    fine_pic = fine_in.reshape(fine_ch, fine_rows, 2 * WIN)
    normed = normalize(fine_pic).reshape(fine_ch, fine_cells)
    projected = jnp.einsum(
        "tnc,cs->tns", inproj_fine, normed, preferred_element_type=jnp.float32
    ).astype(jnp.bfloat16)
    attended = attend(
        projected[0].reshape(fine_pic.shape),
        projected[1].reshape(fine_pic.shape),
        projected[2].reshape(fine_pic.shape),
        HEADS_FINE,
    ).reshape(fine_ch, fine_cells)
    middle = (
        fine_pic.reshape(fine_ch, fine_cells).astype(jnp.float32)
        + jnp.dot(outproj_fine, attended, preferred_element_type=jnp.float32)
    ).astype(jnp.bfloat16)
    normed_mid = normalize(middle)
    hidden = jax.nn.gelu(
        jnp.dot(expand_fine, normed_mid, preferred_element_type=jnp.float32), approximate=False
    ).astype(jnp.bfloat16)
    padded = padded_2(hidden.reshape(-1, fine_rows, 2 * WIN), (("rows", 1), ("cols", 2)), 1)
    convolved = (
        jax.nn.gelu(depthwise(padded, depth_fine), approximate=False)
        .astype(jnp.bfloat16)
        .reshape(-1, fine_cells)
    )
    fine_res = (
        middle.astype(jnp.float32)
        + jnp.dot(shrink_fine, convolved, preferred_element_type=jnp.float32)
    ).astype(jnp.bfloat16)
    field = fine_res.T
    above_row = passed_along(field[-2 * WIN :], "rows", 1)
    beside = passed_along(
        jnp.concatenate([above_row[-1:], field[2 * WIN - 1 :: 2 * WIN]]), "cols", 1
    )
    depth = jnp.pad(depth_coarse.reshape(9, SHARDS, -1), ((0, 0), (0, 0), (0, 4)))
    row, col = lax.axis_index("rows"), lax.axis_index("cols")
    edges = jnp.stack(
        [row > 0, row < lax.axis_size("rows") - 1, col > 0, col < lax.axis_size("cols") - 1]
    ).astype(jnp.int32)
    fine_out, coarse_out = coarse_tail(
        gathered,
        edges,
        coarse_mid,
        depth.reshape(9, -1),
        field,
        jnp.pad(above_row, ((0, 2), (0, 0))),
        jnp.pad(beside, ((0, 1), (0, 0))),
        to_fine,
    )
    return (fine_out.T.reshape(fine_in.shape), coarse_out.T.reshape(coarse_in.shape))


def solution(mesh):
    return jax.shard_map(
        local,
        mesh=mesh,
        in_specs=(
            P("rows", "cols", None, None),
            P("rows", "cols", None, None),
            P(),
            P(),
            P(),
            P(),
            P(),
            P(None, "rows", None),
            P(None, "rows"),
            P("rows", None),
            P(),
            P(None, "rows"),
            P(),
            P(None, "rows", None),
        ),
        out_specs=(P("rows", "cols", None, None), P("rows", "cols", None, None)),
        check_vma=False,
    )
```

```python
import math

import jax
import jax.numpy as jnp
from jax import lax
import numpy as np
from jax.experimental import pallas as pl
from jax.experimental.pallas import tpu as pltpu
from jax.sharding import PartitionSpec as P

HEADS_FINE = 8
HEADS_COARSE = 16
WIN = 7


EPSILON = 1e-05


def padded_2(shard, sides, width):
    for axis, dim in sides:
        size, length = (lax.axis_size(axis), shard.shape[dim])
        up = [(i, (i + 1) % size) for i in range(size - 1)]
        down = [(j, i) for i, j in up]
        last = lax.slice_in_dim(shard, length - width, length, axis=dim)
        first = lax.slice_in_dim(shard, 0, width, axis=dim)
        before = lax.ppermute(last, axis, up)
        after = lax.ppermute(first, axis, down)
        shard = jnp.concatenate([before, shard, after], axis=dim)
    return shard


def passed_along(block, axis, distance):
    devices = range(lax.axis_size(axis))
    route = [(i - distance, i) for i in devices if i - distance in devices]
    return lax.ppermute(block, axis, route)


def normalize(values_in):
    values = values_in.astype(jnp.float32)
    center = jnp.mean(values, axis=0, keepdims=True)
    spread = jnp.mean((values - center) ** 2, axis=0, keepdims=True)
    return ((values - center) * lax.rsqrt(spread + EPSILON)).astype(jnp.bfloat16)


def to_windows(picture, head_count):
    channels, height, breadth = picture.shape
    head_width = channels // head_count
    shaped = picture.reshape(head_count, head_width, height // WIN, WIN, breadth // WIN, WIN)
    return shaped.transpose(0, 2, 4, 3, 5, 1).reshape(
        head_count, height // WIN, breadth // WIN, WIN * WIN, head_width
    )


def from_windows(blocks, height, breadth):
    head_count, grid_rows, grid_cols, cellcount, head_width = blocks.shape
    shaped = blocks.reshape(head_count, grid_rows, grid_cols, WIN, WIN, head_width)
    return shaped.transpose(0, 5, 1, 3, 2, 4).reshape(head_count * head_width, height, breadth)


def attend(queries, key_rows, value_rows, head_count):
    channels, height, breadth = queries.shape
    scaling = 1.0 / math.sqrt(channels // head_count)
    query_win = to_windows(queries, head_count)
    key_win = to_windows(key_rows, head_count)
    value_win = to_windows(value_rows, head_count)
    scores = (
        jnp.einsum("hrcqd,hrckd->hrcqk", query_win, key_win, preferred_element_type=jnp.float32)
        * scaling
    )
    row_max = jnp.max(scores, axis=-1, keepdims=True)
    exponent = jnp.exp(scores - row_max)
    probabilities = (exponent / jnp.sum(exponent, axis=-1, keepdims=True)).astype(jnp.bfloat16)
    mixture = jnp.einsum(
        "hrcqk,hrckd->hrcqd", probabilities, value_win, preferred_element_type=jnp.float32
    ).astype(jnp.bfloat16)
    return from_windows(mixture, height, breadth)


CELLS = WIN * WIN
RING = WIN + 2
HEAD_ROWS = 40
BLOCK_ROWS = 4 * HEAD_ROWS
TAP_ROWS = 5 * HEAD_ROWS + 8
SHARDS = 16
TILE = 56
KEYS = 9 * TILE + 8
QUERIES = 96
ABOVE = 200
BESIDE = 216


def pack(inproj, outproj, expand, shrink, to_coarse):
    width = expand.shape[-1]
    heads = jnp.concatenate([outproj.T[None], inproj[2:], inproj[:2]])
    taps = jnp.pad(to_coarse, ((0, 1), (0, 1), (0, 0))).reshape(5, 2, HEAD_ROWS, -1)
    return jnp.concatenate(
        [
            jnp.pad(heads, ((0, 0), (0, 1), (0, 0))).reshape(BLOCK_ROWS, -1),
            jnp.pad(expand, ((0, 4), (0, 0))),
            jnp.pad(shrink.T, ((0, 4), (0, 0))),
            taps.transpose(0, 2, 1, 3).reshape(-1, width),
            jnp.zeros((8, width), expand.dtype),
        ]
    )


def attention_tables():
    pick = np.zeros((QUERIES, KEYS), np.float32)
    bias = np.full((QUERIES, KEYS), -1e30, np.float32)
    for row in range(RING):
        for col in range(RING):
            down = 1 if row == 0 else 2 if row == RING - 1 else 0
            side = 1 if col == 0 else 2 if col == RING - 1 else 0
            first = (3 * side + down) * TILE
            query = row * RING + col
            pick[query, first + (row - 1) % WIN * WIN + (col - 1) % WIN] = 1
            bias[query, first : first + CELLS] = 0
    bias[RING * RING :, :CELLS] = 0
    return jnp.asarray(bias), jnp.asarray(pick).astype(jnp.bfloat16)


def sample_table():
    side = 2 * WIN
    sample = np.zeros((5 * 64, 512), np.float32)
    for cell in range(CELLS):
        row, col = divmod(cell, WIN)
        for tap in range(9):
            down, right = 2 * row + tap // 3 - 1, 2 * col + tap % 3 - 1
            if right < 0:
                source = BESIDE + down + 1
            elif down < 0:
                source = ABOVE + right
            else:
                source = down * side + right
            sample[tap // 2 * 64 + cell, tap % 2 * 256 + source] = 1
    return jnp.asarray(sample).astype(jnp.bfloat16)


def cell_tables():
    side = 2 * WIN
    centre = np.zeros((64, QUERIES), np.float32)
    repeat = np.zeros((side * side, 64), np.float32)
    compact = np.zeros((CELLS, 64), np.float32)
    for cell in range(CELLS):
        row, col = divmod(cell, WIN)
        centre[row * 8 + col, (row + 1) * RING + col + 1] = 1
        compact[cell, row * 8 + col] = 1
    for cell in range(side * side):
        row, col = divmod(cell, side)
        repeat[cell, row // 2 * 8 + col // 2] = 1
    return tuple(jnp.asarray(t).astype(jnp.bfloat16) for t in (centre, repeat, compact))


def gelu(values):
    return values * (lax.erf(values * math.sqrt(0.5)) + 1.0) * 0.5


def norm_rows(values):
    center = jnp.mean(values, axis=1, keepdims=True)
    away = values - center
    spread = jnp.mean(away * away, axis=1, keepdims=True)
    return (away * lax.rsqrt(spread + EPSILON)).astype(jnp.bfloat16)


def nn(left, right):
    return lax.dot_general(
        left, right, (((1,), (0,)), ((), ())), preferred_element_type=jnp.float32
    )


def nt(left, right):
    return lax.dot_general(
        left, right, (((1,), (1,)), ((), ())), preferred_element_type=jnp.float32
    )


def tiles_kernel(
    centre_ref, above_ref, below_ref, left_ref, right_ref, pick_ref, normed_ref, own_ref, tiles_ref
):
    tiles_ref[9 * TILE :, :] = jnp.zeros((KEYS - 9 * TILE, tiles_ref.shape[1]), jnp.float32)
    first = 0
    for piece in (centre_ref, above_ref, below_ref, left_ref, right_ref):
        count = piece.shape[0]
        tiles_ref[first : first + count, :] = piece[...].astype(jnp.float32)
        first += count
    tiles = tiles_ref[...]
    normed_ref[...] = norm_rows(tiles)
    own_ref[...] = nn(pick_ref[...], tiles.astype(jnp.bfloat16)).astype(jnp.bfloat16)


def normed_tiles(tiles, pick):
    width = tiles[0].shape[1]
    vmem = pl.BlockSpec(memory_space=pltpu.VMEM)
    return pl.pallas_call(
        tiles_kernel,
        out_shape=(
            jax.ShapeDtypeStruct((KEYS, width), jnp.bfloat16),
            jax.ShapeDtypeStruct((QUERIES, width), jnp.bfloat16),
        ),
        in_specs=[vmem] * 6,
        out_specs=(vmem, vmem),
        scratch_shapes=[pltpu.VMEM((KEYS, width), jnp.float32)],
        compiler_params=pltpu.CompilerParams(vmem_limit_bytes=16 * 1024 * 1024),
    )(*tiles, pick)


def sample_kernel(fine_ref, above_ref, beside_ref, sample_ref, samples_ref, field_ref, twice_ref):
    channels = fine_ref.shape[1]
    field_ref[...] = jnp.zeros(field_ref.shape, jnp.float32)
    field_ref[: fine_ref.shape[0], :] = fine_ref[...].astype(jnp.float32)
    field_ref[ABOVE : ABOVE + 16, :] = above_ref[...].astype(jnp.float32)
    field_ref[BESIDE : BESIDE + 16, :] = beside_ref[...].astype(jnp.float32)
    twice_ref[...] = jnp.zeros(twice_ref.shape, jnp.float32)
    twice_ref[:256, :channels] = field_ref[...]
    twice_ref[256:, channels:] = field_ref[...]
    samples_ref[...] = nn(sample_ref[...], twice_ref[...].astype(jnp.bfloat16)).astype(jnp.bfloat16)


def tap_samples(fine_res, above, beside):
    channels = fine_res.shape[1]
    vmem = pl.BlockSpec(memory_space=pltpu.VMEM)
    return pl.pallas_call(
        sample_kernel,
        out_shape=jax.ShapeDtypeStruct((5 * 64, 2 * channels), jnp.bfloat16),
        in_specs=[vmem] * 4,
        out_specs=vmem,
        scratch_shapes=[
            pltpu.VMEM((256, channels), jnp.float32),
            pltpu.VMEM((512, 2 * channels), jnp.float32),
        ],
        compiler_params=pltpu.CompilerParams(vmem_limit_bytes=16 * 1024 * 1024),
    )(fine_res, above, beside, sample_table())


def coarse_kernel(
    edge_ref,
    gathered_ref,
    normed_ref,
    own_ref,
    bias_ref,
    pick_ref,
    depth_ref,
    samples_ref,
    fine_ref,
    to_fine_ref,
    centre_ref,
    repeat_ref,
    compact_ref,
    fine_out_ref,
    coarse_out_ref,
    heads_ref,
    expand_ref,
    shrink_ref,
    taps_ref,
    proj_ref,
    chosen_ref,
    chance_ref,
    attended_ref,
    hidden_ref,
    conv_ref,
    down_ref,
    sems,
):
    spans = (
        (heads_ref, 0, BLOCK_ROWS),
        (expand_ref, BLOCK_ROWS, BLOCK_ROWS),
        (shrink_ref, 2 * BLOCK_ROWS, BLOCK_ROWS),
        (taps_ref, 3 * BLOCK_ROWS, TAP_ROWS),
    )
    copies = [
        pltpu.make_async_copy(gathered_ref.at[:, pl.ds(first, count)], target, sems.at[part])
        for part, (target, first, count) in enumerate(spans)
    ]
    for copy in copies:
        copy.start()
    width = own_ref.shape[1]
    query = lax.broadcasted_iota(jnp.int32, (QUERIES, 128), 0)
    column = query % RING
    outside = (
        ((query < RING) & (edge_ref[0] == 0))
        | ((query >= RING * (RING - 1)) & (edge_ref[1] == 0))
        | ((column == 0) & (edge_ref[2] == 0))
        | ((column == RING - 1) & (edge_ref[3] == 0))
    )
    inside = jnp.where(outside, 0.0, 1.0)[:, :1]
    conv_ref[8 * WIN :, :] = jnp.zeros((8, conv_ref.shape[1]), jnp.float32)
    copies[0].wait()
    heads = heads_ref[:, 32:BLOCK_ROWS, :].reshape(SHARDS * 128, width)
    proj_ref[...] = nt(heads, normed_ref[...]).reshape(SHARDS, 128, KEYS)
    pick = pick_ref[...]
    for head in range(SHARDS):
        queries = proj_ref[head, 48:88].astype(jnp.bfloat16)
        chosen_ref[head] = nt(pick, queries)
    bias = bias_ref[...]
    for head in range(SHARDS):
        keys = proj_ref[head, 88:128].astype(jnp.bfloat16)
        scores = nn(chosen_ref[head].astype(jnp.bfloat16), keys) * (1.0 / math.sqrt(39)) + bias
        exponent = jnp.exp(scores - jnp.max(scores, axis=1, keepdims=True))
        total = jnp.sum(exponent, axis=1, keepdims=True)
        chance_ref[head] = (exponent * (1.0 / total)).astype(jnp.bfloat16)
    for head in range(SHARDS):
        values = proj_ref[head, 8:48].astype(jnp.bfloat16)
        attended_ref[head] = nt(chance_ref[head], values)
    mixed = own_ref[...].astype(jnp.float32)
    for head in range(SHARDS):
        mixed += nn(attended_ref[head].astype(jnp.bfloat16), heads_ref[head][:HEAD_ROWS])
    middle = mixed.astype(jnp.bfloat16)
    normed_mid = norm_rows(middle.astype(jnp.float32))
    copies[1].wait()
    chunk = 512
    expand = expand_ref[...].reshape(SHARDS * BLOCK_ROWS, width)
    for first in range(0, SHARDS * BLOCK_ROWS, chunk):
        span = pl.ds(first, chunk)
        hidden = gelu(nt(normed_mid, expand[first : first + chunk])) * inside
        hidden_ref[:, span] = hidden.astype(jnp.bfloat16).astype(jnp.float32)
        for row in range(WIN):
            total = jnp.zeros((8, chunk), jnp.float32)
            for tap in range(9):
                down, side = divmod(tap, 3)
                window = hidden_ref[pl.ds((row + down) * RING + side, 8), span]
                total += depth_ref[tap : tap + 1, span] * window
            conv_ref[row * 8 : row * 8 + 8, span] = gelu(total)
    copies[2].wait()
    shrink = shrink_ref[...].reshape(SHARDS * BLOCK_ROWS, width)
    update = nn(conv_ref[...].astype(jnp.bfloat16), shrink)
    result = (nn(centre_ref[...], middle) + update).astype(jnp.bfloat16)
    spread = nn(repeat_ref[...], result).astype(jnp.bfloat16)
    upsampled = nt(spread, to_fine_ref[...])
    fine_out_ref[...] = jnp.maximum(
        fine_ref[...].astype(jnp.float32) + upsampled, 0.0
    ).astype(jnp.bfloat16)
    copies[3].wait()
    samples = samples_ref[...]
    for shard in range(SHARDS):
        four = nt(taps_ref[shard], samples[: 4 * 64])
        fifth = nt(taps_ref[shard][4 * HEAD_ROWS :], samples[4 * 64 :])
        total = fifth[:HEAD_ROWS]
        for block in range(4):
            rows = slice(block * HEAD_ROWS, (block + 1) * HEAD_ROWS)
            total += four[rows, block * 64 : (block + 1) * 64]
        down_ref[shard * 39 : shard * 39 + HEAD_ROWS, :64] = total
    downsampled = down_ref[...].T[:CELLS, :width].astype(jnp.bfloat16).astype(jnp.float32)
    coarse_out_ref[...] = jnp.maximum(
        nn(compact_ref[...], result) + downsampled, 0.0
    ).astype(jnp.bfloat16)


def coarse_stream(gathered, edges, normed, own, pick, bias, depth, samples, fine_res, to_fine):
    width = own.shape[1]
    fine_cells, fine_ch = fine_res.shape
    operands = (normed, own, bias, pick, depth, samples, fine_res, to_fine, *cell_tables())
    smem, vmem, anywhere = (
        pl.BlockSpec(memory_space=space) for space in (pltpu.SMEM, pltpu.VMEM, pl.ANY)
    )
    return pl.pallas_call(
        coarse_kernel,
        out_shape=(
            jax.ShapeDtypeStruct((fine_cells, fine_ch), jnp.bfloat16),
            jax.ShapeDtypeStruct((CELLS, width), jnp.bfloat16),
        ),
        in_specs=[smem, anywhere] + [vmem] * len(operands),
        out_specs=(vmem, vmem),
        scratch_shapes=[
            pltpu.VMEM((SHARDS, BLOCK_ROWS, width), jnp.bfloat16),
            pltpu.VMEM((SHARDS, BLOCK_ROWS, width), jnp.bfloat16),
            pltpu.VMEM((SHARDS, BLOCK_ROWS, width), jnp.bfloat16),
            pltpu.VMEM((SHARDS, TAP_ROWS, width), jnp.bfloat16),
            pltpu.VMEM((SHARDS, 128, KEYS), jnp.float32),
            pltpu.VMEM((SHARDS, QUERIES, HEAD_ROWS), jnp.float32),
            pltpu.VMEM((SHARDS, QUERIES, KEYS), jnp.bfloat16),
            pltpu.VMEM((SHARDS, QUERIES, HEAD_ROWS), jnp.float32),
            pltpu.VMEM((QUERIES, SHARDS * BLOCK_ROWS), jnp.float32),
            pltpu.VMEM((64, SHARDS * BLOCK_ROWS), jnp.float32),
            pltpu.VMEM((SHARDS * HEAD_ROWS, 128), jnp.float32),
            pltpu.SemaphoreType.DMA((4,)),
        ],
        compiler_params=pltpu.CompilerParams(vmem_limit_bytes=44 * 1024 * 1024),
    )(edges, gathered, *operands)


def neighbours(tile, axis):
    size = lax.axis_size(axis)
    up = [(i, i + 1) for i in range(size - 1)]
    down = [(j, i) for i, j in up]
    return lax.ppermute(tile, axis, up), lax.ppermute(tile, axis, down)


def depthwise(padded, kernel):
    height = padded.shape[1] - 2
    breadth = padded.shape[2] - 2
    running = jnp.zeros((padded.shape[0], height, breadth), jnp.float32)
    for offset in range(9):
        row_step, col_step = divmod(offset, 3)
        sample = padded[:, row_step : row_step + height, col_step : col_step + breadth].astype(
            jnp.float32
        )
        running = running + kernel[offset][:, None, None] * sample
    return running


def local(
    fine_in,
    coarse_in,
    inproj_fine,
    outproj_fine,
    expand_fine,
    depth_fine,
    shrink_fine,
    inproj_coarse,
    outproj_coarse,
    expand_coarse,
    depth_coarse,
    shrink_coarse,
    to_fine,
    to_coarse,
):
    fine_ch = fine_in.shape[2]
    coarse_ch = coarse_in.shape[2]
    fine_cells = fine_in.shape[3]
    coarse_cells = coarse_in.shape[3]
    gathered = lax.all_gather(
        pack(inproj_coarse, outproj_coarse, expand_coarse, shrink_coarse, to_coarse), "rows"
    )
    tile = jnp.pad(coarse_in.reshape(coarse_ch, coarse_cells).T, ((0, TILE - coarse_cells), (0, 0)))
    above, below = neighbours(tile, "rows")
    left, right = neighbours(jnp.concatenate([tile, above, below]), "cols")
    bias, pick = attention_tables()
    normed_all, own = normed_tiles((tile, above, below, left, right), pick)
    fine_rows = fine_cells // (2 * WIN)
    coarse_rows = coarse_cells // WIN
    fine_pic = fine_in.reshape(fine_ch, fine_rows, 2 * WIN)
    normed = normalize(fine_pic).reshape(fine_ch, fine_cells)
    projected = jnp.einsum(
        "tnc,cs->tns", inproj_fine, normed, preferred_element_type=jnp.float32
    ).astype(jnp.bfloat16)
    attended = attend(
        projected[0].reshape(fine_pic.shape),
        projected[1].reshape(fine_pic.shape),
        projected[2].reshape(fine_pic.shape),
        HEADS_FINE,
    ).reshape(fine_ch, fine_cells)
    middle = (
        fine_pic.reshape(fine_ch, fine_cells).astype(jnp.float32)
        + jnp.dot(outproj_fine, attended, preferred_element_type=jnp.float32)
    ).astype(jnp.bfloat16)
    normed_mid = normalize(middle)
    hidden = jax.nn.gelu(
        jnp.dot(expand_fine, normed_mid, preferred_element_type=jnp.float32), approximate=False
    ).astype(jnp.bfloat16)
    padded = padded_2(hidden.reshape(-1, fine_rows, 2 * WIN), (("rows", 1), ("cols", 2)), 1)
    convolved = (
        jax.nn.gelu(depthwise(padded, depth_fine), approximate=False)
        .astype(jnp.bfloat16)
        .reshape(-1, fine_cells)
    )
    fine_res = (
        middle.astype(jnp.float32)
        + jnp.dot(shrink_fine, convolved, preferred_element_type=jnp.float32)
    ).astype(jnp.bfloat16)
    field = fine_res.T
    above_row = passed_along(field[-2 * WIN :], "rows", 1)
    beside = passed_along(
        jnp.concatenate([above_row[-1:], field[2 * WIN - 1 :: 2 * WIN]]), "cols", 1
    )
    depth = jnp.pad(depth_coarse.reshape(9, SHARDS, -1), ((0, 0), (0, 0), (0, 4)))
    row, col = lax.axis_index("rows"), lax.axis_index("cols")
    edges = jnp.stack(
        [row > 0, row < lax.axis_size("rows") - 1, col > 0, col < lax.axis_size("cols") - 1]
    ).astype(jnp.int32)
    samples = tap_samples(
        field, jnp.pad(above_row, ((0, 2), (0, 0))), jnp.pad(beside, ((0, 1), (0, 0)))
    )
    fine_out, coarse_out = coarse_stream(
        gathered,
        edges,
        normed_all,
        own,
        pick,
        bias,
        depth.reshape(9, -1),
        samples,
        field,
        to_fine,
    )
    return (fine_out.T.reshape(fine_in.shape), coarse_out.T.reshape(coarse_in.shape))


def solution(mesh):
    return jax.shard_map(
        local,
        mesh=mesh,
        in_specs=(
            P("rows", "cols", None, None),
            P("rows", "cols", None, None),
            P(),
            P(),
            P(),
            P(),
            P(),
            P(None, "rows", None),
            P(None, "rows"),
            P("rows", None),
            P(),
            P(None, "rows"),
            P(),
            P(None, "rows", None),
        ),
        out_specs=(P("rows", "cols", None, None), P("rows", "cols", None, None)),
        check_vma=False,
    )
```

```python
import math

import jax
import jax.numpy as jnp
from jax import lax
import numpy as np
from jax.experimental import pallas as pl
from jax.experimental.pallas import tpu as pltpu
from jax.sharding import PartitionSpec as P

HEADS_FINE = 8
WIN = 7


EPSILON = 1e-05


CELLS = WIN * WIN
RING = WIN + 2
HEAD_ROWS = 40
BLOCK_ROWS = 4 * HEAD_ROWS
TAP_ROWS = 5 * HEAD_ROWS + 8
SHARDS = 16
TILE = 56
KEYS = 9 * TILE + 8
QUERIES = 96
SIDE = 2 * WIN
FIELD = SIDE + 3
FIELD_ROWS = 304
FIRST_HALF = 352
TOP, BOTTOM, LEFT, RIGHT = 200, 232, 248, 288


def pack(inproj, outproj, expand, shrink, to_coarse):
    width = expand.shape[-1]
    heads = jnp.concatenate([outproj.T[None], inproj[2:], inproj[:2]])
    taps = jnp.pad(to_coarse, ((0, 1), (0, 1), (0, 0))).reshape(5, 2, HEAD_ROWS, -1)
    return jnp.concatenate(
        [
            jnp.pad(heads, ((0, 0), (0, 1), (0, 0))).reshape(BLOCK_ROWS, -1),
            jnp.pad(expand, ((0, 4), (0, 0))),
            jnp.pad(shrink.T, ((0, 4), (0, 0))),
            taps.transpose(0, 2, 1, 3).reshape(-1, width),
            jnp.zeros((8, width), expand.dtype),
        ]
    )


def all_shards(mine):
    size = lax.axis_size("rows")
    swap = [(i, i ^ 1) for i in range(size)]
    up = [(i, (i + 2) % size) for i in range(size)]
    down = [(j, i) for i, j in up]
    rising, falling = [mine], [mine]
    for _ in range(3):
        rising.append(lax.ppermute(rising[-1], "rows", up))
        falling.append(lax.ppermute(falling[-1], "rows", down))
    near = [mine, rising[1], falling[1], rising[2], falling[2]]
    far = [rising[3], falling[3]]
    last = jnp.concatenate(
        [
            lax.ppermute(rising[3][:FIRST_HALF], "rows", up),
            lax.ppermute(falling[3][FIRST_HALF:], "rows", down),
        ]
    )
    sources = near + far + [last]
    for group in (near, far, [last]):
        sources.append(lax.ppermute(jnp.stack(group), "rows", swap))
    place = lax.axis_index("rows")
    chips = [2 * ((place // 2 + away) % (size // 2)) for away in (0, -1, 1, -2, 2, -3, 3, 4)]
    core = place % 2
    owners = [chip + core for chip in chips] + [chip + 1 - core for chip in chips]
    return sources, jnp.stack(owners).astype(jnp.int32)


def attention_tables():
    pick = np.zeros((QUERIES, KEYS), np.float32)
    bias = np.full((QUERIES, KEYS), -1e30, np.float32)
    for row in range(RING):
        for col in range(RING):
            down = 1 if row == 0 else 2 if row == RING - 1 else 0
            side = 1 if col == 0 else 2 if col == RING - 1 else 0
            first = (3 * side + down) * TILE
            query = row * RING + col
            pick[query, first + (row - 1) % WIN * WIN + (col - 1) % WIN] = 1
            bias[query, first : first + CELLS] = 0
    bias[RING * RING :, :CELLS] = 0
    return jnp.asarray(bias), jnp.asarray(pick).astype(jnp.bfloat16)


def window_table():
    cells = np.arange(SIDE * SIDE)
    window = cells // SIDE // WIN * 2 + cells % SIDE // WIN
    return jnp.asarray(np.where(window[:, None] == window[None], 0.0, -1e30).astype(np.float32))


def border_tables():
    right = np.zeros((40, 248), np.float32)
    left = np.zeros((32, 248), np.float32)

    def source(row, col):
        if row < 0:
            return TOP + (row + 2) * SIDE + col
        return row * SIDE + col if row < SIDE else BOTTOM + col

    for row in range(FIELD):
        for col in range(2):
            right[row * 2 + col, source(row - 2, SIDE - 2 + col)] = 1
        left[row, source(row - 2, 0)] = 1
    return jnp.asarray(right).astype(jnp.bfloat16), jnp.asarray(left).astype(jnp.bfloat16)


def field_tables():
    gather = np.zeros((FIELD_ROWS, 320), np.float32)
    inner = np.zeros((256, FIELD_ROWS), np.float32)
    for row in range(FIELD):
        for col in range(FIELD):
            if col < 2:
                source = LEFT + row * 2 + col
            elif col == FIELD - 1:
                source = RIGHT + row
            elif row < 2:
                source = TOP + row * SIDE + col - 2
            elif row == FIELD - 1:
                source = BOTTOM + col - 2
            else:
                source = (row - 2) * SIDE + col - 2
            gather[row * FIELD + col, source] = 1
    for row in range(15):
        for col in range(15):
            inner[row * 16 + col, (row + 1) * FIELD + col + 1] = 1
    tile = np.zeros((SIDE * SIDE, 256), np.float32)
    for row in range(SIDE):
        for col in range(SIDE):
            tile[row * SIDE + col, (row + 1) * 16 + col + 1] = 1
    sample = np.zeros((5 * 64, 512), np.float32)
    for cell in range(CELLS):
        row, col = divmod(cell, WIN)
        for tap in range(9):
            source = (2 * row + tap // 3) * 16 + 2 * col + tap % 3
            sample[tap // 2 * 64 + cell, tap % 2 * 256 + source] = 1
    return tuple(jnp.asarray(t).astype(jnp.bfloat16) for t in (gather, inner, tile, sample))


def cell_tables():
    side = 2 * WIN
    centre = np.zeros((64, QUERIES), np.float32)
    repeat = np.zeros((side * side, 64), np.float32)
    compact = np.zeros((CELLS, 64), np.float32)
    for cell in range(CELLS):
        row, col = divmod(cell, WIN)
        centre[row * 8 + col, (row + 1) * RING + col + 1] = 1
        compact[cell, row * 8 + col] = 1
    for cell in range(side * side):
        row, col = divmod(cell, side)
        repeat[cell, row // 2 * 8 + col // 2] = 1
    return tuple(jnp.asarray(t).astype(jnp.bfloat16) for t in (centre, repeat, compact))


def gelu(values):
    return values * (lax.erf(values * math.sqrt(0.5)) + 1.0) * 0.5


def norm_rows(values):
    center = jnp.mean(values, axis=1, keepdims=True)
    away = values - center
    spread = jnp.mean(away * away, axis=1, keepdims=True)
    return (away * lax.rsqrt(spread + EPSILON)).astype(jnp.bfloat16)


def nn(left, right):
    return lax.dot_general(
        left, right, (((1,), (0,)), ((), ())), preferred_element_type=jnp.float32
    )


def nt(left, right):
    return lax.dot_general(
        left, right, (((1,), (1,)), ((), ())), preferred_element_type=jnp.float32
    )


def fine_attention_kernel(
    fine_ref, inproj_ref, outproj_ref, mask_ref, tile_ref, middle_ref, down_ref, up_ref
):
    cells, channels = fine_ref.shape
    fine = fine_ref[...].astype(jnp.float32)
    normed = norm_rows(fine)
    queries, keys, values = (nt(normed, inproj_ref[i]).astype(jnp.bfloat16) for i in range(3))
    channel = lax.broadcasted_iota(jnp.int32, (cells, channels), 1)
    mask = mask_ref[...]
    nothing = jnp.zeros((cells, channels), jnp.bfloat16)
    attended = jnp.zeros((cells, channels), jnp.float32)
    for head in range(HEADS_FINE):
        mine = (channel >= head * 39) & (channel < (head + 1) * 39)
        chosen = jnp.where(mine, queries, nothing)
        scores = nt(chosen, keys) * (1.0 / math.sqrt(39)) + mask
        exponent = jnp.exp(scores - jnp.max(scores, axis=1, keepdims=True))
        total = jnp.sum(exponent, axis=1, keepdims=True)
        chance = (exponent * (1.0 / total)).astype(jnp.bfloat16)
        attended += nn(chance, jnp.where(mine, values, nothing))
    middle = fine + nt(attended.astype(jnp.bfloat16), outproj_ref[...])
    middle_ref[...] = middle.astype(jnp.bfloat16)
    for target, first, count in ((down_ref, cells - 2 * SIDE, 2 * SIDE), (up_ref, 0, SIDE)):
        target[...] = jnp.zeros(target.shape, jnp.bfloat16)
        target[:TILE, :] = tile_ref[...]
        target[TILE : TILE + count, :channels] = middle_ref[first : first + count, :]


def columns_kernel(
    tile_ref, above_ref, below_ref, middle_ref, right_ref, left_ref, to_right_ref, to_left_ref,
    field_ref,
):
    cells, channels = middle_ref.shape
    field_ref[...] = jnp.zeros(field_ref.shape, jnp.float32)
    field_ref[:cells, :] = middle_ref[...].astype(jnp.float32)
    field_ref[TOP : TOP + 2 * SIDE, :] = above_ref[TILE : TILE + 2 * SIDE, :channels].astype(
        jnp.float32
    )
    field_ref[BOTTOM : BOTTOM + SIDE, :] = below_ref[TILE : TILE + SIDE, :channels].astype(
        jnp.float32
    )
    field = field_ref[...].astype(jnp.bfloat16)
    for target, table in ((to_right_ref, right_ref), (to_left_ref, left_ref)):
        target[...] = jnp.zeros(target.shape, jnp.bfloat16)
        target[:TILE, :] = tile_ref[...]
        target[TILE : 2 * TILE, :] = above_ref[:TILE, :]
        target[2 * TILE : 3 * TILE, :] = below_ref[:TILE, :]
        count = table.shape[0]
        target[3 * TILE : 3 * TILE + count, :channels] = nn(table[...], field).astype(jnp.bfloat16)


def field_kernel(
    edge_ref,
    tile_ref,
    above_ref,
    below_ref,
    left_ref,
    right_ref,
    pick_ref,
    middle_ref,
    expand_ref,
    depth_ref,
    shrink_ref,
    gather_ref,
    inner_ref,
    cell_ref,
    sample_ref,
    normed_ref,
    own_ref,
    fine_ref,
    samples_ref,
    tiles_ref,
    pieces_ref,
    hidden_ref,
    conv_ref,
    twice_ref,
):
    cells, channels = middle_ref.shape
    tiles_ref[9 * TILE :, :] = jnp.zeros((KEYS - 9 * TILE, tiles_ref.shape[1]), jnp.float32)
    first = 0
    for piece, count in (
        (tile_ref, TILE),
        (above_ref, TILE),
        (below_ref, TILE),
        (left_ref, 3 * TILE),
        (right_ref, 3 * TILE),
    ):
        tiles_ref[first : first + count, :] = piece[:count, :].astype(jnp.float32)
        first += count
    tiles = tiles_ref[...]
    normed_ref[...] = norm_rows(tiles)
    own_ref[...] = nn(pick_ref[...], tiles.astype(jnp.bfloat16)).astype(jnp.bfloat16)

    pieces_ref[...] = jnp.zeros(pieces_ref.shape, jnp.float32)
    pieces_ref[:cells, :] = middle_ref[...].astype(jnp.float32)
    for piece, start, first, count in (
        (above_ref, TILE, TOP, 2 * SIDE),
        (below_ref, TILE, BOTTOM, SIDE),
        (left_ref, 3 * TILE, LEFT, 2 * FIELD),
        (right_ref, 3 * TILE, RIGHT, FIELD),
    ):
        pieces_ref[first : first + count, :] = piece[start : start + count, :channels].astype(
            jnp.float32
        )
    field = nn(gather_ref[...], pieces_ref[...].astype(jnp.bfloat16))
    normed_mid = norm_rows(field)
    row = lax.broadcasted_iota(jnp.int32, (FIELD_ROWS, 128), 0)
    column = row % FIELD
    outside = (
        ((row < 2 * FIELD) & (edge_ref[0] == 0))
        | ((row >= FIELD * (FIELD - 1)) & (edge_ref[1] == 0))
        | ((column < 2) & (edge_ref[2] == 0))
        | ((column == FIELD - 1) & (edge_ref[3] == 0))
    )
    inside = jnp.where(outside, 0.0, 1.0)[:, :1]
    hidden_count = hidden_ref.shape[1]
    conv_ref[15 * 16 :, :] = jnp.zeros((16, hidden_count), jnp.bfloat16)
    for first in range(0, hidden_count, 384):
        span = pl.ds(first, min(384, hidden_count - first))
        hidden = gelu(nn(normed_mid, expand_ref[:, span])) * inside
        hidden_ref[:, span] = hidden.astype(jnp.bfloat16).astype(jnp.float32)
        for out in range(15):
            total = jnp.zeros((16, span.size), jnp.float32)
            for tap in range(9):
                down, side = divmod(tap, 3)
                window = hidden_ref[pl.ds((out + down) * FIELD + side, 16), span]
                total += depth_ref[tap : tap + 1, span] * window
            conv_ref[out * 16 : out * 16 + 16, span] = gelu(total).astype(jnp.bfloat16)
    update = nt(conv_ref[...], shrink_ref[...])
    result = nn(inner_ref[...], field.astype(jnp.bfloat16)) + update
    row = lax.broadcasted_iota(jnp.int32, (256, 128), 0)
    outside = ((row < 16) & (edge_ref[0] == 0)) | ((row % 16 == 0) & (edge_ref[2] == 0))
    result = result * jnp.where(outside, 0.0, 1.0)[:, :1]
    rounded = result.astype(jnp.bfloat16)
    fine_ref[...] = nn(cell_ref[...], rounded).astype(jnp.bfloat16)
    result = rounded.astype(jnp.float32)
    twice_ref[...] = jnp.zeros(twice_ref.shape, jnp.float32)
    twice_ref[:256, :channels] = result
    twice_ref[256:, channels:] = result
    samples_ref[...] = nn(sample_ref[...], twice_ref[...].astype(jnp.bfloat16)).astype(jnp.bfloat16)


def call(kernel, shapes, operands, scratch, scalars=0, limit=32):
    smem, vmem = (pl.BlockSpec(memory_space=space) for space in (pltpu.SMEM, pltpu.VMEM))
    return pl.pallas_call(
        kernel,
        out_shape=tuple(jax.ShapeDtypeStruct(shape, jnp.bfloat16) for shape in shapes),
        in_specs=[smem] * scalars + [vmem] * (len(operands) - scalars),
        out_specs=(vmem,) * len(shapes),
        scratch_shapes=[pltpu.VMEM(shape, kind) for shape, kind in scratch],
        compiler_params=pltpu.CompilerParams(vmem_limit_bytes=limit * 1024 * 1024),
    )(*operands)


def coarse_kernel(
    edge_ref,
    owner_ref,
    *refs,
):
    sources, rest = refs[:11], refs[11:]
    coarse_body(edge_ref, owner_ref, sources, *rest)


def coarse_body(
    edge_ref,
    owner_ref,
    sources,
    normed_ref,
    own_ref,
    bias_ref,
    pick_ref,
    depth_ref,
    samples_ref,
    fine_ref,
    to_fine_ref,
    centre_ref,
    repeat_ref,
    compact_ref,
    fine_out_ref,
    coarse_out_ref,
    heads_ref,
    expand_ref,
    shrink_ref,
    taps_ref,
    proj_ref,
    chosen_ref,
    chance_ref,
    attended_ref,
    hidden_ref,
    conv_ref,
    down_ref,
    sems,
):
    spans = (
        (heads_ref, 0, BLOCK_ROWS),
        (expand_ref, BLOCK_ROWS, BLOCK_ROWS),
        (shrink_ref, 2 * BLOCK_ROWS, BLOCK_ROWS),
        (taps_ref, 3 * BLOCK_ROWS, TAP_ROWS),
    )
    slots = list(sources[:8])
    for source, count in zip(sources[8:], (5, 2, 1)):
        slots += [source.at[i] for i in range(count)]
    copies = []
    for part, (target, first, count) in enumerate(spans):
        copies.append(
            [
                pltpu.make_async_copy(
                    slot.at[pl.ds(first, count)], target.at[owner_ref[place]], sems.at[part, place]
                )
                for place, slot in enumerate(slots)
            ]
        )
        for copy in copies[-1]:
            copy.start()

    def arrive(part):
        for copy in copies[part]:
            copy.wait()

    width = own_ref.shape[1]
    query = lax.broadcasted_iota(jnp.int32, (QUERIES, 128), 0)
    column = query % RING
    outside = (
        ((query < RING) & (edge_ref[0] == 0))
        | ((query >= RING * (RING - 1)) & (edge_ref[1] == 0))
        | ((column == 0) & (edge_ref[2] == 0))
        | ((column == RING - 1) & (edge_ref[3] == 0))
    )
    inside = jnp.where(outside, 0.0, 1.0)[:, :1]
    conv_ref[8 * WIN :, :] = jnp.zeros((8, conv_ref.shape[1]), jnp.float32)
    arrive(0)
    heads = heads_ref[:, 32:BLOCK_ROWS, :].reshape(SHARDS * 128, width)
    proj_ref[...] = nt(heads, normed_ref[...]).reshape(SHARDS, 128, KEYS)
    pick = pick_ref[...]
    for head in range(SHARDS):
        queries = proj_ref[head, 48:88].astype(jnp.bfloat16)
        chosen_ref[head] = nt(pick, queries)
    bias = bias_ref[...]
    for head in range(SHARDS):
        keys = proj_ref[head, 88:128].astype(jnp.bfloat16)
        scores = nn(chosen_ref[head].astype(jnp.bfloat16), keys) * (1.0 / math.sqrt(39)) + bias
        exponent = jnp.exp(scores - jnp.max(scores, axis=1, keepdims=True))
        total = jnp.sum(exponent, axis=1, keepdims=True)
        chance_ref[head] = (exponent * (1.0 / total)).astype(jnp.bfloat16)
    for head in range(SHARDS):
        values = proj_ref[head, 8:48].astype(jnp.bfloat16)
        attended_ref[head] = nt(chance_ref[head], values)
    mixed = own_ref[...].astype(jnp.float32)
    for head in range(SHARDS):
        mixed += nn(attended_ref[head].astype(jnp.bfloat16), heads_ref[head][:HEAD_ROWS])
    middle = mixed.astype(jnp.bfloat16)
    normed_mid = norm_rows(middle.astype(jnp.float32))
    arrive(1)
    chunk = 512
    expand = expand_ref[...].reshape(SHARDS * BLOCK_ROWS, width)
    for first in range(0, SHARDS * BLOCK_ROWS, chunk):
        span = pl.ds(first, chunk)
        hidden = gelu(nt(normed_mid, expand[first : first + chunk])) * inside
        hidden_ref[:, span] = hidden.astype(jnp.bfloat16).astype(jnp.float32)
        for row in range(WIN):
            total = jnp.zeros((8, chunk), jnp.float32)
            for tap in range(9):
                down, side = divmod(tap, 3)
                window = hidden_ref[pl.ds((row + down) * RING + side, 8), span]
                total += depth_ref[tap : tap + 1, span] * window
            conv_ref[row * 8 : row * 8 + 8, span] = gelu(total)
    arrive(2)
    shrink = shrink_ref[...].reshape(SHARDS * BLOCK_ROWS, width)
    update = nn(conv_ref[...].astype(jnp.bfloat16), shrink)
    result = (nn(centre_ref[...], middle) + update).astype(jnp.bfloat16)
    spread = nn(repeat_ref[...], result).astype(jnp.bfloat16)
    upsampled = nt(spread, to_fine_ref[...])
    fine_out_ref[...] = jnp.maximum(
        fine_ref[...].astype(jnp.float32) + upsampled, 0.0
    ).astype(jnp.bfloat16)
    arrive(3)
    samples = samples_ref[...]
    for shard in range(SHARDS):
        four = nt(taps_ref[shard], samples[: 4 * 64])
        fifth = nt(taps_ref[shard][4 * HEAD_ROWS :], samples[4 * 64 :])
        total = fifth[:HEAD_ROWS]
        for block in range(4):
            rows = slice(block * HEAD_ROWS, (block + 1) * HEAD_ROWS)
            total += four[rows, block * 64 : (block + 1) * 64]
        down_ref[shard * 39 : shard * 39 + HEAD_ROWS, :64] = total
    downsampled = down_ref[...].T[:CELLS, :width].astype(jnp.bfloat16).astype(jnp.float32)
    coarse_out_ref[...] = jnp.maximum(
        nn(compact_ref[...], result) + downsampled, 0.0
    ).astype(jnp.bfloat16)


def coarse_stream(sources, edges, owners, normed, own, pick, bias, depth, samples, fine_res, to_fine):
    width = own.shape[1]
    fine_cells, fine_ch = fine_res.shape
    operands = (normed, own, bias, pick, depth, samples, fine_res, to_fine, *cell_tables())
    smem, vmem, anywhere = (
        pl.BlockSpec(memory_space=space) for space in (pltpu.SMEM, pltpu.VMEM, pl.ANY)
    )
    return pl.pallas_call(
        coarse_kernel,
        out_shape=(
            jax.ShapeDtypeStruct((fine_cells, fine_ch), jnp.bfloat16),
            jax.ShapeDtypeStruct((CELLS, width), jnp.bfloat16),
        ),
        in_specs=[smem, smem] + [anywhere] * len(sources) + [vmem] * len(operands),
        out_specs=(vmem, vmem),
        scratch_shapes=[
            pltpu.VMEM((SHARDS, BLOCK_ROWS, width), jnp.bfloat16),
            pltpu.VMEM((SHARDS, BLOCK_ROWS, width), jnp.bfloat16),
            pltpu.VMEM((SHARDS, BLOCK_ROWS, width), jnp.bfloat16),
            pltpu.VMEM((SHARDS, TAP_ROWS, width), jnp.bfloat16),
            pltpu.VMEM((SHARDS, 128, KEYS), jnp.float32),
            pltpu.VMEM((SHARDS, QUERIES, HEAD_ROWS), jnp.float32),
            pltpu.VMEM((SHARDS, QUERIES, KEYS), jnp.bfloat16),
            pltpu.VMEM((SHARDS, QUERIES, HEAD_ROWS), jnp.float32),
            pltpu.VMEM((QUERIES, SHARDS * BLOCK_ROWS), jnp.float32),
            pltpu.VMEM((64, SHARDS * BLOCK_ROWS), jnp.float32),
            pltpu.VMEM((SHARDS * HEAD_ROWS, 128), jnp.float32),
            pltpu.SemaphoreType.DMA((4, SHARDS)),
        ],
        compiler_params=pltpu.CompilerParams(vmem_limit_bytes=44 * 1024 * 1024),
    )(edges, owners, *sources, *operands)


def exchange(onward, back, axis):
    up = [(i, i + 1) for i in range(lax.axis_size(axis) - 1)]
    down = [(j, i) for i, j in up]
    return lax.ppermute(onward, axis, up), lax.ppermute(back, axis, down)


def local(
    fine_in,
    coarse_in,
    inproj_fine,
    outproj_fine,
    expand_fine,
    depth_fine,
    shrink_fine,
    inproj_coarse,
    outproj_coarse,
    expand_coarse,
    depth_coarse,
    shrink_coarse,
    to_fine,
    to_coarse,
):
    fine_ch, fine_cells = fine_in.shape[2:]
    coarse_ch, coarse_cells = coarse_in.shape[2:]
    sources, owners = all_shards(
        pack(inproj_coarse, outproj_coarse, expand_coarse, shrink_coarse, to_coarse)
    )
    tile = jnp.pad(coarse_in.reshape(coarse_ch, coarse_cells).T, ((0, TILE - coarse_cells), (0, 0)))
    fine = fine_in.reshape(fine_ch, fine_cells).T
    place = (lax.axis_index("rows"), lax.axis_index("cols"))
    edges = jnp.stack(
        [
            place[0] > 0,
            place[0] < lax.axis_size("rows") - 1,
            place[1] > 0,
            place[1] < lax.axis_size("cols") - 1,
        ]
    ).astype(jnp.int32)
    message = (TILE + 32, coarse_ch)
    middle, going_down, going_up = call(
        fine_attention_kernel,
        (fine.shape, message, message),
        (fine, inproj_fine, outproj_fine, window_table(), tile),
        (),
    )
    above, below = exchange(going_down, going_up, "rows")
    message = (3 * TILE + 40, coarse_ch)
    going_right, going_left = call(
        columns_kernel,
        (message, message),
        (tile, above, below, middle, *border_tables()),
        (((248, fine_ch), jnp.float32),),
    )
    left, right = exchange(going_right, going_left, "cols")
    bias, pick = attention_tables()
    hidden_count = expand_fine.shape[0]
    normed, own, fine_res, samples = call(
        field_kernel,
        ((KEYS, coarse_ch), (QUERIES, coarse_ch), fine.shape, (5 * 64, 2 * fine_ch)),
        (
            edges,
            tile,
            above,
            below,
            left,
            right,
            pick,
            middle,
            expand_fine.T,
            depth_fine,
            shrink_fine,
            *field_tables(),
        ),
        (
            ((KEYS, coarse_ch), jnp.float32),
            ((320, fine_ch), jnp.float32),
            ((FIELD_ROWS, hidden_count), jnp.float32),
            ((256, hidden_count), jnp.bfloat16),
            ((512, 2 * fine_ch), jnp.float32),
        ),
        scalars=1,
    )
    depth = jnp.pad(depth_coarse.reshape(9, SHARDS, -1), ((0, 0), (0, 0), (0, 4)))
    fine_out, coarse_out = coarse_stream(
        sources,
        edges,
        owners,
        normed,
        own,
        pick,
        bias,
        depth.reshape(9, -1),
        samples,
        fine_res,
        to_fine,
    )
    return (fine_out.T.reshape(fine_in.shape), coarse_out.T.reshape(coarse_in.shape))


def solution(mesh):
    return jax.shard_map(
        local,
        mesh=mesh,
        in_specs=(
            P("rows", "cols", None, None),
            P("rows", "cols", None, None),
            P(),
            P(),
            P(),
            P(),
            P(),
            P(None, "rows", None),
            P(None, "rows"),
            P("rows", None),
            P(),
            P(None, "rows"),
            P(),
            P(None, "rows", None),
        ),
        out_specs=(P("rows", "cols", None, None), P("rows", "cols", None, None)),
        check_vma=False,
    )
```

```python
import math

import jax
import jax.numpy as jnp
from jax import lax
import numpy as np
from jax.experimental import pallas as pl
from jax.experimental.pallas import tpu as pltpu
from jax.sharding import PartitionSpec as P

HEADS_FINE = 8
WIN = 7


EPSILON = 1e-05


CELLS = WIN * WIN
RING = WIN + 2
HEAD_ROWS = 40
BLOCK_ROWS = 4 * HEAD_ROWS
OUT_ROWS = 48
TAP_ROWS = 5 * HEAD_ROWS + 8
SHARDS = 16
TILE = 56
STRIP = 64
QUERIES = 96
SIDE = 2 * WIN
FIELD = SIDE + 3
FIELD_ROWS = 304
TOP, BOTTOM, LEFT, RIGHT = 200, 232, 248, 288


def pack(outproj, expand, shrink, to_coarse):
    width = expand.shape[-1]
    taps = jnp.pad(to_coarse, ((0, 1), (0, 1), (0, 0))).reshape(5, 2, HEAD_ROWS, -1)
    return jnp.concatenate(
        [
            jnp.pad(expand, ((0, 4), (0, 0))),
            jnp.pad(shrink.T, ((0, 4), (0, 0))),
            jnp.pad(outproj.T, ((0, 1), (0, 0))),
            taps.transpose(0, 2, 1, 3).reshape(-1, width),
        ]
    )


def strip_tables():
    spread = np.zeros((STRIP, 3 * TILE), np.float32)
    columns = np.zeros((32, STRIP), np.float32)
    for row in range(RING):
        for col in range(WIN):
            spread[row * WIN + col, (row + 6) // WIN * TILE + (row + 6) % WIN * WIN + col] = 1
        columns[row, row * WIN + WIN - 1] = 1
        columns[16 + row, row * WIN] = 1
    return tuple(jnp.asarray(t).astype(jnp.bfloat16) for t in (spread, columns))


def window_table():
    cells = np.arange(SIDE * SIDE)
    window = cells // SIDE // WIN * 2 + cells % SIDE // WIN
    return jnp.asarray(np.where(window[:, None] == window[None], 0.0, -1e30).astype(np.float32))


def border_tables():
    right = np.zeros((40, 248), np.float32)
    left = np.zeros((32, 248), np.float32)

    def source(row, col):
        if row < 0:
            return TOP + (row + 2) * SIDE + col
        return row * SIDE + col if row < SIDE else BOTTOM + col

    for row in range(FIELD):
        for col in range(2):
            right[row * 2 + col, source(row - 2, SIDE - 2 + col)] = 1
        left[row, source(row - 2, 0)] = 1
    return jnp.asarray(right).astype(jnp.bfloat16), jnp.asarray(left).astype(jnp.bfloat16)


def field_tables():
    gather = np.zeros((FIELD_ROWS, 320), np.float32)
    inner = np.zeros((256, FIELD_ROWS), np.float32)
    for row in range(FIELD):
        for col in range(FIELD):
            if col < 2:
                source = LEFT + row * 2 + col
            elif col == FIELD - 1:
                source = RIGHT + row
            elif row < 2:
                source = TOP + row * SIDE + col - 2
            elif row == FIELD - 1:
                source = BOTTOM + col - 2
            else:
                source = (row - 2) * SIDE + col - 2
            gather[row * FIELD + col, source] = 1
    for row in range(15):
        for col in range(15):
            inner[row * 16 + col, (row + 1) * FIELD + col + 1] = 1
    tile = np.zeros((SIDE * SIDE, 256), np.float32)
    for row in range(SIDE):
        for col in range(SIDE):
            tile[row * SIDE + col, (row + 1) * 16 + col + 1] = 1
    sample = np.zeros((5 * 64, 512), np.float32)
    for cell in range(CELLS):
        row, col = divmod(cell, WIN)
        for tap in range(9):
            source = (2 * row + tap // 3) * 16 + 2 * col + tap % 3
            sample[tap // 2 * 64 + cell, tap % 2 * 256 + source] = 1
    return tuple(jnp.asarray(t).astype(jnp.bfloat16) for t in (gather, inner, tile, sample))


def cell_tables():
    side = 2 * WIN
    square = np.zeros((QUERIES, QUERIES), np.float32)
    for row in range(RING):
        for col in range(WIN):
            square[row * RING + col + 1, row * WIN + col] = 1
        square[row * RING, STRIP + row] = 1
        square[row * RING + RING - 1, STRIP + 16 + row] = 1
    centre = np.zeros((64, QUERIES), np.float32)
    repeat = np.zeros((side * side, 64), np.float32)
    compact = np.zeros((CELLS, 64), np.float32)
    for cell in range(CELLS):
        row, col = divmod(cell, WIN)
        centre[row * 8 + col, (row + 1) * RING + col + 1] = 1
        compact[cell, row * 8 + col] = 1
    for cell in range(side * side):
        row, col = divmod(cell, side)
        repeat[cell, row // 2 * 8 + col // 2] = 1
    return tuple(jnp.asarray(t).astype(jnp.bfloat16) for t in (square, centre, repeat, compact))


def gelu(values):
    return values * (lax.erf(values * math.sqrt(0.5)) + 1.0) * 0.5


def norm_rows(values):
    center = jnp.mean(values, axis=1, keepdims=True)
    away = values - center
    spread = jnp.mean(away * away, axis=1, keepdims=True)
    return (away * lax.rsqrt(spread + EPSILON)).astype(jnp.bfloat16)


def nn(left, right):
    return lax.dot_general(
        left, right, (((1,), (0,)), ((), ())), preferred_element_type=jnp.float32
    )


def nt(left, right):
    return lax.dot_general(
        left, right, (((1,), (1,)), ((), ())), preferred_element_type=jnp.float32
    )


def fine_attention_kernel(
    fine_ref, inproj_ref, outproj_ref, mask_ref, middle_ref, down_ref, up_ref
):
    cells, channels = fine_ref.shape
    fine = fine_ref[...].astype(jnp.float32)
    normed = norm_rows(fine)
    queries, keys, values = (nt(normed, inproj_ref[i]).astype(jnp.bfloat16) for i in range(3))
    channel = lax.broadcasted_iota(jnp.int32, (cells, channels), 1)
    mask = mask_ref[...]
    nothing = jnp.zeros((cells, channels), jnp.bfloat16)
    attended = jnp.zeros((cells, channels), jnp.float32)
    for head in range(HEADS_FINE):
        mine = (channel >= head * 39) & (channel < (head + 1) * 39)
        chosen = jnp.where(mine, queries, nothing)
        scores = nt(chosen, keys) * (1.0 / math.sqrt(39)) + mask
        exponent = jnp.exp(scores - jnp.max(scores, axis=1, keepdims=True))
        total = jnp.sum(exponent, axis=1, keepdims=True)
        chance = (exponent * (1.0 / total)).astype(jnp.bfloat16)
        attended += nn(chance, jnp.where(mine, values, nothing))
    middle = fine + nt(attended.astype(jnp.bfloat16), outproj_ref[...])
    middle_ref[...] = middle.astype(jnp.bfloat16)
    for target, first, count in ((down_ref, cells - 2 * SIDE, 2 * SIDE), (up_ref, 0, SIDE)):
        target[...] = jnp.zeros(target.shape, jnp.bfloat16)
        target[:count, :] = middle_ref[first : first + count, :]


def columns_kernel(
    above_ref, below_ref, middle_ref, columns_ref, right_ref, left_ref, to_right_ref, to_left_ref,
    field_ref,
):
    cells, channels = middle_ref.shape
    field_ref[...] = jnp.zeros(field_ref.shape, jnp.float32)
    field_ref[:cells, :] = middle_ref[...].astype(jnp.float32)
    field_ref[TOP : TOP + 2 * SIDE, :] = above_ref[: 2 * SIDE, :].astype(jnp.float32)
    field_ref[BOTTOM : BOTTOM + SIDE, :] = below_ref[:SIDE, :].astype(jnp.float32)
    field = field_ref[...].astype(jnp.bfloat16)
    for index, (target, table) in enumerate(((to_right_ref, right_ref), (to_left_ref, left_ref))):
        target[...] = jnp.zeros(target.shape, jnp.bfloat16)
        count = table.shape[0]
        target[:count, :channels] = nn(table[...], field).astype(jnp.bfloat16)
        target[48:, :] = columns_ref[16 * index : 16 * index + 16, :]


def strip_kernel(
    edge_ref,
    place_ref,
    strip_ref,
    weights_ref,
    spread_ref,
    column_ref,
    blocks_ref,
    own_ref,
    columns_ref,
    normed_ref,
    proj_ref,
    attended_ref,
    images_ref,
):
    tiles, cells, width = strip_ref.shape
    normed_ref[...] = jnp.zeros(normed_ref.shape, jnp.float32)
    attended_ref[...] = jnp.zeros(attended_ref.shape, jnp.float32)
    images_ref[...] = jnp.zeros(images_ref.shape, jnp.float32)
    for tile in range(tiles):
        normed_ref[tile, :cells, :] = norm_rows(strip_ref[tile].astype(jnp.float32)).astype(
            jnp.float32
        )
    normed = normed_ref[...].astype(jnp.bfloat16).reshape(tiles * TILE, width)
    for part in range(3):
        proj_ref[part] = nt(normed, weights_ref[part]).reshape(tiles, TILE, -1)
    key = lax.broadcasted_iota(jnp.int32, (TILE, TILE), 1)
    mask = jnp.where(key < cells, 0.0, -1e30)
    for tile in range(tiles):
        queries, keys, values = (proj_ref[part, tile].astype(jnp.bfloat16) for part in range(3))
        scores = nt(queries, keys) * (1.0 / math.sqrt(39)) + mask
        exponent = jnp.exp(scores - jnp.max(scores, axis=1, keepdims=True))
        total = jnp.sum(exponent, axis=1, keepdims=True)
        chance = (exponent * (1.0 / total)).astype(jnp.bfloat16)
        attended_ref[tile + 1, :, :39] = nn(chance, values)
    spread = spread_ref[...]
    for tile in range(tiles):
        near = attended_ref[tile : tile + 3].astype(jnp.bfloat16).reshape(3 * TILE, HEAD_ROWS)
        blocks_ref[tile] = nn(spread, near).astype(jnp.bfloat16)
    place = place_ref[0]
    before = jnp.maximum(place - 1, 0)
    after = jnp.minimum(place + 1, tiles - 1)
    for index, (tile, there) in enumerate(
        ((before, edge_ref[0]), (place, 1), (after, edge_ref[1]))
    ):
        image = strip_ref[tile].astype(jnp.float32)
        images_ref[index * TILE : index * TILE + cells, :] = jnp.where(there == 1, image, 0.0)
    own = nn(spread, images_ref[...].astype(jnp.bfloat16)).astype(jnp.bfloat16)
    own_ref[...] = own
    columns_ref[...] = nn(column_ref[...], own).astype(jnp.bfloat16)


def edge_columns_kernel(blocks_ref, column_ref, right_ref, left_ref):
    for head in range(SHARDS):
        columns = nn(column_ref[...], blocks_ref[head]).astype(jnp.bfloat16)
        right_ref[head] = columns[:16]
        left_ref[head] = columns[16:]


def field_kernel(
    edge_ref,
    above_ref,
    below_ref,
    left_ref,
    right_ref,
    middle_ref,
    expand_ref,
    depth_ref,
    shrink_ref,
    gather_ref,
    inner_ref,
    cell_ref,
    sample_ref,
    fine_ref,
    samples_ref,
    pieces_ref,
    hidden_ref,
    conv_ref,
    twice_ref,
):
    cells, channels = middle_ref.shape
    pieces_ref[...] = jnp.zeros(pieces_ref.shape, jnp.float32)
    pieces_ref[:cells, :] = middle_ref[...].astype(jnp.float32)
    for piece, start, first, count in (
        (above_ref, 0, TOP, 2 * SIDE),
        (below_ref, 0, BOTTOM, SIDE),
        (left_ref, 0, LEFT, 2 * FIELD),
        (right_ref, 0, RIGHT, FIELD),
    ):
        pieces_ref[first : first + count, :] = piece[start : start + count, :channels].astype(
            jnp.float32
        )
    field = nn(gather_ref[...], pieces_ref[...].astype(jnp.bfloat16))
    normed_mid = norm_rows(field)
    row = lax.broadcasted_iota(jnp.int32, (FIELD_ROWS, 128), 0)
    column = row % FIELD
    outside = (
        ((row < 2 * FIELD) & (edge_ref[0] == 0))
        | ((row >= FIELD * (FIELD - 1)) & (edge_ref[1] == 0))
        | ((column < 2) & (edge_ref[2] == 0))
        | ((column == FIELD - 1) & (edge_ref[3] == 0))
    )
    inside = jnp.where(outside, 0.0, 1.0)[:, :1]
    hidden_count = hidden_ref.shape[1]
    conv_ref[15 * 16 :, :] = jnp.zeros((16, hidden_count), jnp.bfloat16)
    for first in range(0, hidden_count, 384):
        span = pl.ds(first, min(384, hidden_count - first))
        hidden = gelu(nn(normed_mid, expand_ref[:, span])) * inside
        hidden_ref[:, span] = hidden.astype(jnp.bfloat16).astype(jnp.float32)
        for out in range(15):
            total = jnp.zeros((16, span.size), jnp.float32)
            for tap in range(9):
                down, side = divmod(tap, 3)
                window = hidden_ref[pl.ds((out + down) * FIELD + side, 16), span]
                total += depth_ref[tap : tap + 1, span] * window
            conv_ref[out * 16 : out * 16 + 16, span] = gelu(total).astype(jnp.bfloat16)
    update = nt(conv_ref[...], shrink_ref[...])
    result = nn(inner_ref[...], field.astype(jnp.bfloat16)) + update
    row = lax.broadcasted_iota(jnp.int32, (256, 128), 0)
    outside = ((row < 16) & (edge_ref[0] == 0)) | ((row % 16 == 0) & (edge_ref[2] == 0))
    result = result * jnp.where(outside, 0.0, 1.0)[:, :1]
    rounded = result.astype(jnp.bfloat16)
    fine_ref[...] = nn(cell_ref[...], rounded).astype(jnp.bfloat16)
    result = rounded.astype(jnp.float32)
    twice_ref[...] = jnp.zeros(twice_ref.shape, jnp.float32)
    twice_ref[:256, :channels] = result
    twice_ref[256:, channels:] = result
    samples_ref[...] = nn(sample_ref[...], twice_ref[...].astype(jnp.bfloat16)).astype(jnp.bfloat16)


def call(kernel, shapes, operands, scratch, scalars=0, limit=32):
    smem, vmem = (pl.BlockSpec(memory_space=space) for space in (pltpu.SMEM, pltpu.VMEM))
    return pl.pallas_call(
        kernel,
        out_shape=tuple(jax.ShapeDtypeStruct(shape, jnp.bfloat16) for shape in shapes),
        in_specs=[smem] * scalars + [vmem] * (len(operands) - scalars),
        out_specs=(vmem,) * len(shapes),
        scratch_shapes=[pltpu.VMEM(shape, kind) for shape, kind in scratch],
        compiler_params=pltpu.CompilerParams(vmem_limit_bytes=limit * 1024 * 1024),
    )(*operands)


def coarse_kernel(
    edge_ref,
    gathered_ref,
    attended_ref,
    own_ref,
    depth_ref,
    samples_ref,
    fine_ref,
    to_fine_ref,
    square_ref,
    centre_ref,
    repeat_ref,
    compact_ref,
    fine_out_ref,
    coarse_out_ref,
    out_ref,
    expand_ref,
    shrink_ref,
    taps_ref,
    hidden_ref,
    conv_ref,
    down_ref,
    sems,
):
    spans = (
        (out_ref, 2 * BLOCK_ROWS, OUT_ROWS),
        (expand_ref, 0, BLOCK_ROWS),
        (shrink_ref, BLOCK_ROWS, BLOCK_ROWS),
        (taps_ref, 2 * BLOCK_ROWS + 32, TAP_ROWS),
    )
    copies = [
        pltpu.make_async_copy(gathered_ref.at[:, pl.ds(first, count)], target, sems.at[part])
        for part, (target, first, count) in enumerate(spans)
    ]
    for copy in copies:
        copy.start()
    width = own_ref.shape[1]
    query = lax.broadcasted_iota(jnp.int32, (QUERIES, 128), 0)
    column = query % RING
    outside = (
        ((query < RING) & (edge_ref[0] == 0))
        | ((query >= RING * (RING - 1)) & (edge_ref[1] == 0))
        | ((column == 0) & (edge_ref[2] == 0))
        | ((column == RING - 1) & (edge_ref[3] == 0))
    )
    inside = jnp.where(outside, 0.0, 1.0)[:, :1]
    conv_ref[8 * WIN :, :] = jnp.zeros((8, conv_ref.shape[1]), jnp.float32)
    mixed = own_ref[...].astype(jnp.float32)
    copies[0].wait()
    for head in range(SHARDS):
        mixed += nn(attended_ref[head], out_ref[head][:HEAD_ROWS])
    middle = nn(square_ref[...], mixed.astype(jnp.bfloat16)).astype(jnp.bfloat16)
    normed_mid = norm_rows(middle.astype(jnp.float32))
    copies[1].wait()
    chunk = 512
    expand = expand_ref[...].reshape(SHARDS * BLOCK_ROWS, width)
    for first in range(0, SHARDS * BLOCK_ROWS, chunk):
        span = pl.ds(first, chunk)
        hidden = gelu(nt(normed_mid, expand[first : first + chunk])) * inside
        hidden_ref[:, span] = hidden.astype(jnp.bfloat16).astype(jnp.float32)
        for row in range(WIN):
            total = jnp.zeros((8, chunk), jnp.float32)
            for tap in range(9):
                down, side = divmod(tap, 3)
                window = hidden_ref[pl.ds((row + down) * RING + side, 8), span]
                total += depth_ref[tap : tap + 1, span] * window
            conv_ref[row * 8 : row * 8 + 8, span] = gelu(total)
    copies[2].wait()
    shrink = shrink_ref[...].reshape(SHARDS * BLOCK_ROWS, width)
    update = nn(conv_ref[...].astype(jnp.bfloat16), shrink)
    result = (nn(centre_ref[...], middle) + update).astype(jnp.bfloat16)
    spread = nn(repeat_ref[...], result).astype(jnp.bfloat16)
    upsampled = nt(spread, to_fine_ref[...])
    fine_out_ref[...] = jnp.maximum(
        fine_ref[...].astype(jnp.float32) + upsampled, 0.0
    ).astype(jnp.bfloat16)
    copies[3].wait()
    samples = samples_ref[...]
    for shard in range(SHARDS):
        four = nt(taps_ref[shard], samples[: 4 * 64])
        fifth = nt(taps_ref[shard][4 * HEAD_ROWS :], samples[4 * 64 :])
        total = fifth[8:]
        for block in range(4):
            rows = slice(8 + block * HEAD_ROWS, 8 + (block + 1) * HEAD_ROWS)
            total += four[rows, block * 64 : (block + 1) * 64]
        down_ref[shard * 39 : shard * 39 + HEAD_ROWS, :64] = total
    downsampled = down_ref[...].T[:CELLS, :width].astype(jnp.bfloat16).astype(jnp.float32)
    coarse_out_ref[...] = jnp.maximum(
        nn(compact_ref[...], result) + downsampled, 0.0
    ).astype(jnp.bfloat16)


def coarse_stream(gathered, edges, attended, own, depth, samples, fine_res, to_fine):
    width = own.shape[1]
    fine_cells, fine_ch = fine_res.shape
    operands = (attended, own, depth, samples, fine_res, to_fine, *cell_tables())
    smem, vmem, anywhere = (
        pl.BlockSpec(memory_space=space) for space in (pltpu.SMEM, pltpu.VMEM, pl.ANY)
    )
    return pl.pallas_call(
        coarse_kernel,
        out_shape=(
            jax.ShapeDtypeStruct((fine_cells, fine_ch), jnp.bfloat16),
            jax.ShapeDtypeStruct((CELLS, width), jnp.bfloat16),
        ),
        in_specs=[smem, anywhere] + [vmem] * len(operands),
        out_specs=(vmem, vmem),
        scratch_shapes=[
            pltpu.VMEM((SHARDS, OUT_ROWS, width), jnp.bfloat16),
            pltpu.VMEM((SHARDS, BLOCK_ROWS, width), jnp.bfloat16),
            pltpu.VMEM((SHARDS, BLOCK_ROWS, width), jnp.bfloat16),
            pltpu.VMEM((SHARDS, TAP_ROWS, width), jnp.bfloat16),
            pltpu.VMEM((QUERIES, SHARDS * BLOCK_ROWS), jnp.float32),
            pltpu.VMEM((64, SHARDS * BLOCK_ROWS), jnp.float32),
            pltpu.VMEM((SHARDS * HEAD_ROWS, 128), jnp.float32),
            pltpu.SemaphoreType.DMA((4,)),
        ],
        compiler_params=pltpu.CompilerParams(vmem_limit_bytes=32 * 1024 * 1024),
    )(edges, gathered, *operands)


def exchange(onward, back, axis):
    up = [(i, i + 1) for i in range(lax.axis_size(axis) - 1)]
    down = [(j, i) for i, j in up]
    return lax.ppermute(onward, axis, up), lax.ppermute(back, axis, down)


def local(
    fine_in,
    coarse_in,
    inproj_fine,
    outproj_fine,
    expand_fine,
    depth_fine,
    shrink_fine,
    inproj_coarse,
    outproj_coarse,
    expand_coarse,
    depth_coarse,
    shrink_coarse,
    to_fine,
    to_coarse,
):
    fine_ch, fine_cells = fine_in.shape[2:]
    coarse_ch, coarse_cells = coarse_in.shape[2:]
    gathered = lax.all_gather(pack(outproj_coarse, expand_coarse, shrink_coarse, to_coarse), "rows")
    strip = lax.all_gather(coarse_in.reshape(coarse_ch, coarse_cells).T, "rows")
    fine = fine_in.reshape(fine_ch, fine_cells).T
    place = (lax.axis_index("rows"), lax.axis_index("cols"))
    edges = jnp.stack(
        [
            place[0] > 0,
            place[0] < lax.axis_size("rows") - 1,
            place[1] > 0,
            place[1] < lax.axis_size("cols") - 1,
        ]
    ).astype(jnp.int32)
    middle, going_down, going_up = call(
        fine_attention_kernel,
        (fine.shape, (32, fine_ch), (16, fine_ch)),
        (fine, inproj_fine, outproj_fine, window_table()),
        (),
    )
    above, below = exchange(going_down, going_up, "rows")
    spread, column = strip_tables()
    blocks, own, columns = call(
        strip_kernel,
        ((SHARDS, STRIP, HEAD_ROWS), (STRIP, coarse_ch), (32, coarse_ch)),
        (edges, place[0].reshape(1).astype(jnp.int32), strip, inproj_coarse, spread, column),
        (
            ((SHARDS, TILE, coarse_ch), jnp.float32),
            ((3, SHARDS, TILE, 39), jnp.float32),
            ((SHARDS + 2, TILE, HEAD_ROWS), jnp.float32),
            ((3 * TILE, coarse_ch), jnp.float32),
        ),
        scalars=2,
    )
    blocks = lax.all_to_all(blocks, "rows", 0, 0, tiled=True)
    going_right, going_left = call(
        columns_kernel,
        ((64, coarse_ch), (64, coarse_ch)),
        (above, below, middle, columns, *border_tables()),
        (((248, fine_ch), jnp.float32),),
    )
    left, right = exchange(going_right, going_left, "cols")
    edge = (SHARDS, 16, HEAD_ROWS)
    near = exchange(*call(edge_columns_kernel, (edge, edge), (blocks, column), ()), "cols")
    hidden_count = expand_fine.shape[0]
    fine_res, samples = call(
        field_kernel,
        (fine.shape, (5 * 64, 2 * fine_ch)),
        (
            edges,
            above,
            below,
            left,
            right,
            middle,
            expand_fine.T,
            depth_fine,
            shrink_fine,
            *field_tables(),
        ),
        (
            ((320, fine_ch), jnp.float32),
            ((FIELD_ROWS, hidden_count), jnp.float32),
            ((256, hidden_count), jnp.bfloat16),
            ((512, 2 * fine_ch), jnp.float32),
        ),
        scalars=1,
    )
    depth = jnp.pad(depth_coarse.reshape(9, SHARDS, -1), ((0, 0), (0, 0), (0, 4)))
    fine_out, coarse_out = coarse_stream(
        gathered,
        edges,
        jnp.concatenate([blocks, *near], axis=1),
        jnp.concatenate([own, left[48:], right[48:]]),
        depth.reshape(9, -1),
        samples,
        fine_res,
        to_fine,
    )
    return (fine_out.T.reshape(fine_in.shape), coarse_out.T.reshape(coarse_in.shape))


def solution(mesh):
    return jax.shard_map(
        local,
        mesh=mesh,
        in_specs=(
            P("rows", "cols", None, None),
            P("rows", "cols", None, None),
            P(),
            P(),
            P(),
            P(),
            P(),
            P(None, "rows", None),
            P(None, "rows"),
            P("rows", None),
            P(),
            P(None, "rows"),
            P(),
            P(None, "rows", None),
        ),
        out_specs=(P("rows", "cols", None, None), P("rows", "cols", None, None)),
        check_vma=False,
    )
```

```python
import math

import jax
import jax.numpy as jnp
from jax import lax
import numpy as np
from jax.experimental import pallas as pl
from jax.experimental.pallas import tpu as pltpu
from jax.sharding import PartitionSpec as P

HEADS_FINE = 8
WIN = 7


EPSILON = 1e-05


CELLS = WIN * WIN
RING = WIN + 2
HEAD_ROWS = 40
BLOCK_ROWS = 4 * HEAD_ROWS
OUT_ROWS = 48
TAP_ROWS = 192
HALF = HEAD_ROWS // 2
SHARDS = 16
TILE = 56
STRIP = 64
QUERIES = 96
SIDE = 2 * WIN
FIELD = SIDE + 3
FIELD_ROWS = 304
TOP, BOTTOM, LEFT, RIGHT = 200, 232, 248, 288


def pack(outproj, expand, shrink, to_coarse):
    width = expand.shape[-1]
    taps = jnp.pad(to_coarse, ((0, 0), (0, 1), (0, 0)))
    pairs = taps[:8].reshape(4, 2, HEAD_ROWS, -1).transpose(0, 2, 1, 3).reshape(-1, width)
    return jnp.concatenate(
        [
            jnp.pad(expand, ((0, 4), (0, 0))),
            jnp.pad(shrink.T, ((0, 4), (0, 0))),
            jnp.pad(outproj.T, ((0, 1), (0, 0))),
            pairs,
            jnp.concatenate([taps[8, :HALF], taps[8, HALF:]], axis=1),
            jnp.zeros((4, width), expand.dtype),
        ]
    )


def strip_tables():
    spread = np.zeros((STRIP, 3 * TILE), np.float32)
    columns = np.zeros((32, STRIP), np.float32)
    for row in range(RING):
        for col in range(WIN):
            spread[row * WIN + col, (row + 6) // WIN * TILE + (row + 6) % WIN * WIN + col] = 1
        columns[row, row * WIN + WIN - 1] = 1
        columns[16 + row, row * WIN] = 1
    return tuple(jnp.asarray(t).astype(jnp.bfloat16) for t in (spread, columns))


def window_table():
    cells = np.arange(SIDE * SIDE)
    window = cells // SIDE // WIN * 2 + cells % SIDE // WIN
    return jnp.asarray(np.where(window[:, None] == window[None], 0.0, -1e30).astype(np.float32))


def border_tables():
    right = np.zeros((40, 248), np.float32)
    left = np.zeros((32, 248), np.float32)

    def source(row, col):
        if row < 0:
            return TOP + (row + 2) * SIDE + col
        return row * SIDE + col if row < SIDE else BOTTOM + col

    for row in range(FIELD):
        for col in range(2):
            right[row * 2 + col, source(row - 2, SIDE - 2 + col)] = 1
        left[row, source(row - 2, 0)] = 1
    return jnp.asarray(right).astype(jnp.bfloat16), jnp.asarray(left).astype(jnp.bfloat16)


def field_tables():
    gather = np.zeros((FIELD_ROWS, 320), np.float32)
    inner = np.zeros((256, FIELD_ROWS), np.float32)
    for row in range(FIELD):
        for col in range(FIELD):
            if col < 2:
                source = LEFT + row * 2 + col
            elif col == FIELD - 1:
                source = RIGHT + row
            elif row < 2:
                source = TOP + row * SIDE + col - 2
            elif row == FIELD - 1:
                source = BOTTOM + col - 2
            else:
                source = (row - 2) * SIDE + col - 2
            gather[row * FIELD + col, source] = 1
    for row in range(15):
        for col in range(15):
            inner[row * 16 + col, (row + 1) * FIELD + col + 1] = 1
    tile = np.zeros((SIDE * SIDE, 256), np.float32)
    for row in range(SIDE):
        for col in range(SIDE):
            tile[row * SIDE + col, (row + 1) * 16 + col + 1] = 1
    sample = np.zeros((6 * 64, 512), np.float32)
    for cell in range(CELLS):
        row, col = divmod(cell, WIN)
        for tap in range(9):
            source = (2 * row + tap // 3) * 16 + 2 * col + tap % 3
            sample[tap // 2 * 64 + cell, tap % 2 * 256 + source] = 1
        sample[5 * 64 + cell, 256 + source] = 1
    return tuple(jnp.asarray(t).astype(jnp.bfloat16) for t in (gather, inner, tile, sample))


def cell_tables():
    side = 2 * WIN
    square = np.zeros((QUERIES, QUERIES), np.float32)
    for row in range(RING):
        for col in range(WIN):
            square[row * RING + col + 1, row * WIN + col] = 1
        square[row * RING, STRIP + row] = 1
        square[row * RING + RING - 1, STRIP + 16 + row] = 1
    centre = np.zeros((64, QUERIES), np.float32)
    repeat = np.zeros((side * side, 64), np.float32)
    compact = np.zeros((CELLS, 64), np.float32)
    for cell in range(CELLS):
        row, col = divmod(cell, WIN)
        centre[row * 8 + col, (row + 1) * RING + col + 1] = 1
        compact[cell, row * 8 + col] = 1
    for cell in range(side * side):
        row, col = divmod(cell, side)
        repeat[cell, row // 2 * 8 + col // 2] = 1
    return tuple(jnp.asarray(t).astype(jnp.bfloat16) for t in (square, centre, repeat, compact))


def gelu(values):
    return values * (lax.erf(values * math.sqrt(0.5)) + 1.0) * 0.5


def norm_rows(values):
    center = jnp.mean(values, axis=1, keepdims=True)
    away = values - center
    spread = jnp.mean(away * away, axis=1, keepdims=True)
    return (away * lax.rsqrt(spread + EPSILON)).astype(jnp.bfloat16)


def nn(left, right):
    return lax.dot_general(
        left, right, (((1,), (0,)), ((), ())), preferred_element_type=jnp.float32
    )


def nt(left, right):
    return lax.dot_general(
        left, right, (((1,), (1,)), ((), ())), preferred_element_type=jnp.float32
    )


def fine_attention_kernel(
    fine_ref, inproj_ref, outproj_ref, mask_ref, middle_ref, down_ref, up_ref
):
    cells, channels = fine_ref.shape
    fine = fine_ref[...].astype(jnp.float32)
    normed = norm_rows(fine)
    queries, keys, values = (nt(normed, inproj_ref[i]).astype(jnp.bfloat16) for i in range(3))
    channel = lax.broadcasted_iota(jnp.int32, (cells, channels), 1)
    mask = mask_ref[...]
    nothing = jnp.zeros((cells, channels), jnp.bfloat16)
    attended = jnp.zeros((cells, channels), jnp.float32)
    for head in range(HEADS_FINE):
        mine = (channel >= head * 39) & (channel < (head + 1) * 39)
        chosen = jnp.where(mine, queries, nothing)
        scores = nt(chosen, keys) * (1.0 / math.sqrt(39)) + mask
        exponent = jnp.exp(scores - jnp.max(scores, axis=1, keepdims=True))
        total = jnp.sum(exponent, axis=1, keepdims=True)
        chance = (exponent * (1.0 / total)).astype(jnp.bfloat16)
        attended += nn(chance, jnp.where(mine, values, nothing))
    middle = fine + nt(attended.astype(jnp.bfloat16), outproj_ref[...])
    middle_ref[...] = middle.astype(jnp.bfloat16)
    for target, first, count in ((down_ref, cells - 2 * SIDE, 2 * SIDE), (up_ref, 0, SIDE)):
        target[...] = jnp.zeros(target.shape, jnp.bfloat16)
        target[:count, :] = middle_ref[first : first + count, :]


def columns_kernel(
    above_ref, below_ref, middle_ref, columns_ref, right_ref, left_ref, to_right_ref, to_left_ref,
    field_ref,
):
    cells, channels = middle_ref.shape
    field_ref[...] = jnp.zeros(field_ref.shape, jnp.float32)
    field_ref[:cells, :] = middle_ref[...].astype(jnp.float32)
    field_ref[TOP : TOP + 2 * SIDE, :] = above_ref[: 2 * SIDE, :].astype(jnp.float32)
    field_ref[BOTTOM : BOTTOM + SIDE, :] = below_ref[:SIDE, :].astype(jnp.float32)
    field = field_ref[...].astype(jnp.bfloat16)
    for index, (target, table) in enumerate(((to_right_ref, right_ref), (to_left_ref, left_ref))):
        target[...] = jnp.zeros(target.shape, jnp.bfloat16)
        count = table.shape[0]
        target[:count, :channels] = nn(table[...], field).astype(jnp.bfloat16)
        target[48:, :] = columns_ref[16 * index : 16 * index + 16, :]


def strip_kernel(
    edge_ref,
    place_ref,
    strip_ref,
    weights_ref,
    spread_ref,
    column_ref,
    blocks_ref,
    own_ref,
    columns_ref,
    normed_ref,
    proj_ref,
    scores_ref,
    attended_ref,
    images_ref,
):
    tiles, cells, width = strip_ref.shape
    normed_ref[...] = jnp.zeros(normed_ref.shape, jnp.float32)
    attended_ref[...] = jnp.zeros(attended_ref.shape, jnp.float32)
    images_ref[...] = jnp.zeros(images_ref.shape, jnp.float32)
    for tile in range(tiles):
        normed_ref[tile, :cells, :] = norm_rows(strip_ref[tile].astype(jnp.float32)).astype(
            jnp.float32
        )
    normed = normed_ref[...].astype(jnp.bfloat16).reshape(tiles * TILE, width)
    for part in range(3):
        proj_ref[part] = nt(normed, weights_ref[part]).reshape(tiles, TILE, -1)
    for tile in range(tiles):
        queries, keys = (proj_ref[part, tile].astype(jnp.bfloat16) for part in range(2))
        scores_ref[tile] = nt(queries, keys)
    key = lax.broadcasted_iota(jnp.int32, (tiles * TILE, TILE), 1)
    scores = scores_ref[...].reshape(tiles * TILE, TILE) * (1.0 / math.sqrt(39))
    scores += jnp.where(key < cells, 0.0, -1e30)
    exponent = jnp.exp(scores - jnp.max(scores, axis=1, keepdims=True))
    total = jnp.sum(exponent, axis=1, keepdims=True)
    scores_ref[...] = (exponent * (1.0 / total)).reshape(tiles, TILE, TILE)
    for tile in range(tiles):
        values = proj_ref[2, tile].astype(jnp.bfloat16)
        attended_ref[tile + 1, :, :39] = nn(scores_ref[tile].astype(jnp.bfloat16), values)
    spread = spread_ref[...]
    for tile in range(tiles):
        near = attended_ref[tile : tile + 3].astype(jnp.bfloat16).reshape(3 * TILE, HEAD_ROWS)
        blocks_ref[tile] = nn(spread, near).astype(jnp.bfloat16)
    place = place_ref[0]
    before = jnp.maximum(place - 1, 0)
    after = jnp.minimum(place + 1, tiles - 1)
    for index, (tile, there) in enumerate(
        ((before, edge_ref[0]), (place, 1), (after, edge_ref[1]))
    ):
        image = strip_ref[tile].astype(jnp.float32)
        images_ref[index * TILE : index * TILE + cells, :] = jnp.where(there == 1, image, 0.0)
    own = nn(spread, images_ref[...].astype(jnp.bfloat16)).astype(jnp.bfloat16)
    own_ref[...] = own
    columns_ref[...] = nn(column_ref[...], own).astype(jnp.bfloat16)


def edge_columns_kernel(blocks_ref, column_ref, right_ref, left_ref):
    for head in range(SHARDS):
        columns = nn(column_ref[...], blocks_ref[head]).astype(jnp.bfloat16)
        right_ref[head] = columns[:16]
        left_ref[head] = columns[16:]


def attended_kernel(blocks_ref, left_ref, right_ref, flat_ref, parts_ref):
    parts_ref[:, :STRIP, :] = blocks_ref[...]
    parts_ref[:, STRIP : STRIP + 16, :] = left_ref[...]
    parts_ref[:, STRIP + 16 :, :] = right_ref[...]
    channel = lax.broadcasted_iota(jnp.int32, (HEAD_ROWS, SHARDS * OUT_ROWS), 0)
    lane = lax.broadcasted_iota(jnp.int32, (HEAD_ROWS, SHARDS * OUT_ROWS), 1)
    flat = jnp.zeros(flat_ref.shape, jnp.float32)
    for head in range(SHARDS):
        move = jnp.where(lane == channel + head * OUT_ROWS, 1.0, 0.0).astype(jnp.bfloat16)
        flat += nn(parts_ref[head], move)
    flat_ref[...] = flat.astype(jnp.bfloat16)


def field_kernel(
    edge_ref,
    above_ref,
    below_ref,
    left_ref,
    right_ref,
    middle_ref,
    expand_ref,
    depth_ref,
    shrink_ref,
    gather_ref,
    inner_ref,
    cell_ref,
    sample_ref,
    fine_ref,
    samples_ref,
    pieces_ref,
    hidden_ref,
    conv_ref,
    twice_ref,
):
    cells, channels = middle_ref.shape
    pieces_ref[...] = jnp.zeros(pieces_ref.shape, jnp.float32)
    pieces_ref[:cells, :] = middle_ref[...].astype(jnp.float32)
    for piece, start, first, count in (
        (above_ref, 0, TOP, 2 * SIDE),
        (below_ref, 0, BOTTOM, SIDE),
        (left_ref, 0, LEFT, 2 * FIELD),
        (right_ref, 0, RIGHT, FIELD),
    ):
        pieces_ref[first : first + count, :] = piece[start : start + count, :channels].astype(
            jnp.float32
        )
    field = nn(gather_ref[...], pieces_ref[...].astype(jnp.bfloat16))
    normed_mid = norm_rows(field)
    row = lax.broadcasted_iota(jnp.int32, (FIELD_ROWS, 128), 0)
    column = row % FIELD
    outside = (
        ((row < 2 * FIELD) & (edge_ref[0] == 0))
        | ((row >= FIELD * (FIELD - 1)) & (edge_ref[1] == 0))
        | ((column < 2) & (edge_ref[2] == 0))
        | ((column == FIELD - 1) & (edge_ref[3] == 0))
    )
    inside = jnp.where(outside, 0.0, 1.0)[:, :1]
    hidden_count = hidden_ref.shape[1]
    conv_ref[15 * 16 :, :] = jnp.zeros((16, hidden_count), jnp.bfloat16)
    for first in range(0, hidden_count, 384):
        span = pl.ds(first, min(384, hidden_count - first))
        hidden = gelu(nn(normed_mid, expand_ref[:, span])) * inside
        hidden_ref[:, span] = hidden.astype(jnp.bfloat16).astype(jnp.float32)
        for out in range(15):
            total = jnp.zeros((16, span.size), jnp.float32)
            for tap in range(9):
                down, side = divmod(tap, 3)
                window = hidden_ref[pl.ds((out + down) * FIELD + side, 16), span]
                total += depth_ref[tap : tap + 1, span] * window
            conv_ref[out * 16 : out * 16 + 16, span] = gelu(total).astype(jnp.bfloat16)
    update = nt(conv_ref[...], shrink_ref[...])
    result = nn(inner_ref[...], field.astype(jnp.bfloat16)) + update
    row = lax.broadcasted_iota(jnp.int32, (256, 128), 0)
    outside = ((row < 16) & (edge_ref[0] == 0)) | ((row % 16 == 0) & (edge_ref[2] == 0))
    result = result * jnp.where(outside, 0.0, 1.0)[:, :1]
    rounded = result.astype(jnp.bfloat16)
    fine_ref[...] = nn(cell_ref[...], rounded).astype(jnp.bfloat16)
    result = rounded.astype(jnp.float32)
    twice_ref[...] = jnp.zeros(twice_ref.shape, jnp.float32)
    twice_ref[:256, :channels] = result
    twice_ref[256:, channels:] = result
    samples_ref[...] = nn(sample_ref[...], twice_ref[...].astype(jnp.bfloat16)).astype(jnp.bfloat16)


def call(kernel, shapes, operands, scratch, scalars=0, staged=False, limit=32):
    smem, vmem, anywhere = (
        pl.BlockSpec(memory_space=space) for space in (pltpu.SMEM, pltpu.VMEM, pl.ANY)
    )
    arrays = operands[scalars:]
    count = len(arrays)
    scratch_shapes = [pltpu.VMEM(shape, kind) for shape, kind in scratch]
    if staged:
        scratch_shapes += [pltpu.VMEM(array.shape, array.dtype) for array in arrays]
        scratch_shapes.append(pltpu.SemaphoreType.DMA((count,)))

    def fetching(*refs):
        given, rest, landed, sems = (
            refs[: scalars + count],
            refs[scalars + count : -1 - count],
            refs[-1 - count : -1],
            refs[-1],
        )
        copies = [
            pltpu.make_async_copy(source, target, sems.at[index])
            for index, (source, target) in enumerate(zip(given[scalars:], landed))
        ]
        for copy in copies:
            copy.start()
        for copy in copies:
            copy.wait()
        kernel(*given[:scalars], *landed, *rest)

    return pl.pallas_call(
        fetching if staged else kernel,
        out_shape=tuple(jax.ShapeDtypeStruct(shape, jnp.bfloat16) for shape in shapes),
        in_specs=[smem] * scalars + [anywhere if staged else vmem] * count,
        out_specs=(vmem,) * len(shapes),
        scratch_shapes=scratch_shapes,
        compiler_params=pltpu.CompilerParams(vmem_limit_bytes=limit * 1024 * 1024),
    )(*operands)


def coarse_kernel(edge_ref, gathered_ref, *refs):
    count = 10
    operands, outputs, landed = refs[:count], refs[count : count + 2], refs[-count - 1 : -1]
    small = [
        pltpu.make_async_copy(source, target, refs[-1].at[index])
        for index, (source, target) in enumerate(zip(operands, landed))
    ]
    for copy in small:
        copy.start()
    coarse_body(edge_ref, gathered_ref, small, *landed, *outputs, *refs[count + 2 : -count - 1])


def coarse_body(
    edge_ref,
    gathered_ref,
    small,
    attended_ref,
    own_ref,
    depth_ref,
    samples_ref,
    fine_ref,
    to_fine_ref,
    square_ref,
    centre_ref,
    repeat_ref,
    compact_ref,
    fine_out_ref,
    coarse_out_ref,
    out_ref,
    expand_ref,
    shrink_ref,
    taps_ref,
    hidden_ref,
    conv_ref,
    down_ref,
    sems,
):
    spans = (
        (out_ref, 2 * BLOCK_ROWS, OUT_ROWS),
        (expand_ref, 0, BLOCK_ROWS),
        (shrink_ref, BLOCK_ROWS, BLOCK_ROWS),
        (taps_ref, 2 * BLOCK_ROWS + 32, TAP_ROWS),
    )
    copies = [
        pltpu.make_async_copy(gathered_ref.at[:, pl.ds(first, count)], target, sems.at[part])
        for part, (target, first, count) in enumerate(spans)
    ]
    for copy in copies:
        copy.start()
    for copy in small:
        copy.wait()
    width = own_ref.shape[1]
    query = lax.broadcasted_iota(jnp.int32, (QUERIES, 128), 0)
    column = query % RING
    outside = (
        ((query < RING) & (edge_ref[0] == 0))
        | ((query >= RING * (RING - 1)) & (edge_ref[1] == 0))
        | ((column == 0) & (edge_ref[2] == 0))
        | ((column == RING - 1) & (edge_ref[3] == 0))
    )
    inside = jnp.where(outside, 0.0, 1.0)[:, :1]
    conv_ref[8 * WIN :, :] = jnp.zeros((8, conv_ref.shape[1]), jnp.float32)
    mixed = own_ref[...].astype(jnp.float32)
    copies[0].wait()
    mixed += nn(attended_ref[...], out_ref[...].reshape(SHARDS * OUT_ROWS, width))
    middle = nn(square_ref[...], mixed.astype(jnp.bfloat16)).astype(jnp.bfloat16)
    normed_mid = norm_rows(middle.astype(jnp.float32))
    copies[1].wait()
    chunk = 512
    expand = expand_ref[...].reshape(SHARDS * BLOCK_ROWS, width)
    for first in range(0, SHARDS * BLOCK_ROWS, chunk):
        span = pl.ds(first, chunk)
        hidden = gelu(nt(normed_mid, expand[first : first + chunk])) * inside
        hidden_ref[:, span] = hidden.astype(jnp.bfloat16).astype(jnp.float32)
        for row in range(WIN):
            total = jnp.zeros((8, chunk), jnp.float32)
            for tap in range(9):
                down, side = divmod(tap, 3)
                window = hidden_ref[pl.ds((row + down) * RING + side, 8), span]
                total += depth_ref[tap : tap + 1, span] * window
            conv_ref[row * 8 : row * 8 + 8, span] = gelu(total)
    copies[2].wait()
    shrink = shrink_ref[...].reshape(SHARDS * BLOCK_ROWS, width)
    update = nn(conv_ref[...].astype(jnp.bfloat16), shrink)
    result = (nn(centre_ref[...], middle) + update).astype(jnp.bfloat16)
    spread = nn(repeat_ref[...], result).astype(jnp.bfloat16)
    upsampled = nt(spread, to_fine_ref[...])
    fine_out_ref[...] = jnp.maximum(
        fine_ref[...].astype(jnp.float32) + upsampled, 0.0
    ).astype(jnp.bfloat16)
    copies[3].wait()
    samples = samples_ref[...]
    for shard in range(SHARDS):
        four = nt(taps_ref[shard], samples[: 4 * 64])
        ninth = nt(taps_ref[shard][4 * HEAD_ROWS :], samples[4 * 64 :])
        total = four[8 : 8 + HEAD_ROWS, :64]
        for block in range(1, 4):
            rows = slice(8 + block * HEAD_ROWS, 8 + (block + 1) * HEAD_ROWS)
            total += four[rows, block * 64 : (block + 1) * 64]
        first = shard * 39
        down_ref[first : first + HEAD_ROWS, :64] = total
        down_ref[first : first + HALF, :64] += ninth[8 : 8 + HALF, :64]
        down_ref[first + HALF : first + HEAD_ROWS, :64] += ninth[8 : 8 + HALF, 64:]
    downsampled = down_ref[...].T[:CELLS, :width].astype(jnp.bfloat16).astype(jnp.float32)
    coarse_out_ref[...] = jnp.maximum(
        nn(compact_ref[...], result) + downsampled, 0.0
    ).astype(jnp.bfloat16)


def coarse_stream(gathered, edges, attended, own, depth, samples, fine_res, to_fine):
    width = own.shape[1]
    fine_cells, fine_ch = fine_res.shape
    operands = (attended, own, depth, samples, fine_res, to_fine, *cell_tables())
    smem, vmem, anywhere = (
        pl.BlockSpec(memory_space=space) for space in (pltpu.SMEM, pltpu.VMEM, pl.ANY)
    )
    return pl.pallas_call(
        coarse_kernel,
        out_shape=(
            jax.ShapeDtypeStruct((fine_cells, fine_ch), jnp.bfloat16),
            jax.ShapeDtypeStruct((CELLS, width), jnp.bfloat16),
        ),
        in_specs=[smem, anywhere] + [anywhere] * len(operands),
        out_specs=(vmem, vmem),
        scratch_shapes=[
            pltpu.VMEM((SHARDS, OUT_ROWS, width), jnp.bfloat16),
            pltpu.VMEM((SHARDS, BLOCK_ROWS, width), jnp.bfloat16),
            pltpu.VMEM((SHARDS, BLOCK_ROWS, width), jnp.bfloat16),
            pltpu.VMEM((SHARDS, TAP_ROWS, width), jnp.bfloat16),
            pltpu.VMEM((QUERIES, SHARDS * BLOCK_ROWS), jnp.float32),
            pltpu.VMEM((64, SHARDS * BLOCK_ROWS), jnp.float32),
            pltpu.VMEM((SHARDS * HEAD_ROWS, 128), jnp.float32),
            pltpu.SemaphoreType.DMA((4,)),
            *(pltpu.VMEM(operand.shape, operand.dtype) for operand in operands),
            pltpu.SemaphoreType.DMA((len(operands),)),
        ],
        compiler_params=pltpu.CompilerParams(vmem_limit_bytes=40 * 1024 * 1024),
    )(edges, gathered, *operands)


def exchange(onward, back, axis):
    up = [(i, i + 1) for i in range(lax.axis_size(axis) - 1)]
    down = [(j, i) for i, j in up]
    return lax.ppermute(onward, axis, up), lax.ppermute(back, axis, down)


def local(
    fine_in,
    coarse_in,
    inproj_fine,
    outproj_fine,
    expand_fine,
    depth_fine,
    shrink_fine,
    inproj_coarse,
    outproj_coarse,
    expand_coarse,
    depth_coarse,
    shrink_coarse,
    to_fine,
    to_coarse,
):
    fine_ch, fine_cells = fine_in.shape[2:]
    coarse_ch, coarse_cells = coarse_in.shape[2:]
    gathered = lax.all_gather(pack(outproj_coarse, expand_coarse, shrink_coarse, to_coarse), "rows")
    strip = lax.all_gather(coarse_in.reshape(coarse_ch, coarse_cells).T, "rows")
    fine = fine_in.reshape(fine_ch, fine_cells).T
    place = (lax.axis_index("rows"), lax.axis_index("cols"))
    edges = jnp.stack(
        [
            place[0] > 0,
            place[0] < lax.axis_size("rows") - 1,
            place[1] > 0,
            place[1] < lax.axis_size("cols") - 1,
        ]
    ).astype(jnp.int32)
    middle, going_down, going_up = call(
        fine_attention_kernel,
        (fine.shape, (32, fine_ch), (16, fine_ch)),
        (fine, inproj_fine, outproj_fine, window_table()),
        (),
    )
    above, below = exchange(going_down, going_up, "rows")
    spread, column = strip_tables()
    blocks, own, columns = call(
        strip_kernel,
        ((SHARDS, STRIP, HEAD_ROWS), (STRIP, coarse_ch), (32, coarse_ch)),
        (edges, place[0].reshape(1).astype(jnp.int32), strip, inproj_coarse, spread, column),
        (
            ((SHARDS, TILE, coarse_ch), jnp.float32),
            ((3, SHARDS, TILE, 39), jnp.float32),
            ((SHARDS, TILE, TILE), jnp.float32),
            ((SHARDS + 2, TILE, HEAD_ROWS), jnp.float32),
            ((3 * TILE, coarse_ch), jnp.float32),
        ),
        scalars=2,
    )
    blocks = lax.all_to_all(blocks, "rows", 0, 0, tiled=True)
    going_right, going_left = call(
        columns_kernel,
        ((64, coarse_ch), (64, coarse_ch)),
        (above, below, middle, columns, *border_tables()),
        (((248, fine_ch), jnp.float32),),
    )
    left, right = exchange(going_right, going_left, "cols")
    edge = (SHARDS, 16, HEAD_ROWS)
    near = exchange(*call(edge_columns_kernel, (edge, edge), (blocks, column), ()), "cols")
    hidden_count = expand_fine.shape[0]
    fine_res, samples = call(
        field_kernel,
        (fine.shape, (6 * 64, 2 * fine_ch)),
        (
            edges,
            above,
            below,
            left,
            right,
            middle,
            expand_fine.T,
            depth_fine,
            shrink_fine,
            *field_tables(),
        ),
        (
            ((320, fine_ch), jnp.float32),
            ((FIELD_ROWS, hidden_count), jnp.float32),
            ((256, hidden_count), jnp.bfloat16),
            ((512, 2 * fine_ch), jnp.float32),
        ),
        scalars=1,
        staged=True,
    )
    (attended,) = call(
        attended_kernel,
        ((QUERIES, SHARDS * OUT_ROWS),),
        (blocks, *near),
        (((SHARDS, QUERIES, HEAD_ROWS), jnp.bfloat16),),
    )
    depth = jnp.pad(depth_coarse.reshape(9, SHARDS, -1), ((0, 0), (0, 0), (0, 4)))
    fine_out, coarse_out = coarse_stream(
        gathered,
        edges,
        attended,
        jnp.concatenate([own, left[48:], right[48:]]),
        depth.reshape(9, -1),
        samples,
        fine_res,
        to_fine,
    )
    return (fine_out.T.reshape(fine_in.shape), coarse_out.T.reshape(coarse_in.shape))


def solution(mesh):
    return jax.shard_map(
        local,
        mesh=mesh,
        in_specs=(
            P("rows", "cols", None, None),
            P("rows", "cols", None, None),
            P(),
            P(),
            P(),
            P(),
            P(),
            P(None, "rows", None),
            P(None, "rows"),
            P("rows", None),
            P(),
            P(None, "rows"),
            P(),
            P(None, "rows", None),
        ),
        out_specs=(P("rows", "cols", None, None), P("rows", "cols", None, None)),
        check_vma=False,
    )
```

```python
import math

import jax
import jax.numpy as jnp
from jax import lax
import numpy as np
from jax.experimental import pallas as pl
from jax.experimental.pallas import tpu as pltpu
from jax.sharding import PartitionSpec as P

HEADS_FINE = 8
WIN = 7


EPSILON = 1e-05


CELLS = WIN * WIN
RING = WIN + 2
HEAD_ROWS = 40
BLOCK_ROWS = 4 * HEAD_ROWS
OUT_ROWS = 48
TAP_ROWS = 5 * HEAD_ROWS + 8
SHARDS = 16
TILE = 56
STRIP = 64
QUERIES = 96
SIDE = 2 * WIN
FIELD = SIDE + 3
FIELD_ROWS = 304
TOP, BOTTOM, LEFT, RIGHT = 200, 232, 248, 288


def pack(outproj, expand, shrink, to_coarse):
    width = expand.shape[-1]
    taps = jnp.pad(to_coarse, ((0, 1), (0, 1), (0, 0))).reshape(5, 2, HEAD_ROWS, -1)
    return jnp.concatenate(
        [
            jnp.pad(expand, ((0, 4), (0, 0))),
            jnp.pad(shrink.T, ((0, 4), (0, 0))),
            jnp.pad(outproj.T, ((0, 1), (0, 0))),
            taps.transpose(0, 2, 1, 3).reshape(-1, width),
        ]
    )


def strip_tables():
    spread = np.zeros((STRIP, 3 * TILE), np.float32)
    columns = np.zeros((32, STRIP), np.float32)
    for row in range(RING):
        for col in range(WIN):
            spread[row * WIN + col, (row + 6) // WIN * TILE + (row + 6) % WIN * WIN + col] = 1
        columns[row, row * WIN + WIN - 1] = 1
        columns[16 + row, row * WIN] = 1
    return tuple(jnp.asarray(t).astype(jnp.bfloat16) for t in (spread, columns))


def window_table():
    cells = np.arange(SIDE * SIDE)
    window = cells // SIDE // WIN * 2 + cells % SIDE // WIN
    return jnp.asarray(np.where(window[:, None] == window[None], 0.0, -1e30).astype(np.float32))


def border_tables():
    right = np.zeros((40, 248), np.float32)
    left = np.zeros((32, 248), np.float32)

    def source(row, col):
        if row < 0:
            return TOP + (row + 2) * SIDE + col
        return row * SIDE + col if row < SIDE else BOTTOM + col

    for row in range(FIELD):
        for col in range(2):
            right[row * 2 + col, source(row - 2, SIDE - 2 + col)] = 1
        left[row, source(row - 2, 0)] = 1
    return jnp.asarray(right).astype(jnp.bfloat16), jnp.asarray(left).astype(jnp.bfloat16)


def field_tables():
    gather = np.zeros((FIELD_ROWS, 320), np.float32)
    inner = np.zeros((256, FIELD_ROWS), np.float32)
    for row in range(FIELD):
        for col in range(FIELD):
            if col < 2:
                source = LEFT + row * 2 + col
            elif col == FIELD - 1:
                source = RIGHT + row
            elif row < 2:
                source = TOP + row * SIDE + col - 2
            elif row == FIELD - 1:
                source = BOTTOM + col - 2
            else:
                source = (row - 2) * SIDE + col - 2
            gather[row * FIELD + col, source] = 1
    for row in range(15):
        for col in range(15):
            inner[row * 16 + col, (row + 1) * FIELD + col + 1] = 1
    tile = np.zeros((SIDE * SIDE, 256), np.float32)
    for row in range(SIDE):
        for col in range(SIDE):
            tile[row * SIDE + col, (row + 1) * 16 + col + 1] = 1
    sample = np.zeros((5 * 64, 512), np.float32)
    for cell in range(CELLS):
        row, col = divmod(cell, WIN)
        for tap in range(9):
            source = (2 * row + tap // 3) * 16 + 2 * col + tap % 3
            sample[tap // 2 * 64 + cell, tap % 2 * 256 + source] = 1
    return tuple(jnp.asarray(t).astype(jnp.bfloat16) for t in (gather, inner, tile, sample))


def cell_tables():
    side = 2 * WIN
    square = np.zeros((QUERIES, QUERIES), np.float32)
    for row in range(RING):
        for col in range(WIN):
            square[row * RING + col + 1, row * WIN + col] = 1
        square[row * RING, STRIP + row] = 1
        square[row * RING + RING - 1, STRIP + 16 + row] = 1
    centre = np.zeros((64, QUERIES), np.float32)
    repeat = np.zeros((side * side, 64), np.float32)
    compact = np.zeros((CELLS, 64), np.float32)
    for cell in range(CELLS):
        row, col = divmod(cell, WIN)
        centre[row * 8 + col, (row + 1) * RING + col + 1] = 1
        compact[cell, row * 8 + col] = 1
    for cell in range(side * side):
        row, col = divmod(cell, side)
        repeat[cell, row // 2 * 8 + col // 2] = 1
    return tuple(jnp.asarray(t).astype(jnp.bfloat16) for t in (square, centre, repeat, compact))


def gelu(values):
    return values * (lax.erf(values * math.sqrt(0.5)) + 1.0) * 0.5


def norm_rows(values):
    center = jnp.mean(values, axis=1, keepdims=True)
    away = values - center
    spread = jnp.mean(away * away, axis=1, keepdims=True)
    return (away * lax.rsqrt(spread + EPSILON)).astype(jnp.bfloat16)


def nn(left, right):
    return lax.dot_general(
        left, right, (((1,), (0,)), ((), ())), preferred_element_type=jnp.float32
    )


def nt(left, right):
    return lax.dot_general(
        left, right, (((1,), (1,)), ((), ())), preferred_element_type=jnp.float32
    )


def fine_attention_kernel(
    fine_ref, inproj_ref, outproj_ref, mask_ref, middle_ref, down_ref, up_ref
):
    cells, channels = fine_ref.shape
    fine = fine_ref[...].astype(jnp.float32)
    normed = norm_rows(fine)
    queries, keys, values = (nt(normed, inproj_ref[i]).astype(jnp.bfloat16) for i in range(3))
    channel = lax.broadcasted_iota(jnp.int32, (cells, channels), 1)
    mask = mask_ref[...]
    nothing = jnp.zeros((cells, channels), jnp.bfloat16)
    attended = jnp.zeros((cells, channels), jnp.float32)
    for head in range(HEADS_FINE):
        mine = (channel >= head * 39) & (channel < (head + 1) * 39)
        chosen = jnp.where(mine, queries, nothing)
        scores = nt(chosen, keys) * (1.0 / math.sqrt(39)) + mask
        exponent = jnp.exp(scores - jnp.max(scores, axis=1, keepdims=True))
        total = jnp.sum(exponent, axis=1, keepdims=True)
        chance = (exponent * (1.0 / total)).astype(jnp.bfloat16)
        attended += nn(chance, jnp.where(mine, values, nothing))
    middle = fine + nt(attended.astype(jnp.bfloat16), outproj_ref[...])
    middle_ref[...] = middle.astype(jnp.bfloat16)
    for target, first, count in ((down_ref, cells - 2 * SIDE, 2 * SIDE), (up_ref, 0, SIDE)):
        target[...] = jnp.zeros(target.shape, jnp.bfloat16)
        target[:count, :] = middle_ref[first : first + count, :]


def columns_kernel(
    above_ref, below_ref, middle_ref, columns_ref, right_ref, left_ref, to_right_ref, to_left_ref,
    field_ref,
):
    cells, channels = middle_ref.shape
    field_ref[...] = jnp.zeros(field_ref.shape, jnp.float32)
    field_ref[:cells, :] = middle_ref[...].astype(jnp.float32)
    field_ref[TOP : TOP + 2 * SIDE, :] = above_ref[: 2 * SIDE, :].astype(jnp.float32)
    field_ref[BOTTOM : BOTTOM + SIDE, :] = below_ref[:SIDE, :].astype(jnp.float32)
    field = field_ref[...].astype(jnp.bfloat16)
    for index, (target, table) in enumerate(((to_right_ref, right_ref), (to_left_ref, left_ref))):
        target[...] = jnp.zeros(target.shape, jnp.bfloat16)
        count = table.shape[0]
        target[:count, :channels] = nn(table[...], field).astype(jnp.bfloat16)
        target[48:, :] = columns_ref[16 * index : 16 * index + 16, :]


def strip_kernel(
    edge_ref,
    place_ref,
    strip_ref,
    weights_ref,
    spread_ref,
    column_ref,
    blocks_ref,
    own_ref,
    columns_ref,
    normed_ref,
    proj_ref,
    scores_ref,
    attended_ref,
    images_ref,
):
    tiles, cells, width = strip_ref.shape
    normed_ref[...] = jnp.zeros(normed_ref.shape, jnp.float32)
    attended_ref[...] = jnp.zeros(attended_ref.shape, jnp.float32)
    images_ref[...] = jnp.zeros(images_ref.shape, jnp.float32)
    for tile in range(tiles):
        normed_ref[tile, :cells, :] = norm_rows(strip_ref[tile].astype(jnp.float32)).astype(
            jnp.float32
        )
    normed = normed_ref[...].astype(jnp.bfloat16).reshape(tiles * TILE, width)
    for part in range(3):
        proj_ref[part] = nt(normed, weights_ref[part]).reshape(tiles, TILE, -1)
    for tile in range(tiles):
        queries, keys = (proj_ref[part, tile].astype(jnp.bfloat16) for part in range(2))
        scores_ref[tile] = nt(queries, keys)
    key = lax.broadcasted_iota(jnp.int32, (tiles * TILE, TILE), 1)
    scores = scores_ref[...].reshape(tiles * TILE, TILE) * (1.0 / math.sqrt(39))
    scores += jnp.where(key < cells, 0.0, -1e30)
    exponent = jnp.exp(scores - jnp.max(scores, axis=1, keepdims=True))
    total = jnp.sum(exponent, axis=1, keepdims=True)
    scores_ref[...] = (exponent * (1.0 / total)).reshape(tiles, TILE, TILE)
    for tile in range(tiles):
        values = proj_ref[2, tile].astype(jnp.bfloat16)
        attended_ref[tile + 1, :, :39] = nn(scores_ref[tile].astype(jnp.bfloat16), values)
    spread = spread_ref[...]
    for tile in range(tiles):
        near = attended_ref[tile : tile + 3].astype(jnp.bfloat16).reshape(3 * TILE, HEAD_ROWS)
        blocks_ref[tile] = nn(spread, near).astype(jnp.bfloat16)
    place = place_ref[0]
    before = jnp.maximum(place - 1, 0)
    after = jnp.minimum(place + 1, tiles - 1)
    for index, (tile, there) in enumerate(
        ((before, edge_ref[0]), (place, 1), (after, edge_ref[1]))
    ):
        image = strip_ref[tile].astype(jnp.float32)
        images_ref[index * TILE : index * TILE + cells, :] = jnp.where(there == 1, image, 0.0)
    own = nn(spread, images_ref[...].astype(jnp.bfloat16)).astype(jnp.bfloat16)
    own_ref[...] = own
    columns_ref[...] = nn(column_ref[...], own).astype(jnp.bfloat16)


def edge_columns_kernel(blocks_ref, column_ref, right_ref, left_ref):
    for head in range(SHARDS):
        columns = nn(column_ref[...], blocks_ref[head]).astype(jnp.bfloat16)
        right_ref[head] = columns[:16]
        left_ref[head] = columns[16:]


def attended_kernel(blocks_ref, left_ref, right_ref, flat_ref, parts_ref):
    parts_ref[:, :STRIP, :] = blocks_ref[...]
    parts_ref[:, STRIP : STRIP + 16, :] = left_ref[...]
    parts_ref[:, STRIP + 16 :, :] = right_ref[...]
    channel = lax.broadcasted_iota(jnp.int32, (HEAD_ROWS, SHARDS * OUT_ROWS), 0)
    lane = lax.broadcasted_iota(jnp.int32, (HEAD_ROWS, SHARDS * OUT_ROWS), 1)
    flat = jnp.zeros(flat_ref.shape, jnp.float32)
    for head in range(SHARDS):
        move = jnp.where(lane == channel + head * OUT_ROWS, 1.0, 0.0).astype(jnp.bfloat16)
        flat += nn(parts_ref[head], move)
    flat_ref[...] = flat.astype(jnp.bfloat16)


def field_kernel(
    edge_ref,
    above_ref,
    below_ref,
    left_ref,
    right_ref,
    middle_ref,
    expand_ref,
    depth_ref,
    shrink_ref,
    gather_ref,
    inner_ref,
    cell_ref,
    sample_ref,
    fine_ref,
    samples_ref,
    pieces_ref,
    hidden_ref,
    conv_ref,
    twice_ref,
):
    cells, channels = middle_ref.shape
    pieces_ref[...] = jnp.zeros(pieces_ref.shape, jnp.float32)
    pieces_ref[:cells, :] = middle_ref[...].astype(jnp.float32)
    for piece, start, first, count in (
        (above_ref, 0, TOP, 2 * SIDE),
        (below_ref, 0, BOTTOM, SIDE),
        (left_ref, 0, LEFT, 2 * FIELD),
        (right_ref, 0, RIGHT, FIELD),
    ):
        pieces_ref[first : first + count, :] = piece[start : start + count, :channels].astype(
            jnp.float32
        )
    field = nn(gather_ref[...], pieces_ref[...].astype(jnp.bfloat16))
    normed_mid = norm_rows(field)
    row = lax.broadcasted_iota(jnp.int32, (FIELD_ROWS, 128), 0)
    column = row % FIELD
    outside = (
        ((row < 2 * FIELD) & (edge_ref[0] == 0))
        | ((row >= FIELD * (FIELD - 1)) & (edge_ref[1] == 0))
        | ((column < 2) & (edge_ref[2] == 0))
        | ((column == FIELD - 1) & (edge_ref[3] == 0))
    )
    inside = jnp.where(outside, 0.0, 1.0)[:, :1]
    hidden_count = hidden_ref.shape[1]
    conv_ref[15 * 16 :, :] = jnp.zeros((16, hidden_count), jnp.bfloat16)
    for first in range(0, hidden_count, 384):
        span = pl.ds(first, min(384, hidden_count - first))
        hidden = gelu(nn(normed_mid, expand_ref[:, span])) * inside
        hidden_ref[:, span] = hidden.astype(jnp.bfloat16).astype(jnp.float32)
        for out in range(15):
            total = jnp.zeros((16, span.size), jnp.float32)
            for tap in range(9):
                down, side = divmod(tap, 3)
                window = hidden_ref[pl.ds((out + down) * FIELD + side, 16), span]
                total += depth_ref[tap : tap + 1, span] * window
            conv_ref[out * 16 : out * 16 + 16, span] = gelu(total).astype(jnp.bfloat16)
    update = nt(conv_ref[...], shrink_ref[...])
    result = nn(inner_ref[...], field.astype(jnp.bfloat16)) + update
    row = lax.broadcasted_iota(jnp.int32, (256, 128), 0)
    outside = ((row < 16) & (edge_ref[0] == 0)) | ((row % 16 == 0) & (edge_ref[2] == 0))
    result = result * jnp.where(outside, 0.0, 1.0)[:, :1]
    rounded = result.astype(jnp.bfloat16)
    fine_ref[...] = nn(cell_ref[...], rounded).astype(jnp.bfloat16)
    result = rounded.astype(jnp.float32)
    twice_ref[...] = jnp.zeros(twice_ref.shape, jnp.float32)
    twice_ref[:256, :channels] = result
    twice_ref[256:, channels:] = result
    samples_ref[...] = nn(sample_ref[...], twice_ref[...].astype(jnp.bfloat16)).astype(jnp.bfloat16)


def call(kernel, shapes, operands, scratch, scalars=0, fetch=(), limit=32):
    smem, vmem, hbm = (
        pl.BlockSpec(memory_space=space) for space in (pltpu.SMEM, pltpu.VMEM, pltpu.HBM)
    )
    count = len(operands)
    scratch_shapes = [pltpu.VMEM(shape, kind) for shape, kind in scratch]
    scratch_shapes += [pltpu.VMEM(operands[i].shape, operands[i].dtype) for i in fetch]
    scratch_shapes.append(pltpu.SemaphoreType.DMA((max(len(fetch), 1),)))

    def fetching(*refs):
        given, rest, sems = list(refs[:count]), refs[count:-1], refs[-1]
        own, landed = rest[: len(rest) - len(fetch)], rest[len(rest) - len(fetch) :]
        copies = [
            pltpu.make_async_copy(given[place], target, sems.at[index])
            for index, (place, target) in enumerate(zip(fetch, landed))
        ]
        for copy in copies:
            copy.start()
        for place, target in zip(fetch, landed):
            given[place] = target
        for copy in copies:
            copy.wait()
        kernel(*given, *own)

    return pl.pallas_call(
        fetching,
        out_shape=tuple(jax.ShapeDtypeStruct(shape, jnp.bfloat16) for shape in shapes),
        in_specs=[
            smem if place < scalars else hbm if place in fetch else vmem for place in range(count)
        ],
        out_specs=(vmem,) * len(shapes),
        scratch_shapes=scratch_shapes,
        compiler_params=pltpu.CompilerParams(vmem_limit_bytes=limit * 1024 * 1024),
    )(*operands)


def coarse_kernel(edge_ref, gathered_ref, *refs):
    count = 6
    direct, operands = refs[:4], refs[4 : 4 + count]
    outputs, landed = refs[4 + count : 6 + count], refs[-count - 1 : -1]
    small = [
        pltpu.make_async_copy(source, target, refs[-1].at[index])
        for index, (source, target) in enumerate(zip(operands, landed))
    ]
    for copy in small:
        copy.start()
    coarse_body(
        edge_ref, gathered_ref, small, *direct, *landed, *outputs, *refs[6 + count : -count - 1]
    )


def coarse_body(
    edge_ref,
    gathered_ref,
    small,
    attended_ref,
    own_ref,
    samples_ref,
    fine_ref,
    depth_ref,
    to_fine_ref,
    square_ref,
    centre_ref,
    repeat_ref,
    compact_ref,
    fine_out_ref,
    coarse_out_ref,
    out_ref,
    expand_ref,
    shrink_ref,
    taps_ref,
    hidden_ref,
    conv_ref,
    down_ref,
    sems,
):
    spans = (
        (out_ref, 2 * BLOCK_ROWS, OUT_ROWS),
        (expand_ref, 0, BLOCK_ROWS),
        (shrink_ref, BLOCK_ROWS, BLOCK_ROWS),
        (taps_ref, 2 * BLOCK_ROWS + 32, TAP_ROWS),
    )
    copies = [
        pltpu.make_async_copy(gathered_ref.at[:, pl.ds(first, count)], target, sems.at[part])
        for part, (target, first, count) in enumerate(spans)
    ]
    for copy in copies:
        copy.start()
    for copy in small:
        copy.wait()
    width = own_ref.shape[1]
    query = lax.broadcasted_iota(jnp.int32, (QUERIES, 128), 0)
    column = query % RING
    outside = (
        ((query < RING) & (edge_ref[0] == 0))
        | ((query >= RING * (RING - 1)) & (edge_ref[1] == 0))
        | ((column == 0) & (edge_ref[2] == 0))
        | ((column == RING - 1) & (edge_ref[3] == 0))
    )
    inside = jnp.where(outside, 0.0, 1.0)[:, :1]
    conv_ref[8 * WIN :, :] = jnp.zeros((8, conv_ref.shape[1]), jnp.float32)
    mixed = own_ref[...].astype(jnp.float32)
    copies[0].wait()
    mixed += nn(attended_ref[...], out_ref[...].reshape(SHARDS * OUT_ROWS, width))
    middle = nn(square_ref[...], mixed.astype(jnp.bfloat16)).astype(jnp.bfloat16)
    normed_mid = norm_rows(middle.astype(jnp.float32))
    copies[1].wait()
    chunk = 512
    expand = expand_ref[...].reshape(SHARDS * BLOCK_ROWS, width)
    for first in range(0, SHARDS * BLOCK_ROWS, chunk):
        span = pl.ds(first, chunk)
        hidden = gelu(nt(normed_mid, expand[first : first + chunk])) * inside
        hidden_ref[:, span] = hidden.astype(jnp.bfloat16).astype(jnp.float32)
        for row in range(WIN):
            total = jnp.zeros((8, chunk), jnp.float32)
            for tap in range(9):
                down, side = divmod(tap, 3)
                window = hidden_ref[pl.ds((row + down) * RING + side, 8), span]
                total += depth_ref[tap : tap + 1, span] * window
            conv_ref[row * 8 : row * 8 + 8, span] = gelu(total)
    copies[2].wait()
    shrink = shrink_ref[...].reshape(SHARDS * BLOCK_ROWS, width)
    update = nn(conv_ref[...].astype(jnp.bfloat16), shrink)
    result = (nn(centre_ref[...], middle) + update).astype(jnp.bfloat16)
    spread = nn(repeat_ref[...], result).astype(jnp.bfloat16)
    upsampled = nt(spread, to_fine_ref[...])
    fine_out_ref[...] = jnp.maximum(
        fine_ref[...].astype(jnp.float32) + upsampled, 0.0
    ).astype(jnp.bfloat16)
    copies[3].wait()
    samples = samples_ref[...]
    for shard in range(SHARDS):
        four = nt(taps_ref[shard], samples[: 4 * 64])
        fifth = nt(taps_ref[shard][4 * HEAD_ROWS :], samples[4 * 64 :])
        total = fifth[8:]
        for block in range(4):
            rows = slice(8 + block * HEAD_ROWS, 8 + (block + 1) * HEAD_ROWS)
            total += four[rows, block * 64 : (block + 1) * 64]
        down_ref[shard * 39 : shard * 39 + HEAD_ROWS, :64] = total
    downsampled = down_ref[...].T[:CELLS, :width].astype(jnp.bfloat16).astype(jnp.float32)
    coarse_out_ref[...] = jnp.maximum(
        nn(compact_ref[...], result) + downsampled, 0.0
    ).astype(jnp.bfloat16)


def coarse_stream(gathered, edges, attended, own, depth, samples, fine_res, to_fine):
    width = own.shape[1]
    fine_cells, fine_ch = fine_res.shape
    operands = (attended, own, samples, fine_res, depth, to_fine, *cell_tables())
    smem, vmem, hbm = (
        pl.BlockSpec(memory_space=space) for space in (pltpu.SMEM, pltpu.VMEM, pltpu.HBM)
    )
    return pl.pallas_call(
        coarse_kernel,
        out_shape=(
            jax.ShapeDtypeStruct((fine_cells, fine_ch), jnp.bfloat16),
            jax.ShapeDtypeStruct((CELLS, width), jnp.bfloat16),
        ),
        in_specs=[smem, hbm] + [vmem] * 4 + [hbm] * (len(operands) - 4),
        out_specs=(vmem, vmem),
        scratch_shapes=[
            pltpu.VMEM((SHARDS, OUT_ROWS, width), jnp.bfloat16),
            pltpu.VMEM((SHARDS, BLOCK_ROWS, width), jnp.bfloat16),
            pltpu.VMEM((SHARDS, BLOCK_ROWS, width), jnp.bfloat16),
            pltpu.VMEM((SHARDS, TAP_ROWS, width), jnp.bfloat16),
            pltpu.VMEM((QUERIES, SHARDS * BLOCK_ROWS), jnp.float32),
            pltpu.VMEM((64, SHARDS * BLOCK_ROWS), jnp.float32),
            pltpu.VMEM((SHARDS * HEAD_ROWS, 128), jnp.float32),
            pltpu.SemaphoreType.DMA((4,)),
            *(pltpu.VMEM(operand.shape, operand.dtype) for operand in operands[4:]),
            pltpu.SemaphoreType.DMA((len(operands) - 4,)),
        ],
        compiler_params=pltpu.CompilerParams(vmem_limit_bytes=40 * 1024 * 1024),
    )(edges, gathered, *operands)


def exchange(onward, back, axis):
    up = [(i, i + 1) for i in range(lax.axis_size(axis) - 1)]
    down = [(j, i) for i, j in up]
    return lax.ppermute(onward, axis, up), lax.ppermute(back, axis, down)


def local(
    fine_in,
    coarse_in,
    inproj_fine,
    outproj_fine,
    expand_fine,
    depth_fine,
    shrink_fine,
    inproj_coarse,
    outproj_coarse,
    expand_coarse,
    depth_coarse,
    shrink_coarse,
    to_fine,
    to_coarse,
):
    fine_ch, fine_cells = fine_in.shape[2:]
    coarse_ch, coarse_cells = coarse_in.shape[2:]
    gathered = lax.all_gather(pack(outproj_coarse, expand_coarse, shrink_coarse, to_coarse), "rows")
    strip = lax.all_gather(coarse_in.reshape(coarse_ch, coarse_cells).T, "rows")
    fine = fine_in.reshape(fine_ch, fine_cells).T
    place = (lax.axis_index("rows"), lax.axis_index("cols"))
    edges = jnp.stack(
        [
            place[0] > 0,
            place[0] < lax.axis_size("rows") - 1,
            place[1] > 0,
            place[1] < lax.axis_size("cols") - 1,
        ]
    ).astype(jnp.int32)
    middle, going_down, going_up = call(
        fine_attention_kernel,
        (fine.shape, (32, fine_ch), (16, fine_ch)),
        (fine, inproj_fine, outproj_fine, window_table()),
        (),
        fetch=(0, 1, 2, 3),
    )
    above, below = exchange(going_down, going_up, "rows")
    spread, column = strip_tables()
    blocks, own, columns = call(
        strip_kernel,
        ((SHARDS, STRIP, HEAD_ROWS), (STRIP, coarse_ch), (32, coarse_ch)),
        (edges, place[0].reshape(1).astype(jnp.int32), strip, inproj_coarse, spread, column),
        (
            ((SHARDS, TILE, coarse_ch), jnp.float32),
            ((3, SHARDS, TILE, 39), jnp.float32),
            ((SHARDS, TILE, TILE), jnp.float32),
            ((SHARDS + 2, TILE, HEAD_ROWS), jnp.float32),
            ((3 * TILE, coarse_ch), jnp.float32),
        ),
        scalars=2,
        fetch=(3, 4, 5),
    )
    blocks = lax.all_to_all(blocks, "rows", 0, 0, tiled=True)
    going_right, going_left = call(
        columns_kernel,
        ((64, coarse_ch), (64, coarse_ch)),
        (above, below, middle, columns, *border_tables()),
        (((248, fine_ch), jnp.float32),),
        fetch=(4, 5),
    )
    left, right = exchange(going_right, going_left, "cols")
    edge = (SHARDS, 16, HEAD_ROWS)
    near = exchange(*call(edge_columns_kernel, (edge, edge), (blocks, column), (), fetch=(1,)), "cols")
    hidden_count = expand_fine.shape[0]
    fine_res, samples = call(
        field_kernel,
        (fine.shape, (5 * 64, 2 * fine_ch)),
        (
            edges,
            above,
            below,
            left,
            right,
            middle,
            expand_fine.T,
            depth_fine,
            shrink_fine,
            *field_tables(),
        ),
        (
            ((320, fine_ch), jnp.float32),
            ((FIELD_ROWS, hidden_count), jnp.float32),
            ((256, hidden_count), jnp.bfloat16),
            ((512, 2 * fine_ch), jnp.float32),
        ),
        scalars=1,
        fetch=tuple(range(6, 13)),
    )
    (attended,) = call(
        attended_kernel,
        ((QUERIES, SHARDS * OUT_ROWS),),
        (blocks, *near),
        (((SHARDS, QUERIES, HEAD_ROWS), jnp.bfloat16),),
    )
    depth = jnp.pad(depth_coarse.reshape(9, SHARDS, -1), ((0, 0), (0, 0), (0, 4)))
    fine_out, coarse_out = coarse_stream(
        gathered,
        edges,
        attended,
        jnp.concatenate([own, left[48:], right[48:]]),
        depth.reshape(9, -1),
        samples,
        fine_res,
        to_fine,
    )
    return (fine_out.T.reshape(fine_in.shape), coarse_out.T.reshape(coarse_in.shape))


def solution(mesh):
    return jax.shard_map(
        local,
        mesh=mesh,
        in_specs=(
            P("rows", "cols", None, None),
            P("rows", "cols", None, None),
            P(),
            P(),
            P(),
            P(),
            P(),
            P(None, "rows", None),
            P(None, "rows"),
            P("rows", None),
            P(),
            P(None, "rows"),
            P(),
            P(None, "rows", None),
        ),
        out_specs=(P("rows", "cols", None, None), P("rows", "cols", None, None)),
        check_vma=False,
    )
```

```python
import math

import jax
import jax.numpy as jnp
from jax import lax
import numpy as np
from jax.experimental import pallas as pl
from jax.experimental.pallas import tpu as pltpu
from jax.sharding import PartitionSpec as P

HEADS_FINE = 8
WIN = 7


EPSILON = 1e-05


CELLS = WIN * WIN
RING = WIN + 2
HEAD_ROWS = 40
BLOCK_ROWS = 4 * HEAD_ROWS
OUT_ROWS = 48
TAP_ROWS = 5 * HEAD_ROWS + 8
SHARDS = 16
TILE = 56
STRIP = 64
QUERIES = 96
SIDE = 2 * WIN
FIELD = SIDE + 3
FIELD_ROWS = 304
TOP, BOTTOM, LEFT, RIGHT = 200, 232, 248, 288


def pack(outproj, expand, shrink, to_coarse):
    width = expand.shape[-1]
    taps = jnp.pad(to_coarse, ((0, 1), (0, 1), (0, 0))).reshape(5, 2, HEAD_ROWS, -1)
    return jnp.concatenate(
        [
            jnp.pad(expand, ((0, 4), (0, 0))),
            jnp.pad(shrink.T, ((0, 4), (0, 0))),
            jnp.pad(outproj.T, ((0, 1), (0, 0))),
            taps.transpose(0, 2, 1, 3).reshape(-1, width),
        ]
    )


def strip_tables():
    spread = np.zeros((STRIP, 3 * TILE), np.float32)
    columns = np.zeros((32, STRIP), np.float32)
    for row in range(RING):
        for col in range(WIN):
            spread[row * WIN + col, (row + 6) // WIN * TILE + (row + 6) % WIN * WIN + col] = 1
        columns[row, row * WIN + WIN - 1] = 1
        columns[16 + row, row * WIN] = 1
    return tuple(jnp.asarray(t).astype(jnp.bfloat16) for t in (spread, columns))


def window_table():
    cells = np.arange(SIDE * SIDE)
    window = cells // SIDE // WIN * 2 + cells % SIDE // WIN
    return jnp.asarray(np.where(window[:, None] == window[None], 0.0, -1e30).astype(np.float32))


def border_tables():
    right = np.zeros((40, 248), np.float32)
    left = np.zeros((32, 248), np.float32)

    def source(row, col):
        if row < 0:
            return TOP + (row + 2) * SIDE + col
        return row * SIDE + col if row < SIDE else BOTTOM + col

    for row in range(FIELD):
        for col in range(2):
            right[row * 2 + col, source(row - 2, SIDE - 2 + col)] = 1
        left[row, source(row - 2, 0)] = 1
    return jnp.asarray(right).astype(jnp.bfloat16), jnp.asarray(left).astype(jnp.bfloat16)


def field_tables():
    gather = np.zeros((FIELD_ROWS, 320), np.float32)
    inner = np.zeros((256, FIELD_ROWS), np.float32)
    for row in range(FIELD):
        for col in range(FIELD):
            if col < 2:
                source = LEFT + row * 2 + col
            elif col == FIELD - 1:
                source = RIGHT + row
            elif row < 2:
                source = TOP + row * SIDE + col - 2
            elif row == FIELD - 1:
                source = BOTTOM + col - 2
            else:
                source = (row - 2) * SIDE + col - 2
            gather[row * FIELD + col, source] = 1
    for row in range(15):
        for col in range(15):
            inner[row * 16 + col, (row + 1) * FIELD + col + 1] = 1
    tile = np.zeros((SIDE * SIDE, 256), np.float32)
    for row in range(SIDE):
        for col in range(SIDE):
            tile[row * SIDE + col, (row + 1) * 16 + col + 1] = 1
    sample = np.zeros((5 * 64, 512), np.float32)
    for cell in range(CELLS):
        row, col = divmod(cell, WIN)
        for tap in range(9):
            source = (2 * row + tap // 3) * 16 + 2 * col + tap % 3
            sample[tap // 2 * 64 + cell, tap % 2 * 256 + source] = 1
    return tuple(jnp.asarray(t).astype(jnp.bfloat16) for t in (gather, inner, tile, sample))


def cell_tables():
    side = 2 * WIN
    square = np.zeros((QUERIES, QUERIES), np.float32)
    for row in range(RING):
        for col in range(WIN):
            square[row * RING + col + 1, row * WIN + col] = 1
        square[row * RING, STRIP + row] = 1
        square[row * RING + RING - 1, STRIP + 16 + row] = 1
    centre = np.zeros((64, QUERIES), np.float32)
    repeat = np.zeros((side * side, 64), np.float32)
    compact = np.zeros((CELLS, 64), np.float32)
    for cell in range(CELLS):
        row, col = divmod(cell, WIN)
        centre[row * 8 + col, (row + 1) * RING + col + 1] = 1
        compact[cell, row * 8 + col] = 1
    for cell in range(side * side):
        row, col = divmod(cell, side)
        repeat[cell, row // 2 * 8 + col // 2] = 1
    return tuple(jnp.asarray(t).astype(jnp.bfloat16) for t in (square, centre, repeat, compact))


def gelu(values):
    return values * (lax.erf(values * math.sqrt(0.5)) + 1.0) * 0.5


def norm_rows(values):
    center = jnp.mean(values, axis=1, keepdims=True)
    away = values - center
    spread = jnp.mean(away * away, axis=1, keepdims=True)
    return (away * lax.rsqrt(spread + EPSILON)).astype(jnp.bfloat16)


def nn(left, right):
    return lax.dot_general(
        left, right, (((1,), (0,)), ((), ())), preferred_element_type=jnp.float32
    )


def nt(left, right):
    return lax.dot_general(
        left, right, (((1,), (1,)), ((), ())), preferred_element_type=jnp.float32
    )


def fine_attention_kernel(
    fine_ref, inproj_ref, outproj_ref, mask_ref, middle_ref, down_ref, up_ref
):
    cells, channels = fine_ref.shape
    fine = fine_ref[...].astype(jnp.float32)
    normed = norm_rows(fine)
    queries, keys, values = (nt(normed, inproj_ref[i]).astype(jnp.bfloat16) for i in range(3))
    channel = lax.broadcasted_iota(jnp.int32, (cells, channels), 1)
    mask = mask_ref[...]
    nothing = jnp.zeros((cells, channels), jnp.bfloat16)
    attended = jnp.zeros((cells, channels), jnp.float32)
    for head in range(HEADS_FINE):
        mine = (channel >= head * 39) & (channel < (head + 1) * 39)
        chosen = jnp.where(mine, queries, nothing)
        scores = nt(chosen, keys) * (1.0 / math.sqrt(39)) + mask
        exponent = jnp.exp(scores - jnp.max(scores, axis=1, keepdims=True))
        total = jnp.sum(exponent, axis=1, keepdims=True)
        chance = (exponent * (1.0 / total)).astype(jnp.bfloat16)
        attended += nn(chance, jnp.where(mine, values, nothing))
    middle = fine + nt(attended.astype(jnp.bfloat16), outproj_ref[...])
    middle_ref[...] = middle.astype(jnp.bfloat16)
    for target, first, count in ((down_ref, cells - 2 * SIDE, 2 * SIDE), (up_ref, 0, SIDE)):
        target[...] = jnp.zeros(target.shape, jnp.bfloat16)
        target[:count, :] = middle_ref[first : first + count, :]


def columns_kernel(
    above_ref, below_ref, middle_ref, columns_ref, right_ref, left_ref, to_right_ref, to_left_ref,
    field_ref,
):
    cells, channels = middle_ref.shape
    field_ref[...] = jnp.zeros(field_ref.shape, jnp.float32)
    field_ref[:cells, :] = middle_ref[...].astype(jnp.float32)
    field_ref[TOP : TOP + 2 * SIDE, :] = above_ref[: 2 * SIDE, :].astype(jnp.float32)
    field_ref[BOTTOM : BOTTOM + SIDE, :] = below_ref[:SIDE, :].astype(jnp.float32)
    field = field_ref[...].astype(jnp.bfloat16)
    for index, (target, table) in enumerate(((to_right_ref, right_ref), (to_left_ref, left_ref))):
        target[...] = jnp.zeros(target.shape, jnp.bfloat16)
        count = table.shape[0]
        target[:count, :channels] = nn(table[...], field).astype(jnp.bfloat16)
        target[48:, :] = columns_ref[16 * index : 16 * index + 16, :]


def strip_kernel(
    edge_ref,
    place_ref,
    strip_ref,
    weights_ref,
    spread_ref,
    column_ref,
    blocks_ref,
    own_ref,
    columns_ref,
    normed_ref,
    proj_ref,
    scores_ref,
    attended_ref,
    images_ref,
):
    tiles, cells, width = strip_ref.shape
    normed_ref[...] = jnp.zeros(normed_ref.shape, jnp.float32)
    attended_ref[...] = jnp.zeros(attended_ref.shape, jnp.float32)
    images_ref[...] = jnp.zeros(images_ref.shape, jnp.float32)
    for tile in range(tiles):
        normed_ref[tile, :cells, :] = norm_rows(strip_ref[tile].astype(jnp.float32)).astype(
            jnp.float32
        )
    normed = normed_ref[...].astype(jnp.bfloat16).reshape(tiles * TILE, width)
    for part in range(3):
        proj_ref[part] = nt(normed, weights_ref[part]).reshape(tiles, TILE, -1)
    for tile in range(tiles):
        queries, keys = (proj_ref[part, tile].astype(jnp.bfloat16) for part in range(2))
        scores_ref[tile] = nt(queries, keys)
    key = lax.broadcasted_iota(jnp.int32, (tiles * TILE, TILE), 1)
    scores = scores_ref[...].reshape(tiles * TILE, TILE) * (1.0 / math.sqrt(39))
    scores += jnp.where(key < cells, 0.0, -1e30)
    exponent = jnp.exp(scores - jnp.max(scores, axis=1, keepdims=True))
    total = jnp.sum(exponent, axis=1, keepdims=True)
    scores_ref[...] = (exponent * (1.0 / total)).reshape(tiles, TILE, TILE)
    for tile in range(tiles):
        values = proj_ref[2, tile].astype(jnp.bfloat16)
        attended_ref[tile + 1, :, :39] = nn(scores_ref[tile].astype(jnp.bfloat16), values)
    spread = spread_ref[...]
    for tile in range(tiles):
        near = attended_ref[tile : tile + 3].astype(jnp.bfloat16).reshape(3 * TILE, HEAD_ROWS)
        blocks_ref[tile] = nn(spread, near).astype(jnp.bfloat16)
    place = place_ref[0]
    before = jnp.maximum(place - 1, 0)
    after = jnp.minimum(place + 1, tiles - 1)
    for index, (tile, there) in enumerate(
        ((before, edge_ref[0]), (place, 1), (after, edge_ref[1]))
    ):
        image = strip_ref[tile].astype(jnp.float32)
        images_ref[index * TILE : index * TILE + cells, :] = jnp.where(there == 1, image, 0.0)
    own = nn(spread, images_ref[...].astype(jnp.bfloat16)).astype(jnp.bfloat16)
    own_ref[...] = own
    columns_ref[...] = nn(column_ref[...], own).astype(jnp.bfloat16)


def edge_columns_kernel(blocks_ref, column_ref, right_ref, left_ref):
    for head in range(SHARDS):
        columns = nn(column_ref[...], blocks_ref[head]).astype(jnp.bfloat16)
        right_ref[head] = columns[:16]
        left_ref[head] = columns[16:]


def attended_kernel(blocks_ref, left_ref, right_ref, flat_ref, parts_ref):
    parts_ref[:, :STRIP, :] = blocks_ref[...]
    parts_ref[:, STRIP : STRIP + 16, :] = left_ref[...]
    parts_ref[:, STRIP + 16 :, :] = right_ref[...]
    channel = lax.broadcasted_iota(jnp.int32, (HEAD_ROWS, SHARDS * OUT_ROWS), 0)
    lane = lax.broadcasted_iota(jnp.int32, (HEAD_ROWS, SHARDS * OUT_ROWS), 1)
    flat = jnp.zeros(flat_ref.shape, jnp.float32)
    for head in range(SHARDS):
        move = jnp.where(lane == channel + head * OUT_ROWS, 1.0, 0.0).astype(jnp.bfloat16)
        flat += nn(parts_ref[head], move)
    flat_ref[...] = flat.astype(jnp.bfloat16)


def field_kernel(
    edge_ref,
    above_ref,
    below_ref,
    left_ref,
    right_ref,
    middle_ref,
    expand_ref,
    depth_ref,
    shrink_ref,
    gather_ref,
    inner_ref,
    cell_ref,
    sample_ref,
    fine_ref,
    samples_ref,
    pieces_ref,
    hidden_ref,
    conv_ref,
    twice_ref,
):
    cells, channels = middle_ref.shape
    pieces_ref[...] = jnp.zeros(pieces_ref.shape, jnp.float32)
    pieces_ref[:cells, :] = middle_ref[...].astype(jnp.float32)
    for piece, start, first, count in (
        (above_ref, 0, TOP, 2 * SIDE),
        (below_ref, 0, BOTTOM, SIDE),
        (left_ref, 0, LEFT, 2 * FIELD),
        (right_ref, 0, RIGHT, FIELD),
    ):
        pieces_ref[first : first + count, :] = piece[start : start + count, :channels].astype(
            jnp.float32
        )
    field = nn(gather_ref[...], pieces_ref[...].astype(jnp.bfloat16))
    normed_mid = norm_rows(field)
    row = lax.broadcasted_iota(jnp.int32, (FIELD_ROWS, 128), 0)
    column = row % FIELD
    outside = (
        ((row < 2 * FIELD) & (edge_ref[0] == 0))
        | ((row >= FIELD * (FIELD - 1)) & (edge_ref[1] == 0))
        | ((column < 2) & (edge_ref[2] == 0))
        | ((column == FIELD - 1) & (edge_ref[3] == 0))
    )
    inside = jnp.where(outside, 0.0, 1.0)[:, :1]
    hidden_count = hidden_ref.shape[1]
    conv_ref[15 * 16 :, :] = jnp.zeros((16, hidden_count), jnp.bfloat16)
    for first in range(0, hidden_count, 384):
        span = pl.ds(first, min(384, hidden_count - first))
        hidden = gelu(nn(normed_mid, expand_ref[:, span])) * inside
        hidden_ref[:, span] = hidden.astype(jnp.bfloat16).astype(jnp.float32)
        for out in range(15):
            total = jnp.zeros((16, span.size), jnp.float32)
            for tap in range(9):
                down, side = divmod(tap, 3)
                window = hidden_ref[pl.ds((out + down) * FIELD + side, 16), span]
                total += depth_ref[tap : tap + 1, span] * window
            conv_ref[out * 16 : out * 16 + 16, span] = gelu(total).astype(jnp.bfloat16)
    update = nt(conv_ref[...], shrink_ref[...])
    result = nn(inner_ref[...], field.astype(jnp.bfloat16)) + update
    row = lax.broadcasted_iota(jnp.int32, (256, 128), 0)
    outside = ((row < 16) & (edge_ref[0] == 0)) | ((row % 16 == 0) & (edge_ref[2] == 0))
    result = result * jnp.where(outside, 0.0, 1.0)[:, :1]
    rounded = result.astype(jnp.bfloat16)
    fine_ref[...] = nn(cell_ref[...], rounded).astype(jnp.bfloat16)
    result = rounded.astype(jnp.float32)
    twice_ref[...] = jnp.zeros(twice_ref.shape, jnp.float32)
    twice_ref[:256, :channels] = result
    twice_ref[256:, channels:] = result
    samples_ref[...] = nn(sample_ref[...], twice_ref[...].astype(jnp.bfloat16)).astype(jnp.bfloat16)


def call(kernel, shapes, operands, scratch, scalars=0, fetch=(), limit=32):
    smem, vmem, hbm = (
        pl.BlockSpec(memory_space=space) for space in (pltpu.SMEM, pltpu.VMEM, pltpu.HBM)
    )
    count = len(operands)
    scratch_shapes = [pltpu.VMEM(shape, kind) for shape, kind in scratch]
    scratch_shapes += [pltpu.VMEM(operands[i].shape, operands[i].dtype) for i in fetch]
    scratch_shapes.append(pltpu.SemaphoreType.DMA((max(len(fetch), 1),)))

    def fetching(*refs):
        given, rest, sems = list(refs[:count]), refs[count:-1], refs[-1]
        own, landed = rest[: len(rest) - len(fetch)], rest[len(rest) - len(fetch) :]
        copies = [
            pltpu.make_async_copy(given[place], target, sems.at[index])
            for index, (place, target) in enumerate(zip(fetch, landed))
        ]
        for copy in copies:
            copy.start()
        for place, target in zip(fetch, landed):
            given[place] = target
        for copy in copies:
            copy.wait()
        kernel(*given, *own)

    operands = [
        pltpu.with_memory_space_constraint(array, pltpu.HBM) if place in fetch else array
        for place, array in enumerate(operands)
    ]
    return pl.pallas_call(
        fetching,
        out_shape=tuple(jax.ShapeDtypeStruct(shape, jnp.bfloat16) for shape in shapes),
        in_specs=[
            smem if place < scalars else hbm if place in fetch else vmem for place in range(count)
        ],
        out_specs=(vmem,) * len(shapes),
        scratch_shapes=scratch_shapes,
        compiler_params=pltpu.CompilerParams(vmem_limit_bytes=limit * 1024 * 1024),
    )(*operands)


def coarse_kernel(edge_ref, gathered_ref, *refs):
    count = 6
    direct, operands = refs[:4], refs[4 : 4 + count]
    outputs, landed = refs[4 + count : 6 + count], refs[-count - 1 : -1]
    small = [
        pltpu.make_async_copy(source, target, refs[-1].at[index])
        for index, (source, target) in enumerate(zip(operands, landed))
    ]
    for copy in small:
        copy.start()
    coarse_body(
        edge_ref, gathered_ref, small, *direct, *landed, *outputs, *refs[6 + count : -count - 1]
    )


def coarse_body(
    edge_ref,
    gathered_ref,
    small,
    attended_ref,
    own_ref,
    samples_ref,
    fine_ref,
    depth_ref,
    to_fine_ref,
    square_ref,
    centre_ref,
    repeat_ref,
    compact_ref,
    fine_out_ref,
    coarse_out_ref,
    out_ref,
    expand_ref,
    shrink_ref,
    taps_ref,
    hidden_ref,
    conv_ref,
    down_ref,
    sems,
):
    spans = (
        (out_ref, 2 * BLOCK_ROWS, OUT_ROWS),
        (expand_ref, 0, BLOCK_ROWS),
        (shrink_ref, BLOCK_ROWS, BLOCK_ROWS),
        (taps_ref, 2 * BLOCK_ROWS + 32, TAP_ROWS),
    )
    copies = [
        pltpu.make_async_copy(gathered_ref.at[:, pl.ds(first, count)], target, sems.at[part])
        for part, (target, first, count) in enumerate(spans)
    ]
    for copy in copies:
        copy.start()
    for copy in small:
        copy.wait()
    width = own_ref.shape[1]
    query = lax.broadcasted_iota(jnp.int32, (QUERIES, 128), 0)
    column = query % RING
    outside = (
        ((query < RING) & (edge_ref[0] == 0))
        | ((query >= RING * (RING - 1)) & (edge_ref[1] == 0))
        | ((column == 0) & (edge_ref[2] == 0))
        | ((column == RING - 1) & (edge_ref[3] == 0))
    )
    inside = jnp.where(outside, 0.0, 1.0)[:, :1]
    conv_ref[8 * WIN :, :] = jnp.zeros((8, conv_ref.shape[1]), jnp.float32)
    mixed = own_ref[...].astype(jnp.float32)
    copies[0].wait()
    mixed += nn(attended_ref[...], out_ref[...].reshape(SHARDS * OUT_ROWS, width))
    middle = nn(square_ref[...], mixed.astype(jnp.bfloat16)).astype(jnp.bfloat16)
    normed_mid = norm_rows(middle.astype(jnp.float32))
    copies[1].wait()
    chunk = 512
    expand = expand_ref[...].reshape(SHARDS * BLOCK_ROWS, width)
    for first in range(0, SHARDS * BLOCK_ROWS, chunk):
        span = pl.ds(first, chunk)
        hidden = gelu(nt(normed_mid, expand[first : first + chunk])) * inside
        hidden_ref[:, span] = hidden.astype(jnp.bfloat16).astype(jnp.float32)
        for row in range(WIN):
            total = jnp.zeros((8, chunk), jnp.float32)
            for tap in range(9):
                down, side = divmod(tap, 3)
                window = hidden_ref[pl.ds((row + down) * RING + side, 8), span]
                total += depth_ref[tap : tap + 1, span] * window
            conv_ref[row * 8 : row * 8 + 8, span] = gelu(total)
    copies[2].wait()
    shrink = shrink_ref[...].reshape(SHARDS * BLOCK_ROWS, width)
    update = nn(conv_ref[...].astype(jnp.bfloat16), shrink)
    result = (nn(centre_ref[...], middle) + update).astype(jnp.bfloat16)
    spread = nn(repeat_ref[...], result).astype(jnp.bfloat16)
    upsampled = nt(spread, to_fine_ref[...])
    fine_out_ref[...] = jnp.maximum(
        fine_ref[...].astype(jnp.float32) + upsampled, 0.0
    ).astype(jnp.bfloat16)
    copies[3].wait()
    samples = samples_ref[...]
    for shard in range(SHARDS):
        four = nt(taps_ref[shard], samples[: 4 * 64])
        fifth = nt(taps_ref[shard][4 * HEAD_ROWS :], samples[4 * 64 :])
        total = fifth[8:]
        for block in range(4):
            rows = slice(8 + block * HEAD_ROWS, 8 + (block + 1) * HEAD_ROWS)
            total += four[rows, block * 64 : (block + 1) * 64]
        down_ref[shard * 39 : shard * 39 + HEAD_ROWS, :64] = total
    downsampled = down_ref[...].T[:CELLS, :width].astype(jnp.bfloat16).astype(jnp.float32)
    coarse_out_ref[...] = jnp.maximum(
        nn(compact_ref[...], result) + downsampled, 0.0
    ).astype(jnp.bfloat16)


def coarse_stream(gathered, edges, attended, own, depth, samples, fine_res, to_fine):
    width = own.shape[1]
    fine_cells, fine_ch = fine_res.shape
    fixed = (gathered, depth, to_fine, *cell_tables())
    gathered, *fixed = (pltpu.with_memory_space_constraint(array, pltpu.HBM) for array in fixed)
    operands = (attended, own, samples, fine_res, *fixed)
    smem, vmem, hbm = (
        pl.BlockSpec(memory_space=space) for space in (pltpu.SMEM, pltpu.VMEM, pltpu.HBM)
    )
    return pl.pallas_call(
        coarse_kernel,
        out_shape=(
            jax.ShapeDtypeStruct((fine_cells, fine_ch), jnp.bfloat16),
            jax.ShapeDtypeStruct((CELLS, width), jnp.bfloat16),
        ),
        in_specs=[smem, hbm] + [vmem] * 4 + [hbm] * (len(operands) - 4),
        out_specs=(vmem, vmem),
        scratch_shapes=[
            pltpu.VMEM((SHARDS, OUT_ROWS, width), jnp.bfloat16),
            pltpu.VMEM((SHARDS, BLOCK_ROWS, width), jnp.bfloat16),
            pltpu.VMEM((SHARDS, BLOCK_ROWS, width), jnp.bfloat16),
            pltpu.VMEM((SHARDS, TAP_ROWS, width), jnp.bfloat16),
            pltpu.VMEM((QUERIES, SHARDS * BLOCK_ROWS), jnp.float32),
            pltpu.VMEM((64, SHARDS * BLOCK_ROWS), jnp.float32),
            pltpu.VMEM((SHARDS * HEAD_ROWS, 128), jnp.float32),
            pltpu.SemaphoreType.DMA((4,)),
            *(pltpu.VMEM(operand.shape, operand.dtype) for operand in operands[4:]),
            pltpu.SemaphoreType.DMA((len(operands) - 4,)),
        ],
        compiler_params=pltpu.CompilerParams(vmem_limit_bytes=40 * 1024 * 1024),
    )(edges, gathered, *operands)


def exchange(onward, back, axis):
    up = [(i, i + 1) for i in range(lax.axis_size(axis) - 1)]
    down = [(j, i) for i, j in up]
    return lax.ppermute(onward, axis, up), lax.ppermute(back, axis, down)


def local(
    fine_in,
    coarse_in,
    inproj_fine,
    outproj_fine,
    expand_fine,
    depth_fine,
    shrink_fine,
    inproj_coarse,
    outproj_coarse,
    expand_coarse,
    depth_coarse,
    shrink_coarse,
    to_fine,
    to_coarse,
):
    fine_ch, fine_cells = fine_in.shape[2:]
    coarse_ch, coarse_cells = coarse_in.shape[2:]
    gathered = lax.all_gather(pack(outproj_coarse, expand_coarse, shrink_coarse, to_coarse), "rows")
    strip = lax.all_gather(coarse_in.reshape(coarse_ch, coarse_cells).T, "rows")
    fine = fine_in.reshape(fine_ch, fine_cells).T
    place = (lax.axis_index("rows"), lax.axis_index("cols"))
    edges = jnp.stack(
        [
            place[0] > 0,
            place[0] < lax.axis_size("rows") - 1,
            place[1] > 0,
            place[1] < lax.axis_size("cols") - 1,
        ]
    ).astype(jnp.int32)
    middle, going_down, going_up = call(
        fine_attention_kernel,
        (fine.shape, (32, fine_ch), (16, fine_ch)),
        (fine, inproj_fine, outproj_fine, window_table()),
        (),
        fetch=(0, 1, 2, 3),
    )
    above, below = exchange(going_down, going_up, "rows")
    spread, column = strip_tables()
    blocks, own, columns = call(
        strip_kernel,
        ((SHARDS, STRIP, HEAD_ROWS), (STRIP, coarse_ch), (32, coarse_ch)),
        (edges, place[0].reshape(1).astype(jnp.int32), strip, inproj_coarse, spread, column),
        (
            ((SHARDS, TILE, coarse_ch), jnp.float32),
            ((3, SHARDS, TILE, 39), jnp.float32),
            ((SHARDS, TILE, TILE), jnp.float32),
            ((SHARDS + 2, TILE, HEAD_ROWS), jnp.float32),
            ((3 * TILE, coarse_ch), jnp.float32),
        ),
        scalars=2,
        fetch=(3, 4, 5),
    )
    blocks = lax.all_to_all(blocks, "rows", 0, 0, tiled=True)
    going_right, going_left = call(
        columns_kernel,
        ((64, coarse_ch), (64, coarse_ch)),
        (above, below, middle, columns, *border_tables()),
        (((248, fine_ch), jnp.float32),),
        fetch=(4, 5),
    )
    left, right = exchange(going_right, going_left, "cols")
    edge = (SHARDS, 16, HEAD_ROWS)
    near = exchange(*call(edge_columns_kernel, (edge, edge), (blocks, column), (), fetch=(1,)), "cols")
    hidden_count = expand_fine.shape[0]
    fine_res, samples = call(
        field_kernel,
        (fine.shape, (5 * 64, 2 * fine_ch)),
        (
            edges,
            above,
            below,
            left,
            right,
            middle,
            expand_fine.T,
            depth_fine,
            shrink_fine,
            *field_tables(),
        ),
        (
            ((320, fine_ch), jnp.float32),
            ((FIELD_ROWS, hidden_count), jnp.float32),
            ((256, hidden_count), jnp.bfloat16),
            ((512, 2 * fine_ch), jnp.float32),
        ),
        scalars=1,
        fetch=tuple(range(6, 13)),
    )
    (attended,) = call(
        attended_kernel,
        ((QUERIES, SHARDS * OUT_ROWS),),
        (blocks, *near),
        (((SHARDS, QUERIES, HEAD_ROWS), jnp.bfloat16),),
    )
    depth = jnp.pad(depth_coarse.reshape(9, SHARDS, -1), ((0, 0), (0, 0), (0, 4)))
    fine_out, coarse_out = coarse_stream(
        gathered,
        edges,
        attended,
        jnp.concatenate([own, left[48:], right[48:]]),
        depth.reshape(9, -1),
        samples,
        fine_res,
        to_fine,
    )
    return (fine_out.T.reshape(fine_in.shape), coarse_out.T.reshape(coarse_in.shape))


def solution(mesh):
    return jax.shard_map(
        local,
        mesh=mesh,
        in_specs=(
            P("rows", "cols", None, None),
            P("rows", "cols", None, None),
            P(),
            P(),
            P(),
            P(),
            P(),
            P(None, "rows", None),
            P(None, "rows"),
            P("rows", None),
            P(),
            P(None, "rows"),
            P(),
            P(None, "rows", None),
        ),
        out_specs=(P("rows", "cols", None, None), P("rows", "cols", None, None)),
        check_vma=False,
    )
```

```python
import math

import jax
import jax.numpy as jnp
from jax import lax
import numpy as np
from jax.experimental import pallas as pl
from jax.experimental.pallas import tpu as pltpu
from jax.sharding import PartitionSpec as P

HEADS_FINE = 8
WIN = 7


EPSILON = 1e-05


CELLS = WIN * WIN
RING = WIN + 2
HEAD_ROWS = 40
BLOCK_ROWS = 4 * HEAD_ROWS
OUT_ROWS = 48
TAP_ROWS = 192
HALF = HEAD_ROWS // 2
SHARD_ROWS = 544
SHARDS = 16
TILE = 56
STRIP = 64
QUERIES = 96
SIDE = 2 * WIN
FIELD = SIDE + 3
FIELD_ROWS = 304
TOP, BOTTOM, LEFT, RIGHT = 200, 232, 248, 288


def pack_kernel(outproj_ref, expand_ref, shrink_ref, taps_ref, packed_ref, rows_ref):
    rows_ref[...] = jnp.zeros(rows_ref.shape, jnp.float32)
    half = taps_ref.shape[2]
    for first, piece in ((0, expand_ref), (BLOCK_ROWS, shrink_ref), (2 * BLOCK_ROWS, outproj_ref)):
        rows_ref[first : first + piece.shape[0], :] = piece[...].astype(jnp.float32)
    first = 2 * BLOCK_ROWS + HEAD_ROWS
    for tap in range(8):
        start = first + tap // 2 * HEAD_ROWS
        lanes = slice(tap % 2 * half, (tap % 2 + 1) * half)
        rows_ref[start : start + 39, lanes] = taps_ref[tap].astype(jnp.float32)
    start = first + 4 * HEAD_ROWS
    ninth = taps_ref[8].astype(jnp.float32)
    rows_ref[start : start + HALF, :half] = ninth[:HALF]
    rows_ref[start : start + 19, half:] = ninth[HALF:]
    packed_ref[...] = rows_ref[...].astype(jnp.bfloat16)


def strip_tables():
    spread = np.zeros((STRIP, 3 * TILE), np.float32)
    columns = np.zeros((32, STRIP), np.float32)
    for row in range(RING):
        for col in range(WIN):
            spread[row * WIN + col, (row + 6) // WIN * TILE + (row + 6) % WIN * WIN + col] = 1
        columns[row, row * WIN + WIN - 1] = 1
        columns[16 + row, row * WIN] = 1
    return tuple(jnp.asarray(t).astype(jnp.bfloat16) for t in (spread, columns))


def window_table():
    cells = np.arange(SIDE * SIDE)
    window = cells // SIDE // WIN * 2 + cells % SIDE // WIN
    return jnp.asarray(np.where(window[:, None] == window[None], 0.0, -1e30).astype(np.float32))


def border_tables():
    right = np.zeros((40, 248), np.float32)
    left = np.zeros((32, 248), np.float32)

    def source(row, col):
        if row < 0:
            return TOP + (row + 2) * SIDE + col
        return row * SIDE + col if row < SIDE else BOTTOM + col

    for row in range(FIELD):
        for col in range(2):
            right[row * 2 + col, source(row - 2, SIDE - 2 + col)] = 1
        left[row, source(row - 2, 0)] = 1
    return jnp.asarray(right).astype(jnp.bfloat16), jnp.asarray(left).astype(jnp.bfloat16)


def field_tables():
    gather = np.zeros((FIELD_ROWS, 320), np.float32)
    inner = np.zeros((256, FIELD_ROWS), np.float32)
    for row in range(FIELD):
        for col in range(FIELD):
            if col < 2:
                source = LEFT + row * 2 + col
            elif col == FIELD - 1:
                source = RIGHT + row
            elif row < 2:
                source = TOP + row * SIDE + col - 2
            elif row == FIELD - 1:
                source = BOTTOM + col - 2
            else:
                source = (row - 2) * SIDE + col - 2
            gather[row * FIELD + col, source] = 1
    for row in range(15):
        for col in range(15):
            inner[row * 16 + col, (row + 1) * FIELD + col + 1] = 1
    tile = np.zeros((SIDE * SIDE, 256), np.float32)
    for row in range(SIDE):
        for col in range(SIDE):
            tile[row * SIDE + col, (row + 1) * 16 + col + 1] = 1
    sample = np.zeros((6 * 64, 512), np.float32)
    for cell in range(CELLS):
        row, col = divmod(cell, WIN)
        for tap in range(9):
            source = (2 * row + tap // 3) * 16 + 2 * col + tap % 3
            sample[tap // 2 * 64 + cell, tap % 2 * 256 + source] = 1
        sample[5 * 64 + cell, 256 + source] = 1
    return tuple(jnp.asarray(t).astype(jnp.bfloat16) for t in (gather, inner, tile, sample))


def cell_tables():
    side = 2 * WIN
    square = np.zeros((QUERIES, QUERIES), np.float32)
    for row in range(RING):
        for col in range(WIN):
            square[row * RING + col + 1, row * WIN + col] = 1
        square[row * RING, STRIP + row] = 1
        square[row * RING + RING - 1, STRIP + 16 + row] = 1
    centre = np.zeros((64, QUERIES), np.float32)
    repeat = np.zeros((side * side, 64), np.float32)
    compact = np.zeros((CELLS, 64), np.float32)
    for cell in range(CELLS):
        row, col = divmod(cell, WIN)
        centre[row * 8 + col, (row + 1) * RING + col + 1] = 1
        compact[cell, row * 8 + col] = 1
    for cell in range(side * side):
        row, col = divmod(cell, side)
        repeat[cell, row // 2 * 8 + col // 2] = 1
    return tuple(jnp.asarray(t).astype(jnp.bfloat16) for t in (square, centre, repeat, compact))


def gelu(values):
    return values * (lax.erf(values * math.sqrt(0.5)) + 1.0) * 0.5


def norm_rows(values):
    center = jnp.mean(values, axis=1, keepdims=True)
    away = values - center
    spread = jnp.mean(away * away, axis=1, keepdims=True)
    return (away * lax.rsqrt(spread + EPSILON)).astype(jnp.bfloat16)


def nn(left, right):
    return lax.dot_general(
        left, right, (((1,), (0,)), ((), ())), preferred_element_type=jnp.float32
    )


def nt(left, right):
    return lax.dot_general(
        left, right, (((1,), (1,)), ((), ())), preferred_element_type=jnp.float32
    )


def fine_attention_kernel(
    fine_ref, inproj_ref, outproj_ref, mask_ref, middle_ref, down_ref, up_ref
):
    cells, channels = fine_ref.shape
    fine = fine_ref[...].astype(jnp.float32)
    normed = norm_rows(fine)
    queries, keys, values = (nt(normed, inproj_ref[i]).astype(jnp.bfloat16) for i in range(3))
    channel = lax.broadcasted_iota(jnp.int32, (cells, channels), 1)
    mask = mask_ref[...]
    nothing = jnp.zeros((cells, channels), jnp.bfloat16)
    attended = jnp.zeros((cells, channels), jnp.float32)
    for head in range(HEADS_FINE):
        mine = (channel >= head * 39) & (channel < (head + 1) * 39)
        chosen = jnp.where(mine, queries, nothing)
        scores = nt(chosen, keys) * (1.0 / math.sqrt(39)) + mask
        exponent = jnp.exp(scores - jnp.max(scores, axis=1, keepdims=True))
        total = jnp.sum(exponent, axis=1, keepdims=True)
        chance = (exponent * (1.0 / total)).astype(jnp.bfloat16)
        attended += nn(chance, jnp.where(mine, values, nothing))
    middle = fine + nt(attended.astype(jnp.bfloat16), outproj_ref[...])
    middle_ref[...] = middle.astype(jnp.bfloat16)
    for target, first, count in ((down_ref, cells - 2 * SIDE, 2 * SIDE), (up_ref, 0, SIDE)):
        target[...] = jnp.zeros(target.shape, jnp.bfloat16)
        target[:count, :] = middle_ref[first : first + count, :]


def columns_kernel(
    above_ref, below_ref, middle_ref, columns_ref, blocks_ref, right_ref, left_ref, column_ref,
    to_right_ref, to_left_ref, flat_ref, field_ref,
):
    cells, channels = middle_ref.shape
    field_ref[...] = jnp.zeros(field_ref.shape, jnp.float32)
    field_ref[:cells, :] = middle_ref[...].astype(jnp.float32)
    field_ref[TOP : TOP + 2 * SIDE, :] = above_ref[: 2 * SIDE, :].astype(jnp.float32)
    field_ref[BOTTOM : BOTTOM + SIDE, :] = below_ref[:SIDE, :].astype(jnp.float32)
    field = field_ref[...].astype(jnp.bfloat16)
    width = columns_ref.shape[1]
    channel = lax.broadcasted_iota(jnp.int32, (HEAD_ROWS, SHARDS * OUT_ROWS), 0)
    lane = lax.broadcasted_iota(jnp.int32, (HEAD_ROWS, SHARDS * OUT_ROWS), 1)
    flat = jnp.zeros(flat_ref.shape, jnp.float32)
    for head in range(SHARDS):
        move = jnp.where(lane == channel + head * OUT_ROWS, 1.0, 0.0).astype(jnp.bfloat16)
        flat += nn(blocks_ref[head], move)
    flat = flat.astype(jnp.bfloat16)
    flat_ref[...] = flat
    edges = nn(column_ref[...], flat).astype(jnp.bfloat16)
    for index, (target, table) in enumerate(((to_right_ref, right_ref), (to_left_ref, left_ref))):
        target[...] = jnp.zeros(target.shape, jnp.bfloat16)
        count = table.shape[0]
        rows = slice(16 * index, 16 * index + 16)
        target[:count, :channels] = nn(table[...], field).astype(jnp.bfloat16)
        target[48:64, :width] = columns_ref[rows, :]
        target[64:, :] = edges[rows]


def strip_kernel(
    edge_ref,
    place_ref,
    strip_ref,
    weights_ref,
    spread_ref,
    column_ref,
    blocks_ref,
    own_ref,
    columns_ref,
    normed_ref,
    proj_ref,
    scores_ref,
    attended_ref,
    images_ref,
):
    tiles, cells, width = strip_ref.shape
    normed_ref[...] = jnp.zeros(normed_ref.shape, jnp.float32)
    attended_ref[...] = jnp.zeros(attended_ref.shape, jnp.float32)
    images_ref[...] = jnp.zeros(images_ref.shape, jnp.float32)
    for tile in range(tiles):
        normed_ref[tile, :cells, :] = norm_rows(strip_ref[tile].astype(jnp.float32)).astype(
            jnp.float32
        )
    normed = normed_ref[...].astype(jnp.bfloat16).reshape(tiles * TILE, width)
    for part in range(3):
        proj_ref[part] = nt(normed, weights_ref[part]).reshape(tiles, TILE, -1)
    for tile in range(tiles):
        queries, keys = (proj_ref[part, tile].astype(jnp.bfloat16) for part in range(2))
        scores_ref[tile] = nt(queries, keys)
    key = lax.broadcasted_iota(jnp.int32, (tiles * TILE, TILE), 1)
    scores = scores_ref[...].reshape(tiles * TILE, TILE) * (1.0 / math.sqrt(39))
    scores += jnp.where(key < cells, 0.0, -1e30)
    exponent = jnp.exp(scores - jnp.max(scores, axis=1, keepdims=True))
    total = jnp.sum(exponent, axis=1, keepdims=True)
    scores_ref[...] = (exponent * (1.0 / total)).reshape(tiles, TILE, TILE)
    for tile in range(tiles):
        values = proj_ref[2, tile].astype(jnp.bfloat16)
        attended_ref[tile + 1, :, :39] = nn(scores_ref[tile].astype(jnp.bfloat16), values)
    spread = spread_ref[...]
    for tile in range(tiles):
        near = attended_ref[tile : tile + 3].astype(jnp.bfloat16).reshape(3 * TILE, HEAD_ROWS)
        blocks_ref[tile] = nn(spread, near).astype(jnp.bfloat16)
    place = place_ref[0]
    before = jnp.maximum(place - 1, 0)
    after = jnp.minimum(place + 1, tiles - 1)
    for index, (tile, there) in enumerate(
        ((before, edge_ref[0]), (place, 1), (after, edge_ref[1]))
    ):
        image = strip_ref[tile].astype(jnp.float32)
        images_ref[index * TILE : index * TILE + cells, :] = jnp.where(there == 1, image, 0.0)
    own = nn(spread, images_ref[...].astype(jnp.bfloat16)).astype(jnp.bfloat16)
    own_ref[...] = own
    columns_ref[...] = nn(column_ref[...], own).astype(jnp.bfloat16)


def field_kernel(
    edge_ref,
    above_ref,
    below_ref,
    left_ref,
    right_ref,
    middle_ref,
    expand_ref,
    depth_ref,
    shrink_ref,
    gather_ref,
    inner_ref,
    cell_ref,
    sample_ref,
    fine_ref,
    samples_ref,
    pieces_ref,
    hidden_ref,
    conv_ref,
    twice_ref,
):
    cells, channels = middle_ref.shape
    pieces_ref[...] = jnp.zeros(pieces_ref.shape, jnp.float32)
    pieces_ref[:cells, :] = middle_ref[...].astype(jnp.float32)
    for piece, start, first, count in (
        (above_ref, 0, TOP, 2 * SIDE),
        (below_ref, 0, BOTTOM, SIDE),
        (left_ref, 0, LEFT, 2 * FIELD),
        (right_ref, 0, RIGHT, FIELD),
    ):
        pieces_ref[first : first + count, :] = piece[start : start + count, :channels].astype(
            jnp.float32
        )
    field = nn(gather_ref[...], pieces_ref[...].astype(jnp.bfloat16))
    normed_mid = norm_rows(field)
    row = lax.broadcasted_iota(jnp.int32, (FIELD_ROWS, 128), 0)
    column = row % FIELD
    outside = (
        ((row < 2 * FIELD) & (edge_ref[0] == 0))
        | ((row >= FIELD * (FIELD - 1)) & (edge_ref[1] == 0))
        | ((column < 2) & (edge_ref[2] == 0))
        | ((column == FIELD - 1) & (edge_ref[3] == 0))
    )
    inside = jnp.where(outside, 0.0, 1.0)[:, :1]
    hidden_count = hidden_ref.shape[1]
    conv_ref[15 * 16 :, :] = jnp.zeros((16, hidden_count), jnp.bfloat16)
    for first in range(0, hidden_count, 384):
        span = pl.ds(first, min(384, hidden_count - first))
        hidden = gelu(nn(normed_mid, expand_ref[:, span])) * inside
        hidden_ref[:, span] = hidden.astype(jnp.bfloat16).astype(jnp.float32)
        for out in range(15):
            total = jnp.zeros((16, span.size), jnp.float32)
            for tap in range(9):
                down, side = divmod(tap, 3)
                window = hidden_ref[pl.ds((out + down) * FIELD + side, 16), span]
                total += depth_ref[tap : tap + 1, span] * window
            conv_ref[out * 16 : out * 16 + 16, span] = gelu(total).astype(jnp.bfloat16)
    update = nt(conv_ref[...], shrink_ref[...])
    result = nn(inner_ref[...], field.astype(jnp.bfloat16)) + update
    row = lax.broadcasted_iota(jnp.int32, (256, 128), 0)
    outside = ((row < 16) & (edge_ref[0] == 0)) | ((row % 16 == 0) & (edge_ref[2] == 0))
    result = result * jnp.where(outside, 0.0, 1.0)[:, :1]
    rounded = result.astype(jnp.bfloat16)
    fine_ref[...] = nn(cell_ref[...], rounded).astype(jnp.bfloat16)
    result = rounded.astype(jnp.float32)
    twice_ref[...] = jnp.zeros(twice_ref.shape, jnp.float32)
    twice_ref[:256, :channels] = result
    twice_ref[256:, channels:] = result
    samples_ref[...] = nn(sample_ref[...], twice_ref[...].astype(jnp.bfloat16)).astype(jnp.bfloat16)


def call(kernel, shapes, operands, scratch, scalars=0, fetch=(), limit=32):
    smem, vmem, hbm = (
        pl.BlockSpec(memory_space=space) for space in (pltpu.SMEM, pltpu.VMEM, pltpu.HBM)
    )
    count = len(operands)
    scratch_shapes = [pltpu.VMEM(shape, kind) for shape, kind in scratch]
    scratch_shapes += [pltpu.VMEM(operands[i].shape, operands[i].dtype) for i in fetch]
    scratch_shapes.append(pltpu.SemaphoreType.DMA((max(len(fetch), 1),)))

    def fetching(*refs):
        given, rest, sems = list(refs[:count]), refs[count:-1], refs[-1]
        own, landed = rest[: len(rest) - len(fetch)], rest[len(rest) - len(fetch) :]
        copies = [
            pltpu.make_async_copy(given[place], target, sems.at[index])
            for index, (place, target) in enumerate(zip(fetch, landed))
        ]
        for copy in copies:
            copy.start()
        for place, target in zip(fetch, landed):
            given[place] = target
        for copy in copies:
            copy.wait()
        kernel(*given, *own)

    operands = [
        pltpu.with_memory_space_constraint(array, pltpu.HBM) if place in fetch else array
        for place, array in enumerate(operands)
    ]
    return pl.pallas_call(
        fetching,
        out_shape=tuple(jax.ShapeDtypeStruct(shape, jnp.bfloat16) for shape in shapes),
        in_specs=[
            smem if place < scalars else hbm if place in fetch else vmem for place in range(count)
        ],
        out_specs=(vmem,) * len(shapes),
        scratch_shapes=scratch_shapes,
        compiler_params=pltpu.CompilerParams(vmem_limit_bytes=limit * 1024 * 1024),
    )(*operands)


def coarse_kernel(edge_ref, gathered_ref, *refs):
    count = 6
    direct, operands = refs[:6], refs[6 : 6 + count]
    outputs, landed = refs[6 + count : 8 + count], refs[-count - 1 : -1]
    small = [
        pltpu.make_async_copy(source, target, refs[-1].at[index])
        for index, (source, target) in enumerate(zip(operands, landed))
    ]
    for copy in small:
        copy.start()
    coarse_body(
        edge_ref, gathered_ref, small, *direct, *landed, *outputs, *refs[8 + count : -count - 1]
    )


def coarse_body(
    edge_ref,
    gathered_ref,
    small,
    flat_ref,
    own_ref,
    left_ref,
    right_ref,
    samples_ref,
    fine_ref,
    depth_ref,
    to_fine_ref,
    square_ref,
    centre_ref,
    repeat_ref,
    compact_ref,
    fine_out_ref,
    coarse_out_ref,
    out_ref,
    expand_ref,
    shrink_ref,
    taps_ref,
    hidden_ref,
    conv_ref,
    down_ref,
    mixed_ref,
    sems,
):
    spans = (
        (out_ref, 2 * BLOCK_ROWS, OUT_ROWS),
        (expand_ref, 0, BLOCK_ROWS),
        (shrink_ref, BLOCK_ROWS, BLOCK_ROWS),
        (taps_ref, 2 * BLOCK_ROWS + 32, TAP_ROWS),
    )
    order = (0, 1, 3, 2)
    copies = [
        pltpu.make_async_copy(gathered_ref.at[:, pl.ds(first, count)], target, sems.at[part])
        for part, (target, first, count) in enumerate(spans)
    ]
    for part in order:
        copies[part].start()
    for copy in small:
        copy.wait()
    width = own_ref.shape[1]
    query = lax.broadcasted_iota(jnp.int32, (QUERIES, 128), 0)
    column = query % RING
    outside = (
        ((query < RING) & (edge_ref[0] == 0))
        | ((query >= RING * (RING - 1)) & (edge_ref[1] == 0))
        | ((column == 0) & (edge_ref[2] == 0))
        | ((column == RING - 1) & (edge_ref[3] == 0))
    )
    inside = jnp.where(outside, 0.0, 1.0)[:, :1]
    conv_ref[8 * WIN :, :] = jnp.zeros((8, conv_ref.shape[1]), jnp.float32)
    pieces = ((slice(0, STRIP), flat_ref[...], own_ref[...]),) + tuple(
        (slice(first, first + 16), side[64:80, :], side[48:64, :width])
        for first, side in ((STRIP, left_ref), (STRIP + 16, right_ref))
    )
    copies[0].wait()
    out = out_ref[...].reshape(SHARDS * OUT_ROWS, width)
    for rows, attended, image in pieces:
        mixed_ref[rows, :] = image.astype(jnp.float32) + nn(attended, out)
    mixed = mixed_ref[...]
    middle = nn(square_ref[...], mixed.astype(jnp.bfloat16)).astype(jnp.bfloat16)
    normed_mid = norm_rows(middle.astype(jnp.float32))
    copies[1].wait()
    chunk = 512
    expand = expand_ref[...].reshape(SHARDS * BLOCK_ROWS, width)

    def downsample(shard):
        samples = samples_ref[...]
        four = nt(taps_ref[shard], samples[: 4 * 64])
        ninth = nt(taps_ref[shard][4 * HEAD_ROWS :], samples[4 * 64 :])
        total = four[8 : 8 + HEAD_ROWS, :64]
        for block in range(1, 4):
            rows = slice(8 + block * HEAD_ROWS, 8 + (block + 1) * HEAD_ROWS)
            total += four[rows, block * 64 : (block + 1) * 64]
        first = shard * 39
        down_ref[first : first + HEAD_ROWS, :64] = total
        down_ref[first : first + HALF, :64] += ninth[8 : 8 + HALF, :64]
        down_ref[first + HALF : first + HEAD_ROWS, :64] += ninth[8 : 8 + HALF, 64:]

    shares = {2: range(0, 6), 3: range(6, 11), 4: range(11, SHARDS)}
    for first in range(0, SHARDS * BLOCK_ROWS, chunk):
        if first == 2 * chunk:
            copies[3].wait()
        for shard in shares.get(first // chunk, ()):
            downsample(shard)
        span = pl.ds(first, chunk)
        hidden = gelu(nt(normed_mid, expand[first : first + chunk])) * inside
        hidden_ref[:, span] = hidden.astype(jnp.bfloat16).astype(jnp.float32)
        for row in range(WIN):
            total = jnp.zeros((8, chunk), jnp.float32)
            for tap in range(9):
                down, side = divmod(tap, 3)
                window = hidden_ref[pl.ds((row + down) * RING + side, 8), span]
                total += depth_ref[tap : tap + 1, span] * window
            conv_ref[row * 8 : row * 8 + 8, span] = gelu(total)
    copies[2].wait()
    shrink = shrink_ref[...].reshape(SHARDS * BLOCK_ROWS, width)
    update = nn(conv_ref[...].astype(jnp.bfloat16), shrink)
    result = (nn(centre_ref[...], middle) + update).astype(jnp.bfloat16)
    spread = nn(repeat_ref[...], result).astype(jnp.bfloat16)
    upsampled = nt(spread, to_fine_ref[...])
    fine_out_ref[...] = jnp.maximum(
        fine_ref[...].astype(jnp.float32) + upsampled, 0.0
    ).astype(jnp.bfloat16)
    downsampled = down_ref[...].T[:CELLS, :width].astype(jnp.bfloat16).astype(jnp.float32)
    coarse_out_ref[...] = jnp.maximum(
        nn(compact_ref[...], result) + downsampled, 0.0
    ).astype(jnp.bfloat16)


def coarse_stream(gathered, edges, flat, own, left, right, depth, samples, fine_res, to_fine):
    width = own.shape[1]
    fine_cells, fine_ch = fine_res.shape
    fixed = (gathered, depth, to_fine, *cell_tables())
    gathered, *fixed = (pltpu.with_memory_space_constraint(array, pltpu.HBM) for array in fixed)
    operands = (flat, own, left, right, samples, fine_res, *fixed)
    smem, vmem, hbm = (
        pl.BlockSpec(memory_space=space) for space in (pltpu.SMEM, pltpu.VMEM, pltpu.HBM)
    )
    return pl.pallas_call(
        coarse_kernel,
        out_shape=(
            jax.ShapeDtypeStruct((fine_cells, fine_ch), jnp.bfloat16),
            jax.ShapeDtypeStruct((CELLS, width), jnp.bfloat16),
        ),
        in_specs=[smem, hbm] + [vmem] * 6 + [hbm] * (len(operands) - 6),
        out_specs=(vmem, vmem),
        scratch_shapes=[
            pltpu.VMEM((SHARDS, OUT_ROWS, width), jnp.bfloat16),
            pltpu.VMEM((SHARDS, BLOCK_ROWS, width), jnp.bfloat16),
            pltpu.VMEM((SHARDS, BLOCK_ROWS, width), jnp.bfloat16),
            pltpu.VMEM((SHARDS, TAP_ROWS, width), jnp.bfloat16),
            pltpu.VMEM((QUERIES, SHARDS * BLOCK_ROWS), jnp.float32),
            pltpu.VMEM((64, SHARDS * BLOCK_ROWS), jnp.float32),
            pltpu.VMEM((SHARDS * HEAD_ROWS, 128), jnp.float32),
            pltpu.VMEM((QUERIES, width), jnp.float32),
            pltpu.SemaphoreType.DMA((4,)),
            *(pltpu.VMEM(operand.shape, operand.dtype) for operand in operands[6:]),
            pltpu.SemaphoreType.DMA((len(operands) - 6,)),
        ],
        compiler_params=pltpu.CompilerParams(vmem_limit_bytes=40 * 1024 * 1024),
    )(edges, gathered, *operands)


def exchange(onward, back, axis):
    up = [(i, i + 1) for i in range(lax.axis_size(axis) - 1)]
    down = [(j, i) for i, j in up]
    return lax.ppermute(onward, axis, up), lax.ppermute(back, axis, down)


def local(
    fine_in,
    coarse_in,
    inproj_fine,
    outproj_fine,
    expand_fine,
    depth_fine,
    shrink_fine,
    inproj_coarse,
    outproj_coarse,
    expand_coarse,
    depth_coarse,
    shrink_coarse,
    to_fine,
    to_coarse,
):
    fine_ch, fine_cells = fine_in.shape[2:]
    coarse_ch, coarse_cells = coarse_in.shape[2:]
    packed = (SHARD_ROWS, coarse_ch)
    (mine,) = call(
        pack_kernel,
        (packed,),
        (outproj_coarse.T, expand_coarse, shrink_coarse.T, to_coarse),
        ((packed, jnp.float32),),
        fetch=(0, 1, 2, 3),
    )
    gathered = lax.all_gather(mine, "rows")
    strip = lax.all_gather(coarse_in.reshape(coarse_ch, coarse_cells).T, "rows")
    fine = fine_in.reshape(fine_ch, fine_cells).T
    place = (lax.axis_index("rows"), lax.axis_index("cols"))
    edges = jnp.stack(
        [
            place[0] > 0,
            place[0] < lax.axis_size("rows") - 1,
            place[1] > 0,
            place[1] < lax.axis_size("cols") - 1,
        ]
    ).astype(jnp.int32)
    middle, going_down, going_up = call(
        fine_attention_kernel,
        (fine.shape, (32, fine_ch), (16, fine_ch)),
        (fine, inproj_fine, outproj_fine, window_table()),
        (),
        fetch=(0, 1, 2, 3),
    )
    above, below = exchange(going_down, going_up, "rows")
    spread, column = strip_tables()
    blocks, own, columns = call(
        strip_kernel,
        ((SHARDS, STRIP, HEAD_ROWS), (STRIP, coarse_ch), (32, coarse_ch)),
        (edges, place[0].reshape(1).astype(jnp.int32), strip, inproj_coarse, spread, column),
        (
            ((SHARDS, TILE, coarse_ch), jnp.float32),
            ((3, SHARDS, TILE, 39), jnp.float32),
            ((SHARDS, TILE, TILE), jnp.float32),
            ((SHARDS + 2, TILE, HEAD_ROWS), jnp.float32),
            ((3 * TILE, coarse_ch), jnp.float32),
        ),
        scalars=2,
        fetch=(3, 4, 5),
    )
    blocks = lax.all_to_all(blocks, "rows", 0, 0, tiled=True)
    message = (80, SHARDS * OUT_ROWS)
    going_right, going_left, flat = call(
        columns_kernel,
        (message, message, (STRIP, SHARDS * OUT_ROWS)),
        (above, below, middle, columns, blocks, *border_tables(), column),
        (((248, fine_ch), jnp.float32),),
        fetch=(5, 6, 7),
    )
    left, right = exchange(going_right, going_left, "cols")
    hidden_count = expand_fine.shape[0]
    fine_res, samples = call(
        field_kernel,
        (fine.shape, (6 * 64, 2 * fine_ch)),
        (
            edges,
            above,
            below,
            left,
            right,
            middle,
            expand_fine.T,
            depth_fine,
            shrink_fine,
            *field_tables(),
        ),
        (
            ((320, fine_ch), jnp.float32),
            ((FIELD_ROWS, hidden_count), jnp.float32),
            ((256, hidden_count), jnp.bfloat16),
            ((512, 2 * fine_ch), jnp.float32),
        ),
        scalars=1,
        fetch=tuple(range(6, 13)),
    )
    depth = jnp.pad(depth_coarse.reshape(9, SHARDS, -1), ((0, 0), (0, 0), (0, 4)))
    fine_out, coarse_out = coarse_stream(
        gathered,
        edges,
        flat,
        own,
        left,
        right,
        depth.reshape(9, -1),
        samples,
        fine_res,
        to_fine,
    )
    return (fine_out.T.reshape(fine_in.shape), coarse_out.T.reshape(coarse_in.shape))


def solution(mesh):
    return jax.shard_map(
        local,
        mesh=mesh,
        in_specs=(
            P("rows", "cols", None, None),
            P("rows", "cols", None, None),
            P(),
            P(),
            P(),
            P(),
            P(),
            P(None, "rows", None),
            P(None, "rows"),
            P("rows", None),
            P(),
            P(None, "rows"),
            P(),
            P(None, "rows", None),
        ),
        out_specs=(P("rows", "cols", None, None), P("rows", "cols", None, None)),
        check_vma=False,
    )
```

```python
import math

import jax
import jax.numpy as jnp
from jax import lax
import numpy as np
from jax.experimental import pallas as pl
from jax.experimental.pallas import tpu as pltpu
from jax.sharding import PartitionSpec as P

HEADS_FINE = 8
WIN = 7


EPSILON = 1e-05


CELLS = WIN * WIN
RING = WIN + 2
HEAD_ROWS = 40
BLOCK_ROWS = 4 * HEAD_ROWS
OUT_ROWS = 48
TAP_ROWS = 192
HALF = HEAD_ROWS // 2
SHARD_ROWS = 544
SHARDS = 16
GROUPS = 4
PER_GROUP = SHARDS // GROUPS
TILE = 56
STRIP = 64
QUERIES = 96
SIDE = 2 * WIN
FIELD = SIDE + 3
FIELD_ROWS = 304
TOP, BOTTOM, LEFT, RIGHT = 200, 232, 248, 288


def pack_kernel(outproj_ref, expand_ref, shrink_ref, taps_ref, packed_ref, rows_ref):
    rows_ref[...] = jnp.zeros(rows_ref.shape, jnp.float32)
    half = taps_ref.shape[2]
    for first, piece in ((0, expand_ref), (BLOCK_ROWS, shrink_ref), (2 * BLOCK_ROWS, outproj_ref)):
        rows_ref[first : first + piece.shape[0], :] = piece[...].astype(jnp.float32)
    first = 2 * BLOCK_ROWS + HEAD_ROWS
    for tap in range(8):
        start = first + tap // 2 * HEAD_ROWS
        lanes = slice(tap % 2 * half, (tap % 2 + 1) * half)
        rows_ref[start : start + 39, lanes] = taps_ref[tap].astype(jnp.float32)
    start = first + 4 * HEAD_ROWS
    ninth = taps_ref[8].astype(jnp.float32)
    rows_ref[start : start + HALF, :half] = ninth[:HALF]
    rows_ref[start : start + 19, half:] = ninth[HALF:]
    packed_ref[...] = rows_ref[...].astype(jnp.bfloat16)


def strip_tables():
    spread = np.zeros((STRIP, 3 * TILE), np.float32)
    columns = np.zeros((32, STRIP), np.float32)
    for row in range(RING):
        for col in range(WIN):
            spread[row * WIN + col, (row + 6) // WIN * TILE + (row + 6) % WIN * WIN + col] = 1
        columns[row, row * WIN + WIN - 1] = 1
        columns[16 + row, row * WIN] = 1
    return tuple(jnp.asarray(t).astype(jnp.bfloat16) for t in (spread, columns))


def window_table():
    cells = np.arange(SIDE * SIDE)
    window = cells // SIDE // WIN * 2 + cells % SIDE // WIN
    return jnp.asarray(np.where(window[:, None] == window[None], 0.0, -1e30).astype(np.float32))


def border_tables():
    right = np.zeros((40, 248), np.float32)
    left = np.zeros((32, 248), np.float32)

    def source(row, col):
        if row < 0:
            return TOP + (row + 2) * SIDE + col
        return row * SIDE + col if row < SIDE else BOTTOM + col

    for row in range(FIELD):
        for col in range(2):
            right[row * 2 + col, source(row - 2, SIDE - 2 + col)] = 1
        left[row, source(row - 2, 0)] = 1
    return jnp.asarray(right).astype(jnp.bfloat16), jnp.asarray(left).astype(jnp.bfloat16)


def field_tables():
    gather = np.zeros((FIELD_ROWS, 320), np.float32)
    inner = np.zeros((256, FIELD_ROWS), np.float32)
    for row in range(FIELD):
        for col in range(FIELD):
            if col < 2:
                source = LEFT + row * 2 + col
            elif col == FIELD - 1:
                source = RIGHT + row
            elif row < 2:
                source = TOP + row * SIDE + col - 2
            elif row == FIELD - 1:
                source = BOTTOM + col - 2
            else:
                source = (row - 2) * SIDE + col - 2
            gather[row * FIELD + col, source] = 1
    for row in range(15):
        for col in range(15):
            inner[row * 16 + col, (row + 1) * FIELD + col + 1] = 1
    tile = np.zeros((SIDE * SIDE, 256), np.float32)
    for row in range(SIDE):
        for col in range(SIDE):
            tile[row * SIDE + col, (row + 1) * 16 + col + 1] = 1
    sample = np.zeros((6 * 64, 512), np.float32)
    for cell in range(CELLS):
        row, col = divmod(cell, WIN)
        for tap in range(9):
            source = (2 * row + tap // 3) * 16 + 2 * col + tap % 3
            sample[tap // 2 * 64 + cell, tap % 2 * 256 + source] = 1
        sample[5 * 64 + cell, 256 + source] = 1
    return tuple(jnp.asarray(t).astype(jnp.bfloat16) for t in (gather, inner, tile, sample))


def cell_tables():
    side = 2 * WIN
    square = np.zeros((QUERIES, QUERIES), np.float32)
    for row in range(RING):
        for col in range(WIN):
            square[row * RING + col + 1, row * WIN + col] = 1
        square[row * RING, STRIP + row] = 1
        square[row * RING + RING - 1, STRIP + 16 + row] = 1
    centre = np.zeros((64, QUERIES), np.float32)
    repeat = np.zeros((side * side, 64), np.float32)
    compact = np.zeros((CELLS, 64), np.float32)
    for cell in range(CELLS):
        row, col = divmod(cell, WIN)
        centre[row * 8 + col, (row + 1) * RING + col + 1] = 1
        compact[cell, row * 8 + col] = 1
    for cell in range(side * side):
        row, col = divmod(cell, side)
        repeat[cell, row // 2 * 8 + col // 2] = 1
    return tuple(jnp.asarray(t).astype(jnp.bfloat16) for t in (square, centre, repeat, compact))


def gelu(values):
    return values * (lax.erf(values * math.sqrt(0.5)) + 1.0) * 0.5


def norm_rows(values):
    center = jnp.mean(values, axis=1, keepdims=True)
    away = values - center
    spread = jnp.mean(away * away, axis=1, keepdims=True)
    return (away * lax.rsqrt(spread + EPSILON)).astype(jnp.bfloat16)


def nn(left, right):
    return lax.dot_general(
        left, right, (((1,), (0,)), ((), ())), preferred_element_type=jnp.float32
    )


def nt(left, right):
    return lax.dot_general(
        left, right, (((1,), (1,)), ((), ())), preferred_element_type=jnp.float32
    )


def fine_attention_kernel(
    fine_ref, inproj_ref, outproj_ref, mask_ref, middle_ref, down_ref, up_ref
):
    cells, channels = fine_ref.shape
    fine = fine_ref[...].astype(jnp.float32)
    normed = norm_rows(fine)
    queries, keys, values = (nt(normed, inproj_ref[i]).astype(jnp.bfloat16) for i in range(3))
    channel = lax.broadcasted_iota(jnp.int32, (cells, channels), 1)
    mask = mask_ref[...]
    nothing = jnp.zeros((cells, channels), jnp.bfloat16)
    attended = jnp.zeros((cells, channels), jnp.float32)
    for head in range(HEADS_FINE):
        mine = (channel >= head * 39) & (channel < (head + 1) * 39)
        chosen = jnp.where(mine, queries, nothing)
        scores = nt(chosen, keys) * (1.0 / math.sqrt(39)) + mask
        exponent = jnp.exp(scores - jnp.max(scores, axis=1, keepdims=True))
        total = jnp.sum(exponent, axis=1, keepdims=True)
        chance = (exponent * (1.0 / total)).astype(jnp.bfloat16)
        attended += nn(chance, jnp.where(mine, values, nothing))
    middle = fine + nt(attended.astype(jnp.bfloat16), outproj_ref[...])
    middle_ref[...] = middle.astype(jnp.bfloat16)
    for target, first, count in ((down_ref, cells - 2 * SIDE, 2 * SIDE), (up_ref, 0, SIDE)):
        target[...] = jnp.zeros(target.shape, jnp.bfloat16)
        target[:count, :] = middle_ref[first : first + count, :]


def columns_kernel(
    above_ref, below_ref, middle_ref, columns_ref, blocks_ref, right_ref, left_ref, column_ref,
    to_right_ref, to_left_ref, flat_ref, field_ref,
):
    cells, channels = middle_ref.shape
    field_ref[...] = jnp.zeros(field_ref.shape, jnp.float32)
    field_ref[:cells, :] = middle_ref[...].astype(jnp.float32)
    field_ref[TOP : TOP + 2 * SIDE, :] = above_ref[: 2 * SIDE, :].astype(jnp.float32)
    field_ref[BOTTOM : BOTTOM + SIDE, :] = below_ref[:SIDE, :].astype(jnp.float32)
    field = field_ref[...].astype(jnp.bfloat16)
    width = columns_ref.shape[1]
    channel = lax.broadcasted_iota(jnp.int32, (HEAD_ROWS, SHARDS * OUT_ROWS), 0)
    lane = lax.broadcasted_iota(jnp.int32, (HEAD_ROWS, SHARDS * OUT_ROWS), 1)
    flat = jnp.zeros(flat_ref.shape, jnp.float32)
    for head in range(SHARDS):
        move = jnp.where(lane == channel + head * OUT_ROWS, 1.0, 0.0).astype(jnp.bfloat16)
        flat += nn(blocks_ref[head], move)
    flat = flat.astype(jnp.bfloat16)
    flat_ref[...] = flat
    edges = nn(column_ref[...], flat).astype(jnp.bfloat16)
    for index, (target, table) in enumerate(((to_right_ref, right_ref), (to_left_ref, left_ref))):
        target[...] = jnp.zeros(target.shape, jnp.bfloat16)
        count = table.shape[0]
        rows = slice(16 * index, 16 * index + 16)
        target[:count, :channels] = nn(table[...], field).astype(jnp.bfloat16)
        target[48:64, :width] = columns_ref[rows, :]
        target[64:, :] = edges[rows]


def strip_kernel(
    edge_ref,
    place_ref,
    strip_ref,
    weights_ref,
    spread_ref,
    column_ref,
    blocks_ref,
    own_ref,
    columns_ref,
    normed_ref,
    proj_ref,
    scores_ref,
    attended_ref,
    images_ref,
):
    tiles, cells, width = strip_ref.shape
    normed_ref[...] = jnp.zeros(normed_ref.shape, jnp.float32)
    attended_ref[...] = jnp.zeros(attended_ref.shape, jnp.float32)
    images_ref[...] = jnp.zeros(images_ref.shape, jnp.float32)
    for tile in range(tiles):
        normed_ref[tile, :cells, :] = norm_rows(strip_ref[tile].astype(jnp.float32)).astype(
            jnp.float32
        )
    normed = normed_ref[...].astype(jnp.bfloat16).reshape(tiles * TILE, width)
    for part in range(3):
        proj_ref[part] = nt(normed, weights_ref[part]).reshape(tiles, TILE, -1)
    for tile in range(tiles):
        queries, keys = (proj_ref[part, tile].astype(jnp.bfloat16) for part in range(2))
        scores_ref[tile] = nt(queries, keys)
    key = lax.broadcasted_iota(jnp.int32, (tiles * TILE, TILE), 1)
    scores = scores_ref[...].reshape(tiles * TILE, TILE) * (1.0 / math.sqrt(39))
    scores += jnp.where(key < cells, 0.0, -1e30)
    exponent = jnp.exp(scores - jnp.max(scores, axis=1, keepdims=True))
    total = jnp.sum(exponent, axis=1, keepdims=True)
    scores_ref[...] = (exponent * (1.0 / total)).reshape(tiles, TILE, TILE)
    for tile in range(tiles):
        values = proj_ref[2, tile].astype(jnp.bfloat16)
        attended_ref[tile + 1, :, :39] = nn(scores_ref[tile].astype(jnp.bfloat16), values)
    spread = spread_ref[...]
    for tile in range(tiles):
        near = attended_ref[tile : tile + 3].astype(jnp.bfloat16).reshape(3 * TILE, HEAD_ROWS)
        blocks_ref[tile] = nn(spread, near).astype(jnp.bfloat16)
    place = place_ref[0]
    before = jnp.maximum(place - 1, 0)
    after = jnp.minimum(place + 1, tiles - 1)
    for index, (tile, there) in enumerate(
        ((before, edge_ref[0]), (place, 1), (after, edge_ref[1]))
    ):
        image = strip_ref[tile].astype(jnp.float32)
        images_ref[index * TILE : index * TILE + cells, :] = jnp.where(there == 1, image, 0.0)
    own = nn(spread, images_ref[...].astype(jnp.bfloat16)).astype(jnp.bfloat16)
    own_ref[...] = own
    columns_ref[...] = nn(column_ref[...], own).astype(jnp.bfloat16)


def field_kernel(
    edge_ref,
    above_ref,
    below_ref,
    left_ref,
    right_ref,
    middle_ref,
    expand_ref,
    depth_ref,
    shrink_ref,
    gather_ref,
    inner_ref,
    cell_ref,
    sample_ref,
    fine_ref,
    samples_ref,
    pieces_ref,
    hidden_ref,
    conv_ref,
    twice_ref,
):
    cells, channels = middle_ref.shape
    pieces_ref[...] = jnp.zeros(pieces_ref.shape, jnp.float32)
    pieces_ref[:cells, :] = middle_ref[...].astype(jnp.float32)
    for piece, start, first, count in (
        (above_ref, 0, TOP, 2 * SIDE),
        (below_ref, 0, BOTTOM, SIDE),
        (left_ref, 0, LEFT, 2 * FIELD),
        (right_ref, 0, RIGHT, FIELD),
    ):
        pieces_ref[first : first + count, :] = piece[start : start + count, :channels].astype(
            jnp.float32
        )
    field = nn(gather_ref[...], pieces_ref[...].astype(jnp.bfloat16))
    normed_mid = norm_rows(field)
    row = lax.broadcasted_iota(jnp.int32, (FIELD_ROWS, 128), 0)
    column = row % FIELD
    outside = (
        ((row < 2 * FIELD) & (edge_ref[0] == 0))
        | ((row >= FIELD * (FIELD - 1)) & (edge_ref[1] == 0))
        | ((column < 2) & (edge_ref[2] == 0))
        | ((column == FIELD - 1) & (edge_ref[3] == 0))
    )
    inside = jnp.where(outside, 0.0, 1.0)[:, :1]
    hidden_count = hidden_ref.shape[1]
    conv_ref[15 * 16 :, :] = jnp.zeros((16, hidden_count), jnp.bfloat16)
    for first in range(0, hidden_count, 384):
        span = pl.ds(first, min(384, hidden_count - first))
        hidden = gelu(nn(normed_mid, expand_ref[:, span])) * inside
        hidden_ref[:, span] = hidden.astype(jnp.bfloat16).astype(jnp.float32)
        for out in range(15):
            total = jnp.zeros((16, span.size), jnp.float32)
            for tap in range(9):
                down, side = divmod(tap, 3)
                window = hidden_ref[pl.ds((out + down) * FIELD + side, 16), span]
                total += depth_ref[tap : tap + 1, span] * window
            conv_ref[out * 16 : out * 16 + 16, span] = gelu(total).astype(jnp.bfloat16)
    update = nt(conv_ref[...], shrink_ref[...])
    result = nn(inner_ref[...], field.astype(jnp.bfloat16)) + update
    row = lax.broadcasted_iota(jnp.int32, (256, 128), 0)
    outside = ((row < 16) & (edge_ref[0] == 0)) | ((row % 16 == 0) & (edge_ref[2] == 0))
    result = result * jnp.where(outside, 0.0, 1.0)[:, :1]
    rounded = result.astype(jnp.bfloat16)
    fine_ref[...] = nn(cell_ref[...], rounded).astype(jnp.bfloat16)
    result = rounded.astype(jnp.float32)
    twice_ref[...] = jnp.zeros(twice_ref.shape, jnp.float32)
    twice_ref[:256, :channels] = result
    twice_ref[256:, channels:] = result
    samples_ref[...] = nn(sample_ref[...], twice_ref[...].astype(jnp.bfloat16)).astype(jnp.bfloat16)


def call(kernel, shapes, operands, scratch, scalars=0, fetch=(), limit=32):
    smem, vmem, hbm = (
        pl.BlockSpec(memory_space=space) for space in (pltpu.SMEM, pltpu.VMEM, pltpu.HBM)
    )
    count = len(operands)
    scratch_shapes = [pltpu.VMEM(shape, kind) for shape, kind in scratch]
    scratch_shapes += [pltpu.VMEM(operands[i].shape, operands[i].dtype) for i in fetch]
    scratch_shapes.append(pltpu.SemaphoreType.DMA((max(len(fetch), 1),)))

    def fetching(*refs):
        given, rest, sems = list(refs[:count]), refs[count:-1], refs[-1]
        own, landed = rest[: len(rest) - len(fetch)], rest[len(rest) - len(fetch) :]
        copies = [
            pltpu.make_async_copy(given[place], target, sems.at[index])
            for index, (place, target) in enumerate(zip(fetch, landed))
        ]
        for copy in copies:
            copy.start()
        for place, target in zip(fetch, landed):
            given[place] = target
        for copy in copies:
            copy.wait()
        kernel(*given, *own)

    operands = [
        pltpu.with_memory_space_constraint(array, pltpu.HBM) if place in fetch else array
        for place, array in enumerate(operands)
    ]
    return pl.pallas_call(
        fetching,
        out_shape=tuple(jax.ShapeDtypeStruct(shape, jnp.bfloat16) for shape in shapes),
        in_specs=[
            smem if place < scalars else hbm if place in fetch else vmem for place in range(count)
        ],
        out_specs=(vmem,) * len(shapes),
        scratch_shapes=scratch_shapes,
        compiler_params=pltpu.CompilerParams(vmem_limit_bytes=limit * 1024 * 1024),
    )(*operands)


def coarse_kernel(edge_ref, gathered_ref, *refs):
    count = 6
    direct, operands = refs[:6], refs[6 : 6 + count]
    outputs, landed = refs[6 + count : 8 + count], refs[-count - 1 : -1]
    small = [
        pltpu.make_async_copy(source, target, refs[-1].at[index])
        for index, (source, target) in enumerate(zip(operands, landed))
    ]
    for copy in small:
        copy.start()
    coarse_body(
        edge_ref, gathered_ref, small, *direct, *landed, *outputs, *refs[8 + count : -count - 1]
    )


def coarse_body(
    edge_ref,
    gathered_ref,
    small,
    flat_ref,
    own_ref,
    left_ref,
    right_ref,
    samples_ref,
    fine_ref,
    depth_ref,
    to_fine_ref,
    square_ref,
    centre_ref,
    repeat_ref,
    compact_ref,
    fine_out_ref,
    coarse_out_ref,
    out_ref,
    expand_ref,
    shrink_ref,
    taps_ref,
    hidden_ref,
    conv_ref,
    down_ref,
    mixed_ref,
    sems,
):
    spans = (
        (expand_ref, 0, BLOCK_ROWS),
        (shrink_ref, BLOCK_ROWS, BLOCK_ROWS),
        (taps_ref, 2 * BLOCK_ROWS + 32, TAP_ROWS),
    )
    out_copy = pltpu.make_async_copy(
        gathered_ref.at[:, pl.ds(2 * BLOCK_ROWS, OUT_ROWS)], out_ref, sems.at[3, 0]
    )
    out_copy.start()
    copies = []
    for group in range(GROUPS):
        shards = pl.ds(group * PER_GROUP, PER_GROUP)
        copies.append(
            [
                pltpu.make_async_copy(
                    gathered_ref.at[shards, pl.ds(first, count)],
                    target.at[shards],
                    sems.at[part, group],
                )
                for part, (target, first, count) in enumerate(spans)
            ]
        )
        for copy in copies[-1]:
            copy.start()
    for copy in small:
        copy.wait()
    width = own_ref.shape[1]
    query = lax.broadcasted_iota(jnp.int32, (QUERIES, 128), 0)
    column = query % RING
    outside = (
        ((query < RING) & (edge_ref[0] == 0))
        | ((query >= RING * (RING - 1)) & (edge_ref[1] == 0))
        | ((column == 0) & (edge_ref[2] == 0))
        | ((column == RING - 1) & (edge_ref[3] == 0))
    )
    inside = jnp.where(outside, 0.0, 1.0)[:, :1]
    conv_ref[8 * WIN :, :] = jnp.zeros((8, conv_ref.shape[1]), jnp.float32)
    pieces = ((slice(0, STRIP), flat_ref[...], own_ref[...]),) + tuple(
        (slice(first, first + 16), side[64:80, :], side[48:64, :width])
        for first, side in ((STRIP, left_ref), (STRIP + 16, right_ref))
    )
    out_copy.wait()
    out = out_ref[...].reshape(SHARDS * OUT_ROWS, width)
    for rows, attended, image in pieces:
        mixed_ref[rows, :] = image.astype(jnp.float32) + nn(attended, out)
    mixed = mixed_ref[...]
    middle = nn(square_ref[...], mixed.astype(jnp.bfloat16)).astype(jnp.bfloat16)
    normed_mid = norm_rows(middle.astype(jnp.float32))
    chunk = PER_GROUP * BLOCK_ROWS

    def group_of(ref, group):
        return ref[group * PER_GROUP : (group + 1) * PER_GROUP].reshape(chunk, width)

    def downsample(shard):
        samples = samples_ref[...]
        four = nt(taps_ref[shard], samples[: 4 * 64])
        ninth = nt(taps_ref[shard][4 * HEAD_ROWS :], samples[4 * 64 :])
        total = four[8 : 8 + HEAD_ROWS, :64]
        for block in range(1, 4):
            rows = slice(8 + block * HEAD_ROWS, 8 + (block + 1) * HEAD_ROWS)
            total += four[rows, block * 64 : (block + 1) * 64]
        first = shard * 39
        down_ref[first : first + HEAD_ROWS, :64] = total
        down_ref[first : first + HALF, :64] += ninth[8 : 8 + HALF, :64]
        down_ref[first + HALF : first + HEAD_ROWS, :64] += ninth[8 : 8 + HALF, 64:]

    copies[0][0].wait()
    ahead = nt(normed_mid, group_of(expand_ref, 0))
    update = jnp.zeros((64, width), jnp.float32)
    for group in range(GROUPS):
        raw = ahead
        copies[group][1].wait()
        copies[group][2].wait()
        if group + 1 < GROUPS:
            copies[group + 1][0].wait()
            ahead = nt(normed_mid, group_of(expand_ref, group + 1))
        span = pl.ds(group * chunk, chunk)
        hidden_ref[:, span] = (gelu(raw) * inside).astype(jnp.bfloat16).astype(jnp.float32)
        for row in range(WIN):
            total = jnp.zeros((8, chunk), jnp.float32)
            for tap in range(9):
                down, side = divmod(tap, 3)
                window = hidden_ref[pl.ds((row + down) * RING + side, 8), span]
                total += depth_ref[tap : tap + 1, span] * window
            conv_ref[row * 8 : row * 8 + 8, span] = gelu(total)
        for shard in range(group * PER_GROUP, (group + 1) * PER_GROUP):
            downsample(shard)
        update += nn(conv_ref[:, span].astype(jnp.bfloat16), group_of(shrink_ref, group))
    result = (nn(centre_ref[...], middle) + update).astype(jnp.bfloat16)
    spread = nn(repeat_ref[...], result).astype(jnp.bfloat16)
    upsampled = nt(spread, to_fine_ref[...])
    fine_out_ref[...] = jnp.maximum(
        fine_ref[...].astype(jnp.float32) + upsampled, 0.0
    ).astype(jnp.bfloat16)
    downsampled = down_ref[...].T[:CELLS, :width].astype(jnp.bfloat16).astype(jnp.float32)
    coarse_out_ref[...] = jnp.maximum(
        nn(compact_ref[...], result) + downsampled, 0.0
    ).astype(jnp.bfloat16)


def coarse_stream(gathered, edges, flat, own, left, right, depth, samples, fine_res, to_fine):
    width = own.shape[1]
    fine_cells, fine_ch = fine_res.shape
    fixed = (gathered, depth, to_fine, *cell_tables())
    gathered, *fixed = (pltpu.with_memory_space_constraint(array, pltpu.HBM) for array in fixed)
    operands = (flat, own, left, right, samples, fine_res, *fixed)
    smem, vmem, hbm = (
        pl.BlockSpec(memory_space=space) for space in (pltpu.SMEM, pltpu.VMEM, pltpu.HBM)
    )
    return pl.pallas_call(
        coarse_kernel,
        out_shape=(
            jax.ShapeDtypeStruct((fine_cells, fine_ch), jnp.bfloat16),
            jax.ShapeDtypeStruct((CELLS, width), jnp.bfloat16),
        ),
        in_specs=[smem, hbm] + [vmem] * 6 + [hbm] * (len(operands) - 6),
        out_specs=(vmem, vmem),
        scratch_shapes=[
            pltpu.VMEM((SHARDS, OUT_ROWS, width), jnp.bfloat16),
            pltpu.VMEM((SHARDS, BLOCK_ROWS, width), jnp.bfloat16),
            pltpu.VMEM((SHARDS, BLOCK_ROWS, width), jnp.bfloat16),
            pltpu.VMEM((SHARDS, TAP_ROWS, width), jnp.bfloat16),
            pltpu.VMEM((QUERIES, SHARDS * BLOCK_ROWS), jnp.float32),
            pltpu.VMEM((64, SHARDS * BLOCK_ROWS), jnp.float32),
            pltpu.VMEM((SHARDS * HEAD_ROWS, 128), jnp.float32),
            pltpu.VMEM((QUERIES, width), jnp.float32),
            pltpu.SemaphoreType.DMA((4, GROUPS)),
            *(pltpu.VMEM(operand.shape, operand.dtype) for operand in operands[6:]),
            pltpu.SemaphoreType.DMA((len(operands) - 6,)),
        ],
        compiler_params=pltpu.CompilerParams(vmem_limit_bytes=40 * 1024 * 1024),
    )(edges, gathered, *operands)


def exchange(onward, back, axis):
    up = [(i, i + 1) for i in range(lax.axis_size(axis) - 1)]
    down = [(j, i) for i, j in up]
    return lax.ppermute(onward, axis, up), lax.ppermute(back, axis, down)


def local(
    fine_in,
    coarse_in,
    inproj_fine,
    outproj_fine,
    expand_fine,
    depth_fine,
    shrink_fine,
    inproj_coarse,
    outproj_coarse,
    expand_coarse,
    depth_coarse,
    shrink_coarse,
    to_fine,
    to_coarse,
):
    fine_ch, fine_cells = fine_in.shape[2:]
    coarse_ch, coarse_cells = coarse_in.shape[2:]
    packed = (SHARD_ROWS, coarse_ch)
    (mine,) = call(
        pack_kernel,
        (packed,),
        (outproj_coarse.T, expand_coarse, shrink_coarse.T, to_coarse),
        ((packed, jnp.float32),),
        fetch=(0, 1, 2, 3),
    )
    gathered = lax.all_gather(mine, "rows")
    strip = lax.all_gather(coarse_in.reshape(coarse_ch, coarse_cells).T, "rows")
    fine = fine_in.reshape(fine_ch, fine_cells).T
    place = (lax.axis_index("rows"), lax.axis_index("cols"))
    edges = jnp.stack(
        [
            place[0] > 0,
            place[0] < lax.axis_size("rows") - 1,
            place[1] > 0,
            place[1] < lax.axis_size("cols") - 1,
        ]
    ).astype(jnp.int32)
    middle, going_down, going_up = call(
        fine_attention_kernel,
        (fine.shape, (32, fine_ch), (16, fine_ch)),
        (fine, inproj_fine, outproj_fine, window_table()),
        (),
        fetch=(0, 1, 2, 3),
    )
    above, below = exchange(going_down, going_up, "rows")
    spread, column = strip_tables()
    blocks, own, columns = call(
        strip_kernel,
        ((SHARDS, STRIP, HEAD_ROWS), (STRIP, coarse_ch), (32, coarse_ch)),
        (edges, place[0].reshape(1).astype(jnp.int32), strip, inproj_coarse, spread, column),
        (
            ((SHARDS, TILE, coarse_ch), jnp.float32),
            ((3, SHARDS, TILE, 39), jnp.float32),
            ((SHARDS, TILE, TILE), jnp.float32),
            ((SHARDS + 2, TILE, HEAD_ROWS), jnp.float32),
            ((3 * TILE, coarse_ch), jnp.float32),
        ),
        scalars=2,
        fetch=(3, 4, 5),
    )
    blocks = lax.all_to_all(blocks, "rows", 0, 0, tiled=True)
    message = (80, SHARDS * OUT_ROWS)
    going_right, going_left, flat = call(
        columns_kernel,
        (message, message, (STRIP, SHARDS * OUT_ROWS)),
        (above, below, middle, columns, blocks, *border_tables(), column),
        (((248, fine_ch), jnp.float32),),
        fetch=(5, 6, 7),
    )
    left, right = exchange(going_right, going_left, "cols")
    hidden_count = expand_fine.shape[0]
    fine_res, samples = call(
        field_kernel,
        (fine.shape, (6 * 64, 2 * fine_ch)),
        (
            edges,
            above,
            below,
            left,
            right,
            middle,
            expand_fine.T,
            depth_fine,
            shrink_fine,
            *field_tables(),
        ),
        (
            ((320, fine_ch), jnp.float32),
            ((FIELD_ROWS, hidden_count), jnp.float32),
            ((256, hidden_count), jnp.bfloat16),
            ((512, 2 * fine_ch), jnp.float32),
        ),
        scalars=1,
        fetch=tuple(range(6, 13)),
    )
    depth = jnp.pad(depth_coarse.reshape(9, SHARDS, -1), ((0, 0), (0, 0), (0, 4)))
    fine_out, coarse_out = coarse_stream(
        gathered,
        edges,
        flat,
        own,
        left,
        right,
        depth.reshape(9, -1),
        samples,
        fine_res,
        to_fine,
    )
    return (fine_out.T.reshape(fine_in.shape), coarse_out.T.reshape(coarse_in.shape))


def solution(mesh):
    return jax.shard_map(
        local,
        mesh=mesh,
        in_specs=(
            P("rows", "cols", None, None),
            P("rows", "cols", None, None),
            P(),
            P(),
            P(),
            P(),
            P(),
            P(None, "rows", None),
            P(None, "rows"),
            P("rows", None),
            P(),
            P(None, "rows"),
            P(),
            P(None, "rows", None),
        ),
        out_specs=(P("rows", "cols", None, None), P("rows", "cols", None, None)),
        check_vma=False,
    )
```

```python
import math

import jax
import jax.numpy as jnp
from jax import lax
import numpy as np
from jax.experimental import pallas as pl
from jax.experimental.pallas import tpu as pltpu
from jax.sharding import PartitionSpec as P

HEADS_FINE = 8
WIN = 7


EPSILON = 1e-05


CELLS = WIN * WIN
RING = WIN + 2
HEAD_ROWS = 40
BLOCK_ROWS = 4 * HEAD_ROWS
OUT_ROWS = 48
TAP_ROWS = 192
HALF = HEAD_ROWS // 2
SHARD_ROWS = 544
SHARDS = 16
TILE = 56
STRIP = 64
QUERIES = 96
SIDE = 2 * WIN
FIELD = SIDE + 3
FIELD_ROWS = 304
TOP, BOTTOM, LEFT, RIGHT = 200, 232, 248, 288


def pack_kernel(outproj_ref, expand_ref, shrink_ref, taps_ref, packed_ref, rows_ref):
    rows_ref[...] = jnp.zeros(rows_ref.shape, jnp.float32)
    half = taps_ref.shape[2]
    for first, piece in ((0, expand_ref), (BLOCK_ROWS, shrink_ref), (2 * BLOCK_ROWS, outproj_ref)):
        rows_ref[first : first + piece.shape[0], :] = piece[...].astype(jnp.float32)
    first = 2 * BLOCK_ROWS + HEAD_ROWS
    for tap in range(8):
        start = first + tap // 2 * HEAD_ROWS
        lanes = slice(tap % 2 * half, (tap % 2 + 1) * half)
        rows_ref[start : start + 39, lanes] = taps_ref[tap].astype(jnp.float32)
    start = first + 4 * HEAD_ROWS
    ninth = taps_ref[8].astype(jnp.float32)
    rows_ref[start : start + HALF, :half] = ninth[:HALF]
    rows_ref[start : start + 19, half:] = ninth[HALF:]
    packed_ref[...] = rows_ref[...].astype(jnp.bfloat16)


def strip_tables():
    spread = np.zeros((STRIP, 3 * TILE), np.float32)
    columns = np.zeros((32, STRIP), np.float32)
    for row in range(RING):
        for col in range(WIN):
            spread[row * WIN + col, (row + 6) // WIN * TILE + (row + 6) % WIN * WIN + col] = 1
        columns[row, row * WIN + WIN - 1] = 1
        columns[16 + row, row * WIN] = 1
    return tuple(jnp.asarray(t).astype(jnp.bfloat16) for t in (spread, columns))


def window_table():
    cells = np.arange(SIDE * SIDE)
    window = cells // SIDE // WIN * 2 + cells % SIDE // WIN
    return jnp.asarray(np.where(window[:, None] == window[None], 0.0, -1e30).astype(np.float32))


def border_tables():
    right = np.zeros((40, 248), np.float32)
    left = np.zeros((32, 248), np.float32)

    def source(row, col):
        if row < 0:
            return TOP + (row + 2) * SIDE + col
        return row * SIDE + col if row < SIDE else BOTTOM + col

    for row in range(FIELD):
        for col in range(2):
            right[row * 2 + col, source(row - 2, SIDE - 2 + col)] = 1
        left[row, source(row - 2, 0)] = 1
    return jnp.asarray(right).astype(jnp.bfloat16), jnp.asarray(left).astype(jnp.bfloat16)


def field_tables():
    gather = np.zeros((FIELD_ROWS, 320), np.float32)
    inner = np.zeros((256, FIELD_ROWS), np.float32)
    for row in range(FIELD):
        for col in range(FIELD):
            if col < 2:
                source = LEFT + row * 2 + col
            elif col == FIELD - 1:
                source = RIGHT + row
            elif row < 2:
                source = TOP + row * SIDE + col - 2
            elif row == FIELD - 1:
                source = BOTTOM + col - 2
            else:
                source = (row - 2) * SIDE + col - 2
            gather[row * FIELD + col, source] = 1
    for row in range(15):
        for col in range(15):
            inner[row * 16 + col, (row + 1) * FIELD + col + 1] = 1
    tile = np.zeros((SIDE * SIDE, 256), np.float32)
    for row in range(SIDE):
        for col in range(SIDE):
            tile[row * SIDE + col, (row + 1) * 16 + col + 1] = 1
    sample = np.zeros((6 * 64, 512), np.float32)
    for cell in range(CELLS):
        row, col = divmod(cell, WIN)
        for tap in range(9):
            source = (2 * row + tap // 3) * 16 + 2 * col + tap % 3
            sample[tap // 2 * 64 + cell, tap % 2 * 256 + source] = 1
        sample[5 * 64 + cell, 256 + source] = 1
    return tuple(jnp.asarray(t).astype(jnp.bfloat16) for t in (gather, inner, tile, sample))


def cell_tables():
    side = 2 * WIN
    square = np.zeros((QUERIES, QUERIES), np.float32)
    for row in range(RING):
        for col in range(WIN):
            square[row * RING + col + 1, row * WIN + col] = 1
        square[row * RING, STRIP + row] = 1
        square[row * RING + RING - 1, STRIP + 16 + row] = 1
    centre = np.zeros((64, QUERIES), np.float32)
    repeat = np.zeros((side * side, 64), np.float32)
    compact = np.zeros((CELLS, 64), np.float32)
    for cell in range(CELLS):
        row, col = divmod(cell, WIN)
        centre[row * 8 + col, (row + 1) * RING + col + 1] = 1
        compact[cell, row * 8 + col] = 1
    for cell in range(side * side):
        row, col = divmod(cell, side)
        repeat[cell, row // 2 * 8 + col // 2] = 1
    return tuple(jnp.asarray(t).astype(jnp.bfloat16) for t in (square, centre, repeat, compact))


def gelu(values):
    return values * (lax.erf(values * math.sqrt(0.5)) + 1.0) * 0.5


def norm_rows(values):
    center = jnp.mean(values, axis=1, keepdims=True)
    away = values - center
    spread = jnp.mean(away * away, axis=1, keepdims=True)
    return (away * lax.rsqrt(spread + EPSILON)).astype(jnp.bfloat16)


def nn(left, right):
    return lax.dot_general(
        left, right, (((1,), (0,)), ((), ())), preferred_element_type=jnp.float32
    )


def nt(left, right):
    return lax.dot_general(
        left, right, (((1,), (1,)), ((), ())), preferred_element_type=jnp.float32
    )


def fine_attention_kernel(
    fine_ref, inproj_ref, outproj_ref, mask_ref, middle_ref, down_ref, up_ref
):
    cells, channels = fine_ref.shape
    fine = fine_ref[...].astype(jnp.float32)
    normed = norm_rows(fine)
    queries, keys, values = (nt(normed, inproj_ref[i]).astype(jnp.bfloat16) for i in range(3))
    channel = lax.broadcasted_iota(jnp.int32, (cells, channels), 1)
    mask = mask_ref[...]
    nothing = jnp.zeros((cells, channels), jnp.bfloat16)
    attended = jnp.zeros((cells, channels), jnp.float32)
    for head in range(HEADS_FINE):
        mine = (channel >= head * 39) & (channel < (head + 1) * 39)
        chosen = jnp.where(mine, queries, nothing)
        scores = nt(chosen, keys) * (1.0 / math.sqrt(39)) + mask
        exponent = jnp.exp(scores - jnp.max(scores, axis=1, keepdims=True))
        total = jnp.sum(exponent, axis=1, keepdims=True)
        chance = (exponent * (1.0 / total)).astype(jnp.bfloat16)
        attended += nn(chance, jnp.where(mine, values, nothing))
    middle = fine + nt(attended.astype(jnp.bfloat16), outproj_ref[...])
    middle_ref[...] = middle.astype(jnp.bfloat16)
    for target, first, count in ((down_ref, cells - 2 * SIDE, 2 * SIDE), (up_ref, 0, SIDE)):
        target[...] = jnp.zeros(target.shape, jnp.bfloat16)
        target[:count, :] = middle_ref[first : first + count, :]


def columns_kernel(
    above_ref, below_ref, middle_ref, columns_ref, blocks_ref, right_ref, left_ref, column_ref,
    to_right_ref, to_left_ref, flat_ref, field_ref,
):
    cells, channels = middle_ref.shape
    field_ref[...] = jnp.zeros(field_ref.shape, jnp.float32)
    field_ref[:cells, :] = middle_ref[...].astype(jnp.float32)
    field_ref[TOP : TOP + 2 * SIDE, :] = above_ref[: 2 * SIDE, :].astype(jnp.float32)
    field_ref[BOTTOM : BOTTOM + SIDE, :] = below_ref[:SIDE, :].astype(jnp.float32)
    field = field_ref[...].astype(jnp.bfloat16)
    width = columns_ref.shape[1]
    channel = lax.broadcasted_iota(jnp.int32, (HEAD_ROWS, SHARDS * OUT_ROWS), 0)
    lane = lax.broadcasted_iota(jnp.int32, (HEAD_ROWS, SHARDS * OUT_ROWS), 1)
    flat = jnp.zeros(flat_ref.shape, jnp.float32)
    for head in range(SHARDS):
        move = jnp.where(lane == channel + head * OUT_ROWS, 1.0, 0.0).astype(jnp.bfloat16)
        flat += nn(blocks_ref[head], move)
    flat = flat.astype(jnp.bfloat16)
    flat_ref[...] = flat
    edges = nn(column_ref[...], flat).astype(jnp.bfloat16)
    for index, (target, table) in enumerate(((to_right_ref, right_ref), (to_left_ref, left_ref))):
        target[...] = jnp.zeros(target.shape, jnp.bfloat16)
        count = table.shape[0]
        rows = slice(16 * index, 16 * index + 16)
        target[:count, :channels] = nn(table[...], field).astype(jnp.bfloat16)
        target[48:64, :width] = columns_ref[rows, :]
        target[64:, :] = edges[rows]


def strip_kernel(
    edge_ref,
    place_ref,
    strip_ref,
    weights_ref,
    spread_ref,
    column_ref,
    blocks_ref,
    own_ref,
    columns_ref,
    normed_ref,
    proj_ref,
    scores_ref,
    attended_ref,
    images_ref,
):
    tiles, cells, width = strip_ref.shape
    normed_ref[...] = jnp.zeros(normed_ref.shape, jnp.float32)
    attended_ref[...] = jnp.zeros(attended_ref.shape, jnp.float32)
    images_ref[...] = jnp.zeros(images_ref.shape, jnp.float32)
    for tile in range(tiles):
        normed_ref[tile, :cells, :] = norm_rows(strip_ref[tile].astype(jnp.float32)).astype(
            jnp.float32
        )
    normed = normed_ref[...].astype(jnp.bfloat16).reshape(tiles * TILE, width)
    for part in range(3):
        proj_ref[part] = nt(normed, weights_ref[part]).reshape(tiles, TILE, -1)
    for tile in range(tiles):
        queries, keys = (proj_ref[part, tile].astype(jnp.bfloat16) for part in range(2))
        scores_ref[tile] = nt(queries, keys)
    key = lax.broadcasted_iota(jnp.int32, (tiles * TILE, TILE), 1)
    scores = scores_ref[...].reshape(tiles * TILE, TILE) * (1.0 / math.sqrt(39))
    scores += jnp.where(key < cells, 0.0, -1e30)
    exponent = jnp.exp(scores - jnp.max(scores, axis=1, keepdims=True))
    total = jnp.sum(exponent, axis=1, keepdims=True)
    scores_ref[...] = (exponent * (1.0 / total)).reshape(tiles, TILE, TILE)
    for tile in range(tiles):
        values = proj_ref[2, tile].astype(jnp.bfloat16)
        attended_ref[tile + 1, :, :39] = nn(scores_ref[tile].astype(jnp.bfloat16), values)
    spread = spread_ref[...]
    for tile in range(tiles):
        near = attended_ref[tile : tile + 3].astype(jnp.bfloat16).reshape(3 * TILE, HEAD_ROWS)
        blocks_ref[tile] = nn(spread, near).astype(jnp.bfloat16)
    place = place_ref[0]
    before = jnp.maximum(place - 1, 0)
    after = jnp.minimum(place + 1, tiles - 1)
    for index, (tile, there) in enumerate(
        ((before, edge_ref[0]), (place, 1), (after, edge_ref[1]))
    ):
        image = strip_ref[tile].astype(jnp.float32)
        images_ref[index * TILE : index * TILE + cells, :] = jnp.where(there == 1, image, 0.0)
    own = nn(spread, images_ref[...].astype(jnp.bfloat16)).astype(jnp.bfloat16)
    own_ref[...] = own
    columns_ref[...] = nn(column_ref[...], own).astype(jnp.bfloat16)


def field_kernel(
    edge_ref,
    above_ref,
    below_ref,
    left_ref,
    right_ref,
    middle_ref,
    expand_ref,
    depth_ref,
    shrink_ref,
    gather_ref,
    inner_ref,
    cell_ref,
    sample_ref,
    fine_ref,
    samples_ref,
    pieces_ref,
    hidden_ref,
    conv_ref,
    twice_ref,
):
    cells, channels = middle_ref.shape
    pieces_ref[...] = jnp.zeros(pieces_ref.shape, jnp.float32)
    pieces_ref[:cells, :] = middle_ref[...].astype(jnp.float32)
    for piece, start, first, count in (
        (above_ref, 0, TOP, 2 * SIDE),
        (below_ref, 0, BOTTOM, SIDE),
        (left_ref, 0, LEFT, 2 * FIELD),
        (right_ref, 0, RIGHT, FIELD),
    ):
        pieces_ref[first : first + count, :] = piece[start : start + count, :channels].astype(
            jnp.float32
        )
    field = nn(gather_ref[...], pieces_ref[...].astype(jnp.bfloat16))
    normed_mid = norm_rows(field)
    row = lax.broadcasted_iota(jnp.int32, (FIELD_ROWS, 128), 0)
    column = row % FIELD
    outside = (
        ((row < 2 * FIELD) & (edge_ref[0] == 0))
        | ((row >= FIELD * (FIELD - 1)) & (edge_ref[1] == 0))
        | ((column < 2) & (edge_ref[2] == 0))
        | ((column == FIELD - 1) & (edge_ref[3] == 0))
    )
    inside = jnp.where(outside, 0.0, 1.0)[:, :1]
    hidden_count = hidden_ref.shape[1]
    conv_ref[15 * 16 :, :] = jnp.zeros((16, hidden_count), jnp.bfloat16)
    for first in range(0, hidden_count, 384):
        span = pl.ds(first, min(384, hidden_count - first))
        hidden = gelu(nn(normed_mid, expand_ref[:, span])) * inside
        hidden_ref[:, span] = hidden.astype(jnp.bfloat16).astype(jnp.float32)
        for out in range(15):
            total = jnp.zeros((16, span.size), jnp.float32)
            for tap in range(9):
                down, side = divmod(tap, 3)
                window = hidden_ref[pl.ds((out + down) * FIELD + side, 16), span]
                total += depth_ref[tap : tap + 1, span] * window
            conv_ref[out * 16 : out * 16 + 16, span] = gelu(total).astype(jnp.bfloat16)
    update = nt(conv_ref[...], shrink_ref[...])
    result = nn(inner_ref[...], field.astype(jnp.bfloat16)) + update
    row = lax.broadcasted_iota(jnp.int32, (256, 128), 0)
    outside = ((row < 16) & (edge_ref[0] == 0)) | ((row % 16 == 0) & (edge_ref[2] == 0))
    result = result * jnp.where(outside, 0.0, 1.0)[:, :1]
    rounded = result.astype(jnp.bfloat16)
    fine_ref[...] = nn(cell_ref[...], rounded).astype(jnp.bfloat16)
    result = rounded.astype(jnp.float32)
    twice_ref[...] = jnp.zeros(twice_ref.shape, jnp.float32)
    twice_ref[:256, :channels] = result
    twice_ref[256:, channels:] = result
    samples_ref[...] = nn(sample_ref[...], twice_ref[...].astype(jnp.bfloat16)).astype(jnp.bfloat16)


def call(kernel, shapes, operands, scratch, scalars=0, fetch=(), limit=32):
    smem, vmem, hbm = (
        pl.BlockSpec(memory_space=space) for space in (pltpu.SMEM, pltpu.VMEM, pltpu.HBM)
    )
    count = len(operands)
    scratch_shapes = [pltpu.VMEM(shape, kind) for shape, kind in scratch]
    scratch_shapes += [pltpu.VMEM(operands[i].shape, operands[i].dtype) for i in fetch]
    scratch_shapes.append(pltpu.SemaphoreType.DMA((max(len(fetch), 1),)))

    def fetching(*refs):
        given, rest, sems = list(refs[:count]), refs[count:-1], refs[-1]
        own, landed = rest[: len(rest) - len(fetch)], rest[len(rest) - len(fetch) :]
        copies = [
            pltpu.make_async_copy(given[place], target, sems.at[index])
            for index, (place, target) in enumerate(zip(fetch, landed))
        ]
        for copy in copies:
            copy.start()
        for place, target in zip(fetch, landed):
            given[place] = target
        for copy in copies:
            copy.wait()
        kernel(*given, *own)

    operands = [
        pltpu.with_memory_space_constraint(array, pltpu.HBM) if place in fetch else array
        for place, array in enumerate(operands)
    ]
    return pl.pallas_call(
        fetching,
        out_shape=tuple(jax.ShapeDtypeStruct(shape, jnp.bfloat16) for shape in shapes),
        in_specs=[
            smem if place < scalars else hbm if place in fetch else vmem for place in range(count)
        ],
        out_specs=(vmem,) * len(shapes),
        scratch_shapes=scratch_shapes,
        compiler_params=pltpu.CompilerParams(vmem_limit_bytes=limit * 1024 * 1024),
    )(*operands)


def coarse_kernel(edge_ref, gathered_ref, *refs):
    count = 6
    direct, operands = refs[:6], refs[6 : 6 + count]
    outputs, landed = refs[6 + count : 8 + count], refs[-count - 1 : -1]
    small = [
        pltpu.make_async_copy(source, target, refs[-1].at[index])
        for index, (source, target) in enumerate(zip(operands, landed))
    ]
    for copy in small:
        copy.start()
    coarse_body(
        edge_ref, gathered_ref, small, *direct, *landed, *outputs, *refs[8 + count : -count - 1]
    )


def coarse_body(
    edge_ref,
    gathered_ref,
    small,
    flat_ref,
    own_ref,
    left_ref,
    right_ref,
    samples_ref,
    fine_ref,
    depth_ref,
    to_fine_ref,
    square_ref,
    centre_ref,
    repeat_ref,
    compact_ref,
    fine_out_ref,
    coarse_out_ref,
    out_ref,
    expand_ref,
    shrink_ref,
    taps_ref,
    hidden_ref,
    conv_ref,
    down_ref,
    mixed_ref,
    sems,
):
    spans = (
        (out_ref, 2 * BLOCK_ROWS, OUT_ROWS),
        (expand_ref, 0, BLOCK_ROWS),
        (shrink_ref, BLOCK_ROWS, BLOCK_ROWS),
        (taps_ref, 2 * BLOCK_ROWS + 32, TAP_ROWS),
    )
    order = (0, 1, 3, 2)
    copies = [
        pltpu.make_async_copy(gathered_ref.at[:, pl.ds(first, count)], target, sems.at[part])
        for part, (target, first, count) in enumerate(spans)
    ]
    for part in order:
        copies[part].start()
    for copy in small:
        copy.wait()
    width = own_ref.shape[1]
    query = lax.broadcasted_iota(jnp.int32, (QUERIES, 128), 0)
    column = query % RING
    outside = (
        ((query < RING) & (edge_ref[0] == 0))
        | ((query >= RING * (RING - 1)) & (edge_ref[1] == 0))
        | ((column == 0) & (edge_ref[2] == 0))
        | ((column == RING - 1) & (edge_ref[3] == 0))
    )
    inside = jnp.where(outside, 0.0, 1.0)[:, :1]
    conv_ref[8 * WIN :, :] = jnp.zeros((8, conv_ref.shape[1]), jnp.float32)
    pieces = ((slice(0, STRIP), flat_ref[...], own_ref[...]),) + tuple(
        (slice(first, first + 16), side[64:80, :], side[48:64, :width])
        for first, side in ((STRIP, left_ref), (STRIP + 16, right_ref))
    )
    copies[0].wait()
    out = out_ref[...].reshape(SHARDS * OUT_ROWS, width)
    for rows, attended, image in pieces:
        mixed_ref[rows, :] = image.astype(jnp.float32) + nn(attended, out)
    mixed = mixed_ref[...]
    middle = nn(square_ref[...], mixed.astype(jnp.bfloat16)).astype(jnp.bfloat16)
    normed_mid = norm_rows(middle.astype(jnp.float32))
    copies[1].wait()
    chunk = 256
    expand = expand_ref[...].reshape(SHARDS * BLOCK_ROWS, width)

    def downsample(shard):
        samples = samples_ref[...]
        four = nt(taps_ref[shard], samples[: 4 * 64])
        ninth = nt(taps_ref[shard][4 * HEAD_ROWS :], samples[4 * 64 :])
        total = four[8 : 8 + HEAD_ROWS, :64]
        for block in range(1, 4):
            rows = slice(8 + block * HEAD_ROWS, 8 + (block + 1) * HEAD_ROWS)
            total += four[rows, block * 64 : (block + 1) * 64]
        first = shard * 39
        down_ref[first : first + HEAD_ROWS, :64] = total
        down_ref[first : first + HALF, :64] += ninth[8 : 8 + HALF, :64]
        down_ref[first + HALF : first + HEAD_ROWS, :64] += ninth[8 : 8 + HALF, 64:]

    shares = {4 + i: range(3 * i, min(3 * i + 3, SHARDS)) for i in range(6)}
    for first in range(0, SHARDS * BLOCK_ROWS, chunk):
        if first == 4 * chunk:
            copies[3].wait()
        for shard in shares.get(first // chunk, ()):
            downsample(shard)
        span = pl.ds(first, chunk)
        hidden = gelu(nt(normed_mid, expand[first : first + chunk])) * inside
        hidden_ref[:, span] = hidden.astype(jnp.bfloat16).astype(jnp.float32)
        totals = [jnp.zeros((8, chunk), jnp.float32)] * WIN
        for place in range(3 * RING):
            source, side = divmod(place, 3)
            window = hidden_ref[pl.ds(source * RING + side, 8), span]
            for down in range(3):
                if 0 <= source - down < WIN:
                    tap = 3 * down + side
                    totals[source - down] += depth_ref[tap : tap + 1, span] * window
        for row in range(WIN):
            conv_ref[row * 8 : row * 8 + 8, span] = gelu(totals[row])
    copies[2].wait()
    shrink = shrink_ref[...].reshape(SHARDS * BLOCK_ROWS, width)
    update = nn(conv_ref[...].astype(jnp.bfloat16), shrink)
    result = (nn(centre_ref[...], middle) + update).astype(jnp.bfloat16)
    spread = nn(repeat_ref[...], result).astype(jnp.bfloat16)
    upsampled = nt(spread, to_fine_ref[...])
    fine_out_ref[...] = jnp.maximum(
        fine_ref[...].astype(jnp.float32) + upsampled, 0.0
    ).astype(jnp.bfloat16)
    downsampled = down_ref[...].T[:CELLS, :width].astype(jnp.bfloat16).astype(jnp.float32)
    coarse_out_ref[...] = jnp.maximum(
        nn(compact_ref[...], result) + downsampled, 0.0
    ).astype(jnp.bfloat16)


def coarse_stream(gathered, edges, flat, own, left, right, depth, samples, fine_res, to_fine):
    width = own.shape[1]
    fine_cells, fine_ch = fine_res.shape
    fixed = (gathered, depth, to_fine, *cell_tables())
    gathered, *fixed = (pltpu.with_memory_space_constraint(array, pltpu.HBM) for array in fixed)
    operands = (flat, own, left, right, samples, fine_res, *fixed)
    smem, vmem, hbm = (
        pl.BlockSpec(memory_space=space) for space in (pltpu.SMEM, pltpu.VMEM, pltpu.HBM)
    )
    return pl.pallas_call(
        coarse_kernel,
        out_shape=(
            jax.ShapeDtypeStruct((fine_cells, fine_ch), jnp.bfloat16),
            jax.ShapeDtypeStruct((CELLS, width), jnp.bfloat16),
        ),
        in_specs=[smem, hbm] + [vmem] * 6 + [hbm] * (len(operands) - 6),
        out_specs=(vmem, vmem),
        scratch_shapes=[
            pltpu.VMEM((SHARDS, OUT_ROWS, width), jnp.bfloat16),
            pltpu.VMEM((SHARDS, BLOCK_ROWS, width), jnp.bfloat16),
            pltpu.VMEM((SHARDS, BLOCK_ROWS, width), jnp.bfloat16),
            pltpu.VMEM((SHARDS, TAP_ROWS, width), jnp.bfloat16),
            pltpu.VMEM((QUERIES, SHARDS * BLOCK_ROWS), jnp.float32),
            pltpu.VMEM((64, SHARDS * BLOCK_ROWS), jnp.float32),
            pltpu.VMEM((SHARDS * HEAD_ROWS, 128), jnp.float32),
            pltpu.VMEM((QUERIES, width), jnp.float32),
            pltpu.SemaphoreType.DMA((4,)),
            *(pltpu.VMEM(operand.shape, operand.dtype) for operand in operands[6:]),
            pltpu.SemaphoreType.DMA((len(operands) - 6,)),
        ],
        compiler_params=pltpu.CompilerParams(vmem_limit_bytes=40 * 1024 * 1024),
    )(edges, gathered, *operands)


def exchange(onward, back, axis):
    up = [(i, i + 1) for i in range(lax.axis_size(axis) - 1)]
    down = [(j, i) for i, j in up]
    return lax.ppermute(onward, axis, up), lax.ppermute(back, axis, down)


def local(
    fine_in,
    coarse_in,
    inproj_fine,
    outproj_fine,
    expand_fine,
    depth_fine,
    shrink_fine,
    inproj_coarse,
    outproj_coarse,
    expand_coarse,
    depth_coarse,
    shrink_coarse,
    to_fine,
    to_coarse,
):
    fine_ch, fine_cells = fine_in.shape[2:]
    coarse_ch, coarse_cells = coarse_in.shape[2:]
    packed = (SHARD_ROWS, coarse_ch)
    (mine,) = call(
        pack_kernel,
        (packed,),
        (outproj_coarse.T, expand_coarse, shrink_coarse.T, to_coarse),
        ((packed, jnp.float32),),
        fetch=(0, 1, 2, 3),
    )
    gathered = lax.all_gather(mine, "rows")
    strip = lax.all_gather(coarse_in.reshape(coarse_ch, coarse_cells).T, "rows")
    fine = fine_in.reshape(fine_ch, fine_cells).T
    place = (lax.axis_index("rows"), lax.axis_index("cols"))
    edges = jnp.stack(
        [
            place[0] > 0,
            place[0] < lax.axis_size("rows") - 1,
            place[1] > 0,
            place[1] < lax.axis_size("cols") - 1,
        ]
    ).astype(jnp.int32)
    middle, going_down, going_up = call(
        fine_attention_kernel,
        (fine.shape, (32, fine_ch), (16, fine_ch)),
        (fine, inproj_fine, outproj_fine, window_table()),
        (),
        fetch=(0, 1, 2, 3),
    )
    above, below = exchange(going_down, going_up, "rows")
    spread, column = strip_tables()
    blocks, own, columns = call(
        strip_kernel,
        ((SHARDS, STRIP, HEAD_ROWS), (STRIP, coarse_ch), (32, coarse_ch)),
        (edges, place[0].reshape(1).astype(jnp.int32), strip, inproj_coarse, spread, column),
        (
            ((SHARDS, TILE, coarse_ch), jnp.float32),
            ((3, SHARDS, TILE, 39), jnp.float32),
            ((SHARDS, TILE, TILE), jnp.float32),
            ((SHARDS + 2, TILE, HEAD_ROWS), jnp.float32),
            ((3 * TILE, coarse_ch), jnp.float32),
        ),
        scalars=2,
        fetch=(3, 4, 5),
    )
    blocks = lax.all_to_all(blocks, "rows", 0, 0, tiled=True)
    message = (80, SHARDS * OUT_ROWS)
    going_right, going_left, flat = call(
        columns_kernel,
        (message, message, (STRIP, SHARDS * OUT_ROWS)),
        (above, below, middle, columns, blocks, *border_tables(), column),
        (((248, fine_ch), jnp.float32),),
        fetch=(5, 6, 7),
    )
    left, right = exchange(going_right, going_left, "cols")
    hidden_count = expand_fine.shape[0]
    fine_res, samples = call(
        field_kernel,
        (fine.shape, (6 * 64, 2 * fine_ch)),
        (
            edges,
            above,
            below,
            left,
            right,
            middle,
            expand_fine.T,
            depth_fine,
            shrink_fine,
            *field_tables(),
        ),
        (
            ((320, fine_ch), jnp.float32),
            ((FIELD_ROWS, hidden_count), jnp.float32),
            ((256, hidden_count), jnp.bfloat16),
            ((512, 2 * fine_ch), jnp.float32),
        ),
        scalars=1,
        fetch=tuple(range(6, 13)),
    )
    depth = jnp.pad(depth_coarse.reshape(9, SHARDS, -1), ((0, 0), (0, 0), (0, 4)))
    fine_out, coarse_out = coarse_stream(
        gathered,
        edges,
        flat,
        own,
        left,
        right,
        depth.reshape(9, -1),
        samples,
        fine_res,
        to_fine,
    )
    return (fine_out.T.reshape(fine_in.shape), coarse_out.T.reshape(coarse_in.shape))


def solution(mesh):
    return jax.shard_map(
        local,
        mesh=mesh,
        in_specs=(
            P("rows", "cols", None, None),
            P("rows", "cols", None, None),
            P(),
            P(),
            P(),
            P(),
            P(),
            P(None, "rows", None),
            P(None, "rows"),
            P("rows", None),
            P(),
            P(None, "rows"),
            P(),
            P(None, "rows", None),
        ),
        out_specs=(P("rows", "cols", None, None), P("rows", "cols", None, None)),
        check_vma=False,
    )
```
